256 devices in a mesh: chain: 32 (over z, x), sector: 8 (over y, core).
Axes of the slice: x: 4, y: 4, z: 8, core: 2. Of those that a mesh axis runs over, the one named last changes fastest.
Arguments:
- wave_start: float32 [32, 16, 128, 16, 128], P('chain', 'sector'), may hold values from -6 to 6
- transfer: float32 [32, 16, 128, 128], P('chain', 'sector'), as said below
- energy_terms: float32 [32, 16, 128, 128], P('chain', 'sector'), may hold values from -1.5 to 1.5
- coupling: float32 [32, 16, 128, 128], P('chain', 'sector'), may hold values from -0.5 to 0.5
- physical: float32 [32, 16, 16], P('chain'), may hold values from -6 to 6
- kept_ranks: int32 [32, 16], P('chain', 'sector'), may hold values from 32 to 128
Outputs:
- wave_kept: float32 [32, 16, 128, 16, 128], P('chain', 'sector')
- energy: float32 [32], P('chain')
- left_env: float32 [32, 16, 128, 128], P('chain', 'sector')
The draws below stay inside these ranges and needn't reach their ends.
Inputs may be any that keep to these rules, and one draw needn't show every extreme that they name: `kept_ranks`: kept bond states of a sector, at most 128. Each sector's transfer matrix has a dominant positive diagonal and small off-diagonal entries.
All inputs are finite; a program needn't handle non-finite values.
Results may differ from the reference program's by a relative error of at most 0.0003.
Values sent between devices are 32-bit elements; how exact they have to be, the bound alone decides.
A program may use at most 128 MiB of HBM per device.

```python
import jax
import jax.numpy as jnp
from jax import lax

BLK = 128
PHYS = 16
ITERS = 2
NSEC = 16
SEGMENTS = 32


def draw_transfer(key, part):
    key = jax.random.fold_in(key, 7)
    rate_key, noise_key = jax.random.split(key)
    low_rate, high_rate = (0.5 / SEGMENTS, 0.4)
    logs = jax.random.uniform(rate_key, (SEGMENTS, NSEC, 1, BLK), jnp.float32, jnp.log(low_rate), jnp.log(high_rate))
    decays = jnp.exp(-jnp.exp(logs))
    noise = jax.random.normal(noise_key, (SEGMENTS, NSEC, BLK, BLK), jnp.float32) * (0.05 / jnp.sqrt(BLK * 1.0))
    identity = jnp.eye(BLK, dtype=jnp.float32)
    return identity * decays + noise


def with_ends(values, rng, low, high):
    longest = values.shape.index(max(values.shape))
    spots = []
    for shift in (0, 1):
        where = [jax.random.randint(jax.random.fold_in(rng, axis), (), 0, length) for axis, length in enumerate(values.shape)]
        where[longest] = (where[longest] + shift) % values.shape[longest]
        spots.append(tuple(where))
    return values.at[spots[0]].set(low).at[spots[1]].set(high)


def block_levels(stream_key, extent, pieces, smallest, top_value):
    def one(axis_at, shards_of):
        draws = jax.random.uniform(jax.random.fold_in(jax.random.fold_in(stream_key, 6), axis_at), (shards_of,), jnp.float32, smallest / len(pieces), top_value / len(pieces))
        return jnp.repeat(jnp.exp(draws), extent[axis_at] // shards_of).reshape((-1,) + (1,) * (len(extent) - axis_at - 1))

    gain = one(*pieces[0])
    for cut in pieces[1:]:
        gain = gain * one(*cut)
    return gain


def scatter_about(own_key, extent, width, limit, cuts=(), kind=jnp.bfloat16):
    values = width * jax.random.normal(own_key, extent, jnp.float32)
    if cuts:
        values = values * block_levels(own_key, extent, cuts, -0.22, 0.18)
    return jnp.clip(values, -limit, limit).astype(kind)


def setup_inputs(seed: int = 0) -> dict:
    keys = jax.random.split(jax.random.key(seed), 7)
    return {
        "wave_start": scatter_about(keys[0], (SEGMENTS, NSEC, BLK, PHYS, BLK), 1.0, 6.0, ((0, 32), (1, 8)), jnp.float32),
        "transfer": draw_transfer(jax.random.fold_in(keys[6], 71), 0),
        "energy_terms": scatter_about(keys[2], (SEGMENTS, NSEC, BLK, BLK), 0.1, 1.5, ((0, 32), (1, 8)), jnp.float32),
        "coupling": scatter_about(keys[3], (SEGMENTS, NSEC, BLK, BLK), BLK ** -0.5, 0.5, ((0, 32), (1, 8)), jnp.float32),
        "physical": scatter_about(keys[4], (SEGMENTS, PHYS, PHYS), 0.5, 6.0, ((0, 32),), jnp.float32),
        "kept_ranks": with_ends(jax.random.randint(keys[5], (SEGMENTS, NSEC), BLK // 4, BLK + 1), jax.random.fold_in(keys[5], 1), BLK // 4, BLK).astype(jnp.int32),
    }


HIGHEST = lax.Precision.HIGHEST
EPS = 1e-06

def symmetric(matrix):
    return 0.5 * (matrix + jnp.swapaxes(matrix, -1, -2))

def apply_operator(wave, left_blk, right_blk, sym_phys, coupler):
    result = jnp.einsum('kab,kbpc->kapc', left_blk, wave, precision=HIGHEST)
    result = result + jnp.einsum('kapb,kbc->kapc', wave, right_blk, precision=HIGHEST)
    result = result + jnp.einsum('pq,kaqc->kapc', sym_phys, wave, precision=HIGHEST)
    raised = jnp.einsum('kab,kbpc->kapc', coupler, wave, precision=HIGHEST)
    empty = jnp.zeros_like(wave[:1])
    incoming = jnp.concatenate([empty, raised[:-1]], axis=0)
    above = jnp.concatenate([wave[1:], empty], axis=0)
    lowered = jnp.einsum('kba,kbpc->kapc', coupler, above, precision=HIGHEST)
    return result + incoming + lowered

def davidson(wave, left_blk, right_blk, sym_phys, coupler, ranks):
    wave = wave / jnp.sqrt(jnp.sum(wave * wave))
    applied = apply_operator(wave, left_blk, right_blk, sym_phys, coupler)
    energy = jnp.float32(0.0)
    for iteration in range(ITERS):
        correlation = jnp.sum(wave * applied)
        residual = applied - correlation * wave
        res_norm = jnp.sum(residual * residual)
        unit_dir = residual / jnp.sqrt(res_norm + EPS)
        turned = apply_operator(unit_dir, left_blk, right_blk, sym_phys, coupler)
        curvature = jnp.sum(unit_dir * turned)
        coupled = jnp.sum(applied * unit_dir)
        energy = 0.5 * (correlation + curvature) - jnp.sqrt(0.25 * (correlation - curvature) ** 2 + coupled * coupled)
        coef_new = energy - correlation
        magnitude = jnp.sqrt(coupled * coupled + coef_new * coef_new)
        wave = (coupled * wave + coef_new * unit_dir) / magnitude
        applied = (coupled * applied + coef_new * turned) / magnitude
    columns = jnp.arange(wave.shape[-1], dtype=jnp.int32)
    kept_mask = (columns[None, None, None, :] < ranks[:, None, None, None]).astype(wave.dtype)
    truncated = wave * kept_mask
    truncated = truncated / jnp.sqrt(jnp.sum(truncated * truncated) + EPS)
    return (truncated, energy)

def reference(wave_start, transfer, energy_terms, coupling, physical, kept_ranks):
    sources = symmetric(energy_terms)
    zero_env = jnp.zeros(transfer.shape[1:], transfer.dtype)

    def left_step(carried, item):
        matrix, source = item
        updated = jnp.einsum('kji,kjl,klm->kim', matrix, carried, matrix, precision=HIGHEST) + source
        return (updated, carried)

    def right_step(carried, item):
        matrix, source = item
        updated = jnp.einsum('kij,kjl,kml->kim', matrix, carried, matrix, precision=HIGHEST) + source
        return (updated, carried)
    _, left_env = lax.scan(left_step, zero_env, (transfer, sources))
    _, right_env = lax.scan(right_step, zero_env, (transfer, sources), reverse=True)
    sym_phys = symmetric(physical)

    def one_segment(item):
        return davidson(*item)
    wave_kept, energy = lax.map(one_segment, (wave_start, left_env, right_env, sym_phys, coupling, kept_ranks))
    return (wave_kept, energy, left_env)
```

```python
import functools

import jax
import jax.numpy as jnp
from jax import lax
from jax.experimental import pallas as pl
from jax.experimental.pallas import tpu as pltpu
from jax.sharding import PartitionSpec as P

ITERS = 2
BLK = 128
NX = 4
NZ = 8

HIGHEST = lax.Precision.HIGHEST
EPS = 1e-06
MESH = pl.DeviceIdType.MESH
F32 = jnp.float32
NN = (((1,), (0,)), ((), ()))
NT = (((1,), (1,)), ((), ()))


def halves(value):
    high = value.astype(jnp.bfloat16)
    return high, (value - high.astype(F32)).astype(jnp.bfloat16)


def dot(lhs, rhs, dims):
    return lax.dot_general(lhs, rhs, dims, preferred_element_type=F32)


def product(lhs, rhs, dims=NN):
    lhs_high, lhs_low = halves(lhs)
    rhs_high, rhs_low = halves(rhs)
    both = jnp.concatenate([lhs_high, lhs_low], axis=1)
    twice = jnp.concatenate([rhs_high, rhs_high], axis=1 if dims is NT else 0)
    return dot(both, twice, dims) + dot(lhs_high, rhs_low, dims)


def carry_over(matrix, env, source):
    return product(product(matrix, env), matrix, NT) + source


def env_kernel(t_ref, e_ref, left_ref, right_ref, mine, elements, window, came, far, ends, envs,
               send_a, recv_a, send_z, recv_z, send_e, recv_e):
    chain = lax.axis_index("chain")
    sector = lax.axis_index("sector")
    x = lax.rem(chain, NX)
    z = lax.div(chain, NX)
    odd = lax.rem(x, 2)
    zz = z + odd * (NZ - 1 - 2 * z)
    my_slot = x + odd * (NX - 1 - 2 * x)

    def in_row(other):
        return (z * NX + other, sector)

    def in_column(other):
        return ((other + odd * (NZ - 1 - 2 * other)) * NX + x, sector)

    def slot_of(column):
        return x if column % 2 == 0 else NX - 1 - x

    for k in range(2):
        transfer = t_ref[k]
        source = 0.5 * (e_ref[k] + e_ref[k].T)
        mine[2 * k, :BLK] = transfer.T
        mine[2 * k + 1, :BLK] = transfer
        mine[2 * k, BLK:] = source
        mine[2 * k + 1, BLK:] = source
    came[...] = jnp.zeros_like(came)
    far[...] = jnp.zeros_like(far)

    barrier = pltpu.get_barrier_semaphore()
    greeted = 0
    for hop in range(1, NX):
        pl.semaphore_signal(barrier, inc=1, device_id=in_row(lax.rem(x + hop, NX)), device_id_type=MESH)
        greeted = greeted + 1
    for hop in (1, 2, 5):
        for other, there in ((zz + hop, zz + hop < NZ), (zz - hop, zz >= hop)):
            @pl.when(there)
            def _():
                pl.semaphore_signal(barrier, inc=1, device_id=in_column(other), device_id_type=MESH)
            greeted = greeted + there.astype(jnp.int32)
    pl.semaphore_wait(barrier, greeted)

    def deal(column):
        slot = slot_of(column)
        return pltpu.make_async_remote_copy(
            mine.at[column], elements.at[slot], send_a.at[column], recv_a.at[slot],
            device_id=in_row(column), device_id_type=MESH)

    for column in range(NX):
        @pl.when(x != column)
        def _():
            deal(column).start()
    elements[pl.ds(my_slot, 1)] = mine[pl.ds(x, 1)]
    for slot in range(NX):
        @pl.when(my_slot != slot)
        def _():
            pltpu.make_async_remote_copy(
                mine.at[slot], elements.at[slot], send_a.at[slot], recv_a.at[slot],
                device_id=in_row(lax.rem(x + 1, NX)), device_id_type=MESH).wait_recv()

    q0, q1, q2, q3 = [elements[s, :BLK] for s in range(NX)]
    s0, s1, s2, s3 = [elements[s, BLK:] for s in range(NX)]
    q01 = product(q1, q0)
    y01 = carry_over(q1, s0, s1)
    q23 = product(q3, q2)
    y23 = carry_over(q3, s2, s3)
    qw = product(q23, q01)
    yw = carry_over(q23, y01, y23)

    def step(at, hop):
        return pltpu.make_async_remote_copy(
            window.at[at], came.at[at], send_z.at[at], recv_z.at[at],
            device_id=in_column(zz + hop), device_id_type=MESH)

    def receive(at, hop):
        @pl.when(zz >= hop)
        def _():
            pltpu.make_async_remote_copy(
                window.at[at], came.at[at], send_z.at[at], recv_z.at[at],
                device_id=in_column(zz - hop), device_id_type=MESH).wait_recv()

    for at, hop in ((0, 1), (1, 2)):
        window[at, :BLK] = qw
        window[at, BLK:] = yw
        @pl.when(zz + hop < NZ)
        def _():
            step(at, hop).start()
        if at == 0:
            q012 = product(q2, q01)
            y012 = carry_over(q2, y01, s2)
        receive(at, hop)
        qp, yp = came[at, :BLK], came[at, BLK:]
        qn = product(qw, qp)
        yw = carry_over(qw, yp, yw)
        qw = qn

    window[2, :BLK] = qw
    window[2, BLK:] = yw
    far_copy = pltpu.make_async_remote_copy(
        window.at[2, pl.ds(BLK, BLK)], far, send_z.at[3], recv_z.at[3],
        device_id=in_column(zz + 5), device_id_type=MESH)

    @pl.when(zz + 1 < NZ)
    def _():
        step(2, 1).start()

    @pl.when(zz + 5 < NZ)
    def _():
        far_copy.start()

    @pl.when(zz >= 5)
    def _():
        pltpu.make_async_remote_copy(
            window.at[2, pl.ds(BLK, BLK)], far, send_z.at[3], recv_z.at[3],
            device_id=in_column(zz - 5), device_id_type=MESH).wait_recv()
    receive(2, 1)
    start = carry_over(came[2, :BLK], far[...], came[2, BLK:])

    def owner(slot):
        return slot + odd * (NX - 1 - 2 * slot)

    def give(slot):
        return pltpu.make_async_remote_copy(
            ends.at[slot], envs.at[x], send_e.at[slot], recv_e.at[x],
            device_id=in_row(owner(slot)), device_id_type=MESH)

    for slot, (q, y) in enumerate(((None, None), (q0, s0), (q01, y01), (q012, y012))):
        ends[slot] = start if slot == 0 else carry_over(q, start, y)
        @pl.when(my_slot != slot)
        def _():
            give(slot).start()
    envs[pl.ds(x, 1)] = ends[pl.ds(my_slot, 1)]
    for column in range(NX):
        @pl.when(x != column)
        def _():
            pltpu.make_async_remote_copy(
                ends.at[column], envs.at[column], send_e.at[column], recv_e.at[column],
                device_id=in_row(column), device_id_type=MESH).wait_recv()
    for k in range(2):
        left_ref[k] = envs[2 * k]
        right_ref[k] = envs[2 * k + 1]

    for column in range(NX):
        @pl.when(x != column)
        def _():
            deal(column).wait_send()
    for at, hop in ((0, 1), (1, 2), (2, 1)):
        @pl.when(zz + hop < NZ)
        def _():
            step(at, hop).wait_send()
    @pl.when(zz + 5 < NZ)
    def _():
        far_copy.wait_send()
    for slot in range(NX):
        @pl.when(my_slot != slot)
        def _():
            give(slot).wait_send()


def environments(transfer, energy_terms):
    pair = jax.ShapeDtypeStruct((2, BLK, BLK), F32)
    vmem = pl.BlockSpec(memory_space=pltpu.VMEM)
    return pl.pallas_call(
        env_kernel,
        out_shape=(pair, pair),
        in_specs=[vmem, vmem],
        out_specs=(vmem, vmem),
        scratch_shapes=[
            pltpu.VMEM((NX, 2 * BLK, BLK), F32),
            pltpu.VMEM((NX, 2 * BLK, BLK), F32),
            pltpu.VMEM((3, 2 * BLK, BLK), F32),
            pltpu.VMEM((3, 2 * BLK, BLK), F32),
            pltpu.VMEM((BLK, BLK), F32),
            pltpu.VMEM((NX, BLK, BLK), F32),
            pltpu.VMEM((NX, BLK, BLK), F32),
            pltpu.SemaphoreType.DMA((NX,)),
            pltpu.SemaphoreType.DMA((NX,)),
            pltpu.SemaphoreType.DMA((4,)),
            pltpu.SemaphoreType.DMA((4,)),
            pltpu.SemaphoreType.DMA((NX,)),
            pltpu.SemaphoreType.DMA((NX,)),
        ],
        compiler_params=pltpu.CompilerParams(collective_id=0, has_side_effects=True),
    )(transfer, energy_terms)


def shifted(block, axis, distance):
    devices = range(lax.axis_size(axis))
    route = [(i - distance, i) for i in devices if i - distance in devices]
    return lax.ppermute(block, axis, route)


def symmetric(matrix):
    return 0.5 * (matrix + jnp.swapaxes(matrix, -1, -2))


def local_terms(wave, left_blk, right_blk, sym_phys):
    result = jnp.einsum("kab,kbpc->kapc", left_blk, wave, precision=HIGHEST)
    result = result + jnp.einsum("kapb,kbc->kapc", wave, right_blk, precision=HIGHEST)
    return result + jnp.einsum("pq,kaqc->kapc", sym_phys, wave, precision=HIGHEST)


def apply_products(wave, left_blk, right_blk, sym_phys, coupler):
    result = local_terms(wave, left_blk, right_blk, sym_phys)
    raised = jnp.einsum("kab,kbpc->kapc", coupler, wave, precision=HIGHEST)
    from_below = shifted(raised[-1:], "sector", 1)
    from_above = shifted(wave[:1], "sector", -1)
    incoming = jnp.concatenate([from_below, raised[:-1]], axis=0)
    above = jnp.concatenate([wave[1:], from_above], axis=0)
    lowered = jnp.einsum("kba,kbpc->kapc", coupler, above, precision=HIGHEST)
    return result + incoming + lowered


def per_device(wave_start, transfer, energy_terms, coupling, physical, kept_ranks):
    left_blk, right_blk = environments(transfer[0], energy_terms[0])
    left_env = left_blk[None]
    sym_phys = symmetric(physical[0])
    coupler = coupling[0]

    def operate(vector):
        return apply_products(vector, left_blk, right_blk, sym_phys, coupler)

    wave = wave_start[0]
    norm_start = lax.psum(jnp.sum(wave * wave), "sector")
    wave = wave / jnp.sqrt(norm_start)
    applied = operate(wave)
    energy = jnp.float32(0.0)
    for iteration in range(ITERS):
        correlation = lax.psum(jnp.sum(wave * applied), "sector")
        residual = applied - correlation * wave
        res_norm = lax.psum(jnp.sum(residual * residual), "sector")
        unit_dir = residual / jnp.sqrt(res_norm + EPS)
        turned = operate(unit_dir)
        curvature, coupled = lax.psum(
            (jnp.sum(unit_dir * turned), jnp.sum(applied * unit_dir)), "sector"
        )
        energy = 0.5 * (correlation + curvature) - jnp.sqrt(
            0.25 * (correlation - curvature) ** 2 + coupled * coupled
        )
        coef_new = energy - correlation
        magnitude = jnp.sqrt(coupled * coupled + coef_new * coef_new)
        wave = (coupled * wave + coef_new * unit_dir) / magnitude
        applied = (coupled * applied + coef_new * turned) / magnitude
    columns = lax.broadcasted_iota(jnp.int32, (1, 1, 1, wave.shape[-1]), 3)
    kept_mask = (columns < kept_ranks[0][:, None, None, None]).astype(wave.dtype)
    truncated = wave * kept_mask
    kept_total = lax.psum(jnp.sum(truncated * truncated), "sector")
    truncated = truncated / jnp.sqrt(kept_total + EPS)
    return (truncated[None], jnp.reshape(energy, (1,)), left_env)


def solution(mesh):
    placed = (
        P("chain", "sector", None, None, None),
        P("chain", "sector", None, None),
        P("chain", "sector", None, None),
        P("chain", "sector", None, None),
        P("chain", None, None),
        P("chain", "sector"),
    )
    return jax.shard_map(
        per_device,
        mesh=mesh,
        in_specs=placed,
        out_specs=(
            P("chain", "sector", None, None, None),
            P("chain"),
            P("chain", "sector", None, None),
        ),
        check_vma=False,
    )
```

```python
import functools

import jax
import jax.numpy as jnp
from jax import lax
from jax.experimental import pallas as pl
from jax.experimental.pallas import tpu as pltpu
from jax.sharding import PartitionSpec as P

BLK = 128
PHYS = 16
NX = 4
NZ = 8
NS = 8
ROWS = BLK * PHYS
CHUNKS = 4
CHUNK = PHYS // CHUNKS
PAIRS = PHYS // 2

EPS = 1e-06
MESH = pl.DeviceIdType.MESH
F32 = jnp.float32
BF16 = jnp.bfloat16
NN = (((1,), (0,)), ((), ()))
NT = (((1,), (1,)), ((), ()))


def halves(value):
    high = value.astype(BF16)
    return high, (value - high.astype(F32)).astype(BF16)


def dot(lhs, rhs, dims=NN):
    return lax.dot_general(lhs, rhs, dims, preferred_element_type=F32)


def product(lhs, rhs, dims=NN):
    lhs_high, lhs_low = halves(lhs)
    rhs_high, rhs_low = halves(rhs)
    both = jnp.concatenate([lhs_high, lhs_low], axis=1)
    twice = jnp.concatenate([rhs_high, rhs_high], axis=1 if dims is NT else 0)
    return dot(both, twice, dims) + dot(lhs_high, rhs_low, dims)


def split_dot(lhs, rhs):
    return dot(lhs[0], rhs[0]) + (dot(lhs[0], rhs[1]) + dot(lhs[1], rhs[0]))


def carry_over(matrix, env, source):
    return product(product(matrix, env), matrix, NT) + source


def fold(value):
    return jnp.sum(value.reshape(-1, 8, BLK), axis=0)


def remote(src, dst, send_sem, recv_sem, device):
    return pltpu.make_async_remote_copy(src, dst, send_sem, recv_sem, device_id=device, device_id_type=MESH)


def update_kernel(v_ref, t_ref, e_ref, c_ref, p_ref, kept_ref, out_ref, energy_ref, left_ref,
                  mine, elements, window, came, far, ends, envs,
                  ghost, ghost_c, vp, w0, r0, w1, w_ghost, t_ghost, crossed,
                  xh, xl, yh, yl, own_a, ghost_a, cross_a, right_w, phys_a, sums,
                  send_a, recv_a, send_z, recv_z, send_e, recv_e,
                  send_v, recv_v, send_w, recv_w, send_t, recv_t, send_p, recv_p):
    chain = lax.axis_index("chain")
    sector = lax.axis_index("sector")
    x = lax.rem(chain, NX)
    z = lax.div(chain, NX)
    odd = lax.rem(x, 2)
    zz = z + odd * (NZ - 1 - 2 * z)
    my_slot = x + odd * (NX - 1 - 2 * x)
    has_below = sector > 0
    has_above = sector < NS - 1
    below = (chain, sector - 1)
    above = (chain, sector + 1)

    def in_row(other):
        return (z * NX + other, sector)

    def in_column(other):
        return ((other + odd * (NZ - 1 - 2 * other)) * NX + x, sector)

    def slot_of(column):
        return x if column % 2 == 0 else NX - 1 - x

    def peer(hop):
        return lax.rem(sector + hop, NS)

    for k in range(2):
        transfer = t_ref[k]
        source = 0.5 * (e_ref[k] + e_ref[k].T)
        mine[2 * k, :BLK] = transfer.T
        mine[2 * k + 1, :BLK] = transfer
        mine[2 * k, BLK:] = source
        mine[2 * k + 1, BLK:] = source
    came[...] = jnp.zeros_like(came)
    far[...] = jnp.zeros_like(far)

    @pl.when(sector == 0)
    def _():
        ghost[0] = jnp.zeros((ROWS, BLK), F32)
        ghost_c[...] = jnp.zeros_like(ghost_c)
        w_ghost[0] = jnp.zeros((PHYS, BLK, BLK), F32)
        t_ghost[1] = jnp.zeros((PAIRS, BLK, BLK), F32)

    @pl.when(sector == NS - 1)
    def _():
        ghost[1] = jnp.zeros((ROWS, BLK), F32)
        w_ghost[1] = jnp.zeros((PHYS, BLK, BLK), F32)
        t_ghost[0] = jnp.zeros((PAIRS, BLK, BLK), F32)

    barrier = pltpu.get_barrier_semaphore()
    greeted = NX - 1 + NS - 1
    for hop in range(1, NX):
        pl.semaphore_signal(barrier, inc=1, device_id=in_row(lax.rem(x + hop, NX)), device_id_type=MESH)
    for hop in range(1, NS):
        pl.semaphore_signal(barrier, inc=1, device_id=(chain, peer(hop)), device_id_type=MESH)
    for hop in (1, 2, 5):
        for other, there in ((zz + hop, zz + hop < NZ), (zz - hop, zz >= hop)):
            @pl.when(there)
            def _():
                pl.semaphore_signal(barrier, inc=1, device_id=in_column(other), device_id_type=MESH)
            greeted = greeted + there.astype(jnp.int32)
    pl.semaphore_wait(barrier, greeted)

    def spread(at, parts):
        rows = [jnp.sum(part, axis=0, keepdims=True) for part in parts]
        rows += [jnp.zeros((1, BLK), F32)] * (8 - len(rows))
        sums[at, pl.ds(sector, 1)] = jnp.concatenate(rows, axis=0)[None]
        for hop in range(1, NS):
            remote(sums.at[at, sector], sums.at[at, sector], send_p.at[at, hop], recv_p.at[at, sector],
                   (chain, peer(hop))).start()

    def collect(at, count):
        for hop in range(1, NS):
            other = peer(hop)
            remote(sums.at[at, other], sums.at[at, other], send_p.at[at, hop], recv_p.at[at, other],
                   (chain, other)).wait_recv()
        total = sums[at, 0]
        for other in range(1, NS):
            total = total + sums[at, other]
        total = jnp.sum(total, axis=1, keepdims=True)
        return [total[i:i + 1] for i in range(count)]

    def deal(column):
        slot = slot_of(column)
        return remote(mine.at[column], elements.at[slot], send_a.at[column], recv_a.at[slot], in_row(column))

    for column in range(NX):
        @pl.when(x != column)
        def _():
            deal(column).start()
    elements[pl.ds(my_slot, 1)] = mine[pl.ds(x, 1)]

    def ghost_up():
        return remote(v_ref.at[1], ghost.at[0], send_v.at[0], recv_v.at[0], above)

    def ghost_down():
        return remote(v_ref.at[0], ghost.at[1], send_v.at[1], recv_v.at[1], below)

    def coupling_up():
        return remote(c_ref.at[1], ghost_c, send_v.at[2], recv_v.at[2], above)

    @pl.when(has_above)
    def _():
        coupling_up().start()
        ghost_up().start()

    @pl.when(has_below)
    def _():
        ghost_down().start()

    def square(i, total):
        part = v_ref[:, pl.ds(pl.multiple_of(i * 256, 256), 256), :]
        return total + fold(part * part)

    spread(0, [lax.fori_loop(0, 8, square, jnp.zeros((8, BLK), F32))])

    for slot in range(NX):
        @pl.when(my_slot != slot)
        def _():
            remote(mine.at[slot], elements.at[slot], send_a.at[slot], recv_a.at[slot],
                   in_row(lax.rem(x + 1, NX))).wait_recv()

    q0, q1, q2, q3 = [elements[s, :BLK] for s in range(NX)]
    s0, s1, s2, s3 = [elements[s, BLK:] for s in range(NX)]
    q01 = product(q1, q0)
    y01 = carry_over(q1, s0, s1)
    q23 = product(q3, q2)
    y23 = carry_over(q3, s2, s3)
    qw = product(q23, q01)
    yw = carry_over(q23, y01, y23)

    def step(at, hop):
        return remote(window.at[at], came.at[at], send_z.at[at], recv_z.at[at], in_column(zz + hop))

    def receive(at, hop):
        @pl.when(zz >= hop)
        def _():
            remote(window.at[at], came.at[at], send_z.at[at], recv_z.at[at], in_column(zz - hop)).wait_recv()

    def start_wave():
        inverse = 1.0 / jnp.sqrt(collect(0, 1)[0])
        inverses = jnp.broadcast_to(inverse, (BLK, BLK))

        def one(p, carry):
            for k in range(2):
                value = v_ref[k, pl.ds(p, BLK, stride=PHYS), :] * inverses
                vp[k, p] = value
                high, low = halves(value)
                xh[p, BLK * (k + 1):BLK * (k + 2), :] = high
                xl[p, BLK * (k + 1):BLK * (k + 2), :] = low
            return carry

        lax.fori_loop(0, PHYS, one, 0)
        return inverses

    def make_phys():
        sym = 0.5 * (p_ref[...] + p_ref[...].T)
        lane = lax.broadcasted_iota(jnp.int32, (PHYS, 256), 1)
        row = lax.broadcasted_iota(jnp.int32, (PHYS, 256), 0)
        spread_p = (lax.div(lane, PHYS) == row).astype(BF16)
        same = (lax.rem(lane, PHYS) == row).astype(F32)
        for i, half in enumerate(halves(sym)):
            wide = dot(half, spread_p)
            for p in range(PHYS):
                phys_a[i, PHYS * p:PHYS * (p + 1), :] = (wide[p:p + 1, :] * same).astype(BF16)

    def phys_piece(high, low, k, i):
        first = pl.multiple_of(BLK * (k + 1) + 32 * i, 32)
        second = pl.multiple_of(BLK * (k + 1) + 32 * i + 16, 16)
        rhs = [jnp.concatenate([
            jnp.concatenate([ref[p, pl.ds(at, 16), :] for p in range(PHYS)], axis=0)
            for at in (first, second)], axis=1) for ref in (high, low)]
        return split_dot((phys_a[0], phys_a[1]), rhs)

    def phys_product(high, low, dst):
        def one(i, carry):
            for k in range(2):
                value = phys_piece(high, low, k, i)
                at = pl.multiple_of(32 * i, 32)
                for p in range(PHYS):
                    rows = value[PHYS * p:PHYS * (p + 1)]
                    dst[k, p, pl.ds(at, 32), :] = jnp.concatenate([rows[:, :BLK], rows[:, BLK:]], axis=0)
            return carry

        lax.fori_loop(0, BLK // 32, one, 0)

    def make_ghost_matrices():
        zero = jnp.zeros((BLK, BLK), BF16)
        from_below = halves(ghost_c[...])
        from_above = halves(c_ref[1].T)
        up = halves(c_ref[1])
        down = halves(ghost_c[...].T)
        for i in range(2):
            ghost_a[i] = jnp.concatenate([jnp.concatenate([from_below[i], zero], axis=1),
                                          jnp.concatenate([zero, from_above[i]], axis=1)], axis=0)
            cross_a[i] = jnp.concatenate([jnp.concatenate([up[i], zero], axis=1),
                                          jnp.concatenate([zero, down[i]], axis=1)], axis=0)

    def ghost_halves(i, low, high):
        p = 2 * i
        parts = [halves(jnp.concatenate([low(p + j), high(p + j)], axis=0)) for j in range(2)]
        return [jnp.concatenate([parts[0][h], parts[1][h]], axis=1) for h in range(2)]

    def add_ghosts(inverses):
        def one(i, carry):
            rhs = ghost_halves(i, lambda p: ghost[0, pl.ds(p, BLK, stride=PHYS), :] * inverses,
                               lambda p: ghost[1, pl.ds(p, BLK, stride=PHYS), :] * inverses)
            value = split_dot((ghost_a[0], ghost_a[1]), rhs)
            for k in range(2):
                for j in range(2):
                    w0[k, 2 * i + j] = w0[k, 2 * i + j] + value[BLK * k:BLK * (k + 1), BLK * j:BLK * (j + 1)]
            return carry

        lax.fori_loop(0, PAIRS, one, 0)

    for at, hop in ((0, 1), (1, 2)):
        window[at, :BLK] = qw
        window[at, BLK:] = yw
        @pl.when(zz + hop < NZ)
        def _():
            step(at, hop).start()
        if at == 0:
            q012 = product(q2, q01)
            y012 = carry_over(q2, y01, s2)
            inverses = start_wave()
            make_phys()
        else:
            phys_product(xh, xl, w0)
        receive(at, hop)
        qp, yp = came[at, :BLK], came[at, BLK:]
        qn = product(qw, qp)
        yw = carry_over(qw, yp, yw)
        qw = qn

    window[2, :BLK] = qw
    window[2, BLK:] = yw
    far_copy = remote(window.at[2, pl.ds(BLK, BLK)], far, send_z.at[3], recv_z.at[3], in_column(zz + 5))

    @pl.when(zz + 1 < NZ)
    def _():
        step(2, 1).start()

    @pl.when(zz + 5 < NZ)
    def _():
        far_copy.start()

    @pl.when(has_below)
    def _():
        coupling_up().wait_recv()
        ghost_up().wait_recv()

    @pl.when(has_above)
    def _():
        ghost_down().wait_recv()

    make_ghost_matrices()
    add_ghosts(inverses)

    @pl.when(zz >= 5)
    def _():
        remote(window.at[2, pl.ds(BLK, BLK)], far, send_z.at[3], recv_z.at[3], in_column(zz - 5)).wait_recv()
    receive(2, 1)
    start = carry_over(came[2, :BLK], far[...], came[2, BLK:])

    def owner(slot):
        return slot + odd * (NX - 1 - 2 * slot)

    def give(slot):
        return remote(ends.at[slot], envs.at[x], send_e.at[slot], recv_e.at[x], in_row(owner(slot)))

    for slot, (q, y) in enumerate(((None, None), (q0, s0), (q01, y01), (q012, y012))):
        ends[slot] = start if slot == 0 else carry_over(q, start, y)
        @pl.when(my_slot != slot)
        def _():
            give(slot).start()
    envs[pl.ds(x, 1)] = ends[pl.ds(my_slot, 1)]
    for column in range(NX):
        @pl.when(x != column)
        def _():
            remote(ends.at[column], envs.at[column], send_e.at[column], recv_e.at[column], in_row(column)).wait_recv()

    for k in range(2):
        left_ref[k] = envs[2 * k]
        high, low = halves(envs[2 * k + 1])
        right_w[k] = jnp.concatenate([jnp.concatenate([high, low], axis=1),
                                      jnp.concatenate([high, jnp.zeros_like(low)], axis=1)], axis=0)
    own = halves(jnp.concatenate([jnp.concatenate([envs[0], c_ref[0].T], axis=1),
                                  jnp.concatenate([c_ref[0], envs[2]], axis=1)], axis=0))
    own_a[0] = own[0]
    own_a[1] = own[1]

    def own_product(high, low, i):
        p = 2 * i
        hs = [high[p + j, BLK:3 * BLK, :] for j in range(2)]
        ls = [low[p + j, BLK:3 * BLK, :] for j in range(2)]
        left = split_dot((own_a[0], own_a[1]), (jnp.concatenate(hs, axis=1), jnp.concatenate(ls, axis=1)))
        blocks = []
        for k in range(2):
            rows = slice(BLK * k, BLK * (k + 1))
            lhs = jnp.concatenate([jnp.concatenate([h[rows], l[rows]], axis=1) for h, l in zip(hs, ls)], axis=0)
            right = dot(lhs, right_w[k])
            right = right[:, :BLK] + right[:, BLK:]
            blocks.append([left[rows, BLK * j:BLK * (j + 1)] + right[BLK * j:BLK * (j + 1)] for j in range(2)])
        return blocks

    def wave_down(part):
        at = pl.ds(part * CHUNK, CHUNK)
        return remote(w0.at[0, at], w_ghost.at[1, at], send_w.at[1, part], recv_w.at[1, part], below)

    def wave_up(part):
        at = pl.ds(part * CHUNK, CHUNK)
        return remote(w0.at[1, at], w_ghost.at[0, at], send_w.at[0, part], recv_w.at[0, part], above)

    def first_apply(i, total):
        blocks = own_product(xh, xl, i)
        for k in range(2):
            for j in range(2):
                p = 2 * i + j
                value = w0[k, p] + blocks[k][j]
                w0[k, p] = value
                high, low = halves(value)
                yh[p, BLK * (k + 1):BLK * (k + 2), :] = high
                yl[p, BLK * (k + 1):BLK * (k + 2), :] = low
                total = total + fold(value * vp[k, p])
        return total

    zeros = jnp.zeros((8, BLK), F32)
    total = zeros
    for part in range(CHUNKS):
        total = lax.fori_loop(part * CHUNK // 2, (part + 1) * CHUNK // 2, first_apply, total)

        @pl.when(has_below)
        def _():
            wave_down(part).start()

        @pl.when(has_above)
        def _():
            wave_up(part).start()
    spread(1, [total])

    phys_product(yh, yl, w1)

    def second_apply(i, carry):
        blocks = own_product(yh, yl, i)
        for k in range(2):
            for j in range(2):
                w1[k, 2 * i + j] = w1[k, 2 * i + j] + blocks[k][j]
        return carry

    lax.fori_loop(0, PAIRS, second_apply, 0)
    corr = collect(1, 1)[0]
    corrs = jnp.broadcast_to(corr, (BLK, BLK))

    def finish(i, totals):
        rr, w0r, rt, vt, w0t, tt = totals
        rhs = ghost_halves(i, lambda p: w_ghost[0, p], lambda p: w_ghost[1, p])
        value = split_dot((ghost_a[0], ghost_a[1]), rhs)
        for k in range(2):
            for j in range(2):
                p = 2 * i + j
                applied = w0[k, p]
                wave = vp[k, p]
                residual = applied - corrs * wave
                turned = w1[k, p] + value[BLK * k:BLK * (k + 1), BLK * j:BLK * (j + 1)] - corrs * applied
                r0[k, p] = residual
                w1[k, p] = turned
                high, low = halves(turned)
                xh[p, BLK * (k + 1):BLK * (k + 2), :] = high
                xl[p, BLK * (k + 1):BLK * (k + 2), :] = low
                rr = rr + fold(residual * residual)
                w0r = w0r + fold(applied * residual)
                rt = rt + fold(residual * turned)
                vt = vt + fold(wave * turned)
                w0t = w0t + fold(applied * turned)
                tt = tt + fold(turned * turned)
        return rr, w0r, rt, vt, w0t, tt

    def turned_down(part):
        at = pl.ds(part * CHUNK, CHUNK)
        return remote(w1.at[0, at], t_ghost.at[0, at], send_t.at[part], recv_t.at[part], below)

    def turned_up(part):
        at = pl.ds(part * CHUNK, CHUNK)
        to = pl.ds(part * CHUNK - PAIRS, CHUNK)
        return remote(w1.at[1, at], t_ghost.at[1, to], send_t.at[part], recv_t.at[part], above)

    totals = (zeros,) * 6
    for part in range(CHUNKS):
        @pl.when(has_below)
        def _():
            wave_up(part).wait_recv()

        @pl.when(has_above)
        def _():
            wave_down(part).wait_recv()

        totals = lax.fori_loop(part * CHUNK // 2, (part + 1) * CHUNK // 2, finish, totals)
        if part < CHUNKS // 2:
            @pl.when(has_below)
            def _():
                turned_down(part).start()
        else:
            @pl.when(has_above)
            def _():
                turned_up(part).start()
    w0t, tt = totals[4:]
    spread(2, list(totals[:4]))

    def third_apply(i, total):
        blocks = own_product(xh, xl, i)
        for k in range(2):
            for j in range(2):
                total = total + fold(blocks[k][j] * w1[k, 2 * i + j])
        return total

    def third_phys(i, total):
        for k in range(2):
            value = phys_piece(xh, xl, k, i)
            at = pl.multiple_of(32 * i, 32)
            for p in range(PHYS):
                rows = value[PHYS * p:PHYS * (p + 1)]
                both = jnp.concatenate([rows[:, :BLK], rows[:, BLK:]], axis=0)
                total = total + fold(both * w1[k, p, pl.ds(at, 32), :])
        return total

    def cross(i, carry):
        p = 2 * i
        rhs = [jnp.concatenate([
            jnp.concatenate([ref[p + j, 2 * BLK:3 * BLK, :], ref[p + PAIRS + j, BLK:2 * BLK, :]], axis=0)
            for j in range(2)], axis=1) for ref in (xh, xl)]
        value = split_dot((cross_a[0], cross_a[1]), rhs)
        for side in range(2):
            for j in range(2):
                crossed[side, p + j] = value[BLK * side:BLK * (side + 1), BLK * j:BLK * (j + 1)]
        return carry

    lax.fori_loop(0, PAIRS // 2, cross, 0)
    tht = lax.fori_loop(0, PAIRS, third_apply, zeros)
    tht = lax.fori_loop(0, BLK // 32, third_phys, tht)

    rr, w0r, rt, vt = collect(2, 4)
    norm = jnp.sqrt(rr + EPS)
    curvature = rt / (rr + EPS)
    coupled = w0r / norm
    ritz = 0.5 * (corr + curvature) - jnp.sqrt(0.25 * (corr - curvature) ** 2 + coupled * coupled)
    coef = ritz - corr
    magnitude = jnp.sqrt(coupled * coupled + coef * coef)
    wave_v = coupled / magnitude
    wave_r = coef / (magnitude * norm)
    corr2 = wave_v * wave_v * corr + wave_v * wave_r * (vt + w0r) + wave_r * wave_r * rt
    res_v = wave_v * (corr - corr2)
    res_r = wave_v - corr2 * wave_r
    res_t = wave_r

    masks = [(lax.broadcasted_iota(jnp.int32, (1, BLK), 1) < kept_ref[0, k]).astype(F32) for k in range(2)]
    wide = [jnp.broadcast_to(value, (BLK, BLK)) for value in (wave_v, wave_r, wave_v * corr, res_v, res_r, res_t)]

    def second_residual(p, totals):
        rr2, ar2, mww, mwr, mrr = totals
        for k in range(2):
            wave, residual, turned = vp[k, p], r0[k, p], w1[k, p]
            now = wide[0] * wave + wide[1] * residual
            applied = wide[2] * wave + wide[0] * residual + wide[1] * turned
            second = wide[3] * wave + wide[4] * residual + wide[5] * turned
            rr2 = rr2 + fold(second * second)
            ar2 = ar2 + fold(applied * second)
            mww = mww + masks[k] * fold(now * now)
            mwr = mwr + masks[k] * fold(now * second)
            mrr = mrr + masks[k] * fold(second * second)
        return rr2, ar2, mww, mwr, mrr

    finals = lax.fori_loop(0, PHYS, second_residual, (zeros,) * 5)

    for part in range(CHUNKS):
        if part < CHUNKS // 2:
            @pl.when(has_above)
            def _():
                turned_down(part).wait_recv()
        else:
            @pl.when(has_below)
            def _():
                turned_up(part).wait_recv()

    def meet(i, total):
        return total + fold(crossed[0, i] * t_ghost[0, i]) + fold(crossed[1, i] * t_ghost[1, i])

    tht = tht + 2.0 * lax.fori_loop(0, PAIRS, meet, zeros)
    spread(3, list(finals) + [tht, w0t, tt])
    rr2, ar2, mww, mwr, mrr, tht, w0t, tt = collect(3, 8)
    norm2 = jnp.sqrt(rr2 + EPS)
    turned2 = (res_v * res_v * corr + res_r * res_r * rt + res_t * res_t * tht
               + 2.0 * (res_v * res_r * vt + res_v * res_t * w0t + res_r * res_t * tt))
    curvature = turned2 / (rr2 + EPS)
    coupled = ar2 / norm2
    ritz = 0.5 * (corr2 + curvature) - jnp.sqrt(0.25 * (corr2 - curvature) ** 2 + coupled * coupled)
    coef = ritz - corr2
    magnitude = jnp.sqrt(coupled * coupled + coef * coef)
    of_wave = coupled / magnitude
    of_res = coef / (magnitude * norm2)
    kept = of_wave * of_wave * mww + 2.0 * of_wave * of_res * mwr + of_res * of_res * mrr
    scale = 1.0 / jnp.sqrt(kept + EPS)
    energy_ref[...] = jnp.broadcast_to(ritz, (8, BLK))
    last = [jnp.broadcast_to(scale * value, (BLK, BLK)) for value in (
        of_wave * wave_v + of_res * res_v, of_wave * wave_r + of_res * res_r, of_res * res_t)]

    def write(p, carry):
        for k in range(2):
            value = last[0] * vp[k, p] + last[1] * r0[k, p] + last[2] * w1[k, p]
            out_ref[k, pl.ds(p, BLK, stride=PHYS), :] = value * masks[k]
        return carry

    lax.fori_loop(0, PHYS, write, 0)

    for column in range(NX):
        @pl.when(x != column)
        def _():
            deal(column).wait_send()
    for at, hop in ((0, 1), (1, 2), (2, 1)):
        @pl.when(zz + hop < NZ)
        def _():
            step(at, hop).wait_send()
    @pl.when(zz + 5 < NZ)
    def _():
        far_copy.wait_send()
    for slot in range(NX):
        @pl.when(my_slot != slot)
        def _():
            give(slot).wait_send()
    for at in range(4):
        for hop in range(1, NS):
            remote(sums.at[at, sector], sums.at[at, sector], send_p.at[at, hop], recv_p.at[at, sector],
                   (chain, peer(hop))).wait_send()

    @pl.when(has_above)
    def _():
        coupling_up().wait_send()
        ghost_up().wait_send()
        for part in range(CHUNKS):
            wave_up(part).wait_send()
            if part >= CHUNKS // 2:
                turned_up(part).wait_send()

    @pl.when(has_below)
    def _():
        ghost_down().wait_send()
        for part in range(CHUNKS):
            wave_down(part).wait_send()
            if part < CHUNKS // 2:
                turned_down(part).wait_send()


def per_device(wave_start, transfer, energy_terms, coupling, physical, kept_ranks):
    vmem = pl.BlockSpec(memory_space=pltpu.VMEM)
    dma = pltpu.SemaphoreType.DMA
    out, energy, left = pl.pallas_call(
        update_kernel,
        out_shape=(
            jax.ShapeDtypeStruct((2, ROWS, BLK), F32),
            jax.ShapeDtypeStruct((8, BLK), F32),
            jax.ShapeDtypeStruct((2, BLK, BLK), F32),
        ),
        in_specs=[vmem] * 5 + [pl.BlockSpec(memory_space=pltpu.SMEM)],
        out_specs=(vmem, vmem, vmem),
        scratch_shapes=[
            pltpu.VMEM((NX, 2 * BLK, BLK), F32),
            pltpu.VMEM((NX, 2 * BLK, BLK), F32),
            pltpu.VMEM((3, 2 * BLK, BLK), F32),
            pltpu.VMEM((3, 2 * BLK, BLK), F32),
            pltpu.VMEM((BLK, BLK), F32),
            pltpu.VMEM((NX, BLK, BLK), F32),
            pltpu.VMEM((NX, BLK, BLK), F32),
            pltpu.VMEM((2, ROWS, BLK), F32),
            pltpu.VMEM((BLK, BLK), F32),
            pltpu.VMEM((2, PHYS, BLK, BLK), F32),
            pltpu.VMEM((2, PHYS, BLK, BLK), F32),
            pltpu.VMEM((2, PHYS, BLK, BLK), F32),
            pltpu.VMEM((2, PHYS, BLK, BLK), F32),
            pltpu.VMEM((2, PHYS, BLK, BLK), F32),
            pltpu.VMEM((2, PAIRS, BLK, BLK), F32),
            pltpu.VMEM((2, PAIRS, BLK, BLK), F32),
            pltpu.VMEM((PHYS, 4 * BLK, BLK), BF16),
            pltpu.VMEM((PHYS, 4 * BLK, BLK), BF16),
            pltpu.VMEM((PHYS, 4 * BLK, BLK), BF16),
            pltpu.VMEM((PHYS, 4 * BLK, BLK), BF16),
            pltpu.VMEM((2, 2 * BLK, 2 * BLK), BF16),
            pltpu.VMEM((2, 2 * BLK, 2 * BLK), BF16),
            pltpu.VMEM((2, 2 * BLK, 2 * BLK), BF16),
            pltpu.VMEM((2, 2 * BLK, 2 * BLK), BF16),
            pltpu.VMEM((2, 2 * BLK, 2 * BLK), BF16),
            pltpu.VMEM((4, NS, 8, BLK), F32),
            dma((NX,)), dma((NX,)), dma((4,)), dma((4,)), dma((NX,)), dma((NX,)),
            dma((3,)), dma((3,)), dma((2, CHUNKS)), dma((2, CHUNKS)), dma((CHUNKS,)), dma((CHUNKS,)),
            dma((4, NS)), dma((4, NS)),
        ],
        compiler_params=pltpu.CompilerParams(
            collective_id=0, has_side_effects=True, vmem_limit_bytes=52 << 20),
    )(wave_start.reshape(2, ROWS, BLK), transfer[0], energy_terms[0], coupling[0], physical[0], kept_ranks)
    return (out.reshape(wave_start.shape), energy[0, :1], left[None])


def solution(mesh):
    placed = (
        P("chain", "sector", None, None, None),
        P("chain", "sector", None, None),
        P("chain", "sector", None, None),
        P("chain", "sector", None, None),
        P("chain", None, None),
        P("chain", "sector"),
    )
    return jax.shard_map(
        per_device,
        mesh=mesh,
        in_specs=placed,
        out_specs=(
            P("chain", "sector", None, None, None),
            P("chain"),
            P("chain", "sector", None, None),
        ),
        check_vma=False,
    )
```

```python
import functools

import jax
import jax.numpy as jnp
from jax import lax
from jax.experimental import pallas as pl
from jax.experimental.pallas import tpu as pltpu
from jax.sharding import PartitionSpec as P

BLK = 128
PHYS = 16
NX = 4
NZ = 8
NS = 8
ROWS = BLK * PHYS
CHUNKS = 4
CHUNK = PHYS // CHUNKS
PAIRS = PHYS // 2

EPS = 1e-06
MESH = pl.DeviceIdType.MESH
F32 = jnp.float32
BF16 = jnp.bfloat16
NN = (((1,), (0,)), ((), ()))
NT = (((1,), (1,)), ((), ()))


def halves(value):
    high = value.astype(BF16)
    return high, (value - high.astype(F32)).astype(BF16)


def dot(lhs, rhs, dims=NN):
    return lax.dot_general(lhs, rhs, dims, preferred_element_type=F32)


def product(lhs, rhs, dims=NN):
    lhs_high, lhs_low = halves(lhs)
    rhs_high, rhs_low = halves(rhs)
    both = jnp.concatenate([lhs_high, lhs_low], axis=1)
    twice = jnp.concatenate([rhs_high, rhs_high], axis=1 if dims is NT else 0)
    return dot(both, twice, dims) + dot(lhs_high, rhs_low, dims)


def split_dot(lhs, rhs):
    return dot(lhs[0], rhs[0]) + (dot(lhs[0], rhs[1]) + dot(lhs[1], rhs[0]))


def carry_over(matrix, env, source):
    return product(product(matrix, env), matrix, NT) + source


def fold(value):
    return jnp.sum(value.reshape(-1, 8, BLK), axis=0)


def remote(src, dst, send_sem, recv_sem, device):
    return pltpu.make_async_remote_copy(src, dst, send_sem, recv_sem, device_id=device, device_id_type=MESH)


def update_kernel(v_hbm, t_hbm, e_hbm, c_hbm, p_hbm, kept_hbm, out_ref, energy_ref, left_ref,
                  v_ref, t_ref, e_ref, c_ref, p_ref, kept_ref,
                  mine, elements, window, came, far, partial, ends, envs,
                  ghost, ghost_c, vp, w0, r0, w1, w_ghost, t_ghost, lr_ghost, crossed,
                  xh, xl, yh, yl, own_l, own_a, ghost_a, cross_a, ghost_l, right_w, phys_a, sums,
                  load, send_a, recv_a, send_z, recv_z, send_f, recv_f, send_e, recv_e,
                  send_v, recv_v, send_w, recv_w, send_t, recv_t, send_p, recv_p):
    chain = lax.axis_index("chain")
    sector = lax.axis_index("sector")
    x = lax.rem(chain, NX)
    z = lax.div(chain, NX)
    odd = lax.rem(x, 2)
    zz = z + odd * (NZ - 1 - 2 * z)
    my_slot = x + odd * (NX - 1 - 2 * x)
    has_below = sector > 0
    has_above = sector < NS - 1
    below = (chain, sector - 1)
    above = (chain, sector + 1)

    def in_row(other):
        return (z * NX + other, sector)

    def in_column(other):
        return ((other + odd * (NZ - 1 - 2 * other)) * NX + x, sector)

    def slot_of(column):
        return x if column % 2 == 0 else NX - 1 - x

    def peer(hop):
        return lax.rem(sector + hop, NS)

    loads = [pltpu.make_async_copy(src, dst, load.at[i]) for i, (src, dst) in enumerate((
        (t_hbm, t_ref), (e_hbm, e_ref), (v_hbm, v_ref), (c_hbm, c_ref), (p_hbm, p_ref),
        (kept_hbm, kept_ref)))]
    for copy in loads:
        copy.start()

    barrier = pltpu.get_barrier_semaphore()
    greeted = NX - 1 + NS - 1
    for hop in range(1, NX):
        pl.semaphore_signal(barrier, inc=1, device_id=in_row(lax.rem(x + hop, NX)), device_id_type=MESH)
    for hop in range(1, NS):
        pl.semaphore_signal(barrier, inc=1, device_id=(chain, peer(hop)), device_id_type=MESH)
    for hop in (1, 2, 5):
        for other, there in ((zz + hop, zz + hop < NZ), (zz - hop, zz >= hop)):
            @pl.when(there)
            def _():
                pl.semaphore_signal(barrier, inc=1, device_id=in_column(other), device_id_type=MESH)
            greeted = greeted + there.astype(jnp.int32)

    loads[0].wait()
    loads[1].wait()
    for k in range(2):
        transfer = t_ref[k]
        source = 0.5 * (e_ref[k] + e_ref[k].T)
        mine[2 * k, 0] = transfer.T
        mine[2 * k + 1, 0] = transfer
        mine[2 * k, 1] = source
        mine[2 * k + 1, 1] = source
    pl.semaphore_wait(barrier, greeted)

    def spread(at, parts):
        rows = [jnp.sum(part, axis=0, keepdims=True) for part in parts]
        rows += [jnp.zeros((1, BLK), F32)] * (8 - len(rows))
        sums[at, pl.ds(sector, 1)] = jnp.concatenate(rows, axis=0)[None]
        for hop in range(1, NS):
            remote(sums.at[at, sector], sums.at[at, sector], send_p.at[at, hop], recv_p.at[at, sector],
                   (chain, peer(hop))).start()

    def collect(at, count):
        for hop in range(1, NS):
            other = peer(hop)
            remote(sums.at[at, other], sums.at[at, other], send_p.at[at, hop], recv_p.at[at, other],
                   (chain, other)).wait_recv()
        total = sums[at, 0]
        for other in range(1, NS):
            total = total + sums[at, other]
        total = jnp.sum(total, axis=1, keepdims=True)
        return [total[i:i + 1] for i in range(count)]

    def deal(column):
        slot = slot_of(column)
        return remote(mine.at[column], elements.at[slot], send_a.at[column], recv_a.at[slot], in_row(column))

    for hop in (2, 1, 3):
        for column in range(NX):
            @pl.when(column == lax.rem(x + hop, NX))
            def _():
                deal(column).start()
    elements[pl.ds(my_slot, 1)] = mine[pl.ds(x, 1)]

    def ghost_up():
        return remote(v_hbm.at[1], ghost.at[0], send_v.at[0], recv_v.at[0], above)

    def ghost_down():
        return remote(v_hbm.at[0], ghost.at[1], send_v.at[1], recv_v.at[1], below)

    def coupling_up():
        return remote(c_hbm.at[1], ghost_c, send_v.at[2], recv_v.at[2], above)

    @pl.when(has_above)
    def _():
        coupling_up().start()
        ghost_up().start()

    @pl.when(has_below)
    def _():
        ghost_down().start()

    def square(i, total):
        part = v_ref[:, pl.ds(pl.multiple_of(i * 256, 256), 256), :]
        return total + fold(part * part)

    loads[2].wait()
    spread(0, [lax.fori_loop(0, 8, square, jnp.zeros((8, BLK), F32))])

    square_zero = jnp.zeros((BLK, BLK), F32)
    for ref, unused in (
            (came.at[0, 0], (zz < 2) | (zz == NZ - 1)), (came.at[0, 1], (zz < 1) | (zz == NZ - 1)),
            (came.at[1, 0], (zz < 4) | (zz == NZ - 1)), (came.at[1, 1], (zz < 2) | (zz == NZ - 1)),
            (came.at[2, 0], zz < 5), (came.at[2, 1], zz < 1), (far, zz < 5)):
        @pl.when(unused)
        def _():
            ref[...] = square_zero

    @pl.when(sector == 0)
    def _():
        ghost[0] = jnp.zeros((ROWS, BLK), F32)
        ghost_c[...] = square_zero
        w_ghost[0] = jnp.zeros((PHYS, BLK, BLK), F32)
        t_ghost[1] = jnp.zeros((PAIRS, BLK, BLK), F32)
        lr_ghost[0] = jnp.zeros((2, BLK, BLK), F32)

    @pl.when(sector == NS - 1)
    def _():
        ghost[1] = jnp.zeros((ROWS, BLK), F32)
        w_ghost[1] = jnp.zeros((PHYS, BLK, BLK), F32)
        t_ghost[0] = jnp.zeros((PAIRS, BLK, BLK), F32)
        lr_ghost[1] = jnp.zeros((2, BLK, BLK), F32)

    for slot in range(NX):
        @pl.when(my_slot != slot)
        def _():
            remote(mine.at[slot], elements.at[slot], send_a.at[slot], recv_a.at[slot],
                   in_row(lax.rem(x + 1, NX))).wait_recv()

    q0, q1, q2, q3 = [elements[s, 0] for s in range(NX)]
    s0, s1, s2, s3 = [elements[s, 1] for s in range(NX)]
    q01 = product(q1, q0)
    y01 = carry_over(q1, s0, s1)
    q23 = product(q3, q2)
    y23 = carry_over(q3, s2, s3)
    qw = product(q23, q01)
    yw = carry_over(q23, y01, y23)

    hops = (1, 2, 1)
    sends = (((zz >= 1) & (zz <= 5), zz <= 5), ((zz >= 2) & (zz <= 4), zz <= 4), ((zz >= 4) & (zz <= 6), zz <= 6))
    takes = (((zz >= 2) & (zz <= 6), (zz >= 1) & (zz <= 6)), ((zz >= 4) & (zz <= 6), (zz >= 2) & (zz <= 6)),
             (zz >= 5, zz >= 1))

    def step(at, part):
        return remote(window.at[at, part], came.at[at, part], send_z.at[at, part], recv_z.at[at, part],
                      in_column(zz + hops[at]))

    def send(at, part, value):
        window[at, part] = value

        @pl.when(sends[at][part])
        def _():
            step(at, part).start()

    def receive(at, part):
        @pl.when(takes[at][part])
        def _():
            remote(window.at[at, part], came.at[at, part], send_z.at[at, part], recv_z.at[at, part],
                   in_column(zz - hops[at])).wait_recv()
        return came[at, part]

    def far_copy(at):
        return remote(window.at[at, 1], far, send_f.at[0], recv_f.at[0], in_column(zz + 5))

    def send_far(at):
        @pl.when(zz == at)
        def _():
            far_copy(at).start()

    def start_wave():
        inverse = 1.0 / jnp.sqrt(collect(0, 1)[0])
        inverses = jnp.broadcast_to(inverse, (BLK, BLK))

        def one(p, carry):
            for k in range(2):
                value = v_ref[k, pl.ds(p, BLK, stride=PHYS), :] * inverses
                vp[k, p] = value
                high, low = halves(value)
                xh[p, BLK * (k + 1):BLK * (k + 2), :] = high
                xl[p, BLK * (k + 1):BLK * (k + 2), :] = low
            return carry

        lax.fori_loop(0, PHYS, one, 0)
        return inverses

    def make_phys():
        loads[4].wait()
        sym = 0.5 * (p_ref[...] + p_ref[...].T)
        lane = lax.broadcasted_iota(jnp.int32, (PHYS, 256), 1)
        row = lax.broadcasted_iota(jnp.int32, (PHYS, 256), 0)
        spread_p = (lax.div(lane, PHYS) == row).astype(BF16)
        same = (lax.rem(lane, PHYS) == row).astype(F32)
        for i, half in enumerate(halves(sym)):
            wide = dot(half, spread_p)
            for p in range(PHYS):
                phys_a[i, PHYS * p:PHYS * (p + 1), :] = (wide[p:p + 1, :] * same).astype(BF16)

    def phys_piece(high, low, k, i):
        first = pl.multiple_of(BLK * (k + 1) + 32 * i, 32)
        second = pl.multiple_of(BLK * (k + 1) + 32 * i + 16, 16)
        rhs = [jnp.concatenate([
            jnp.concatenate([ref[p, pl.ds(at, 16), :] for p in range(PHYS)], axis=0)
            for at in (first, second)], axis=1) for ref in (high, low)]
        return split_dot((phys_a[0], phys_a[1]), rhs)

    def phys_product(high, low, dst):
        def one(i, carry):
            for k in range(2):
                value = phys_piece(high, low, k, i)
                at = pl.multiple_of(32 * i, 32)
                for p in range(PHYS):
                    rows = value[PHYS * p:PHYS * (p + 1)]
                    dst[k, p, pl.ds(at, 32), :] = jnp.concatenate([rows[:, :BLK], rows[:, BLK:]], axis=0)
            return carry

        lax.fori_loop(0, BLK // 32, one, 0)

    def make_ghost_matrices():
        loads[3].wait()
        zero = jnp.zeros((BLK, BLK), BF16)
        from_below = halves(ghost_c[...])
        from_above = halves(c_ref[1].T)
        up = halves(c_ref[1])
        down = halves(ghost_c[...].T)
        own_up = halves(c_ref[0])
        own_down = halves(c_ref[0].T)
        for i in range(2):
            own_a[i] = jnp.concatenate([jnp.concatenate([zero, own_down[i]], axis=1),
                                        jnp.concatenate([own_up[i], zero], axis=1)], axis=0)
            ghost_a[i] = jnp.concatenate([jnp.concatenate([from_below[i], zero], axis=1),
                                          jnp.concatenate([zero, from_above[i]], axis=1)], axis=0)
            cross_a[i] = jnp.concatenate([jnp.concatenate([up[i], zero], axis=1),
                                          jnp.concatenate([zero, down[i]], axis=1)], axis=0)

    def pair_of(refs, i, low, high):
        p = 2 * i
        return [jnp.concatenate([
            jnp.concatenate([ref[p + j, BLK * low:BLK * (low + 1), :], ref[p + j, BLK * high:BLK * (high + 1), :]], axis=0)
            for j in range(2)], axis=1) for ref in refs]

    def add_ghosts(inverses):
        def one(i, carry):
            for j in range(2):
                p = 2 * i + j
                for side, row in ((0, 0), (1, 3)):
                    high, low = halves(ghost[side, pl.ds(p, BLK, stride=PHYS), :] * inverses)
                    xh[p, BLK * row:BLK * (row + 1), :] = high
                    xl[p, BLK * row:BLK * (row + 1), :] = low
            value = (split_dot((ghost_a[0], ghost_a[1]), pair_of((xh, xl), i, 0, 3))
                     + split_dot((own_a[0], own_a[1]), pair_of((xh, xl), i, 1, 2)))
            for k in range(2):
                for j in range(2):
                    both = w0[k, 2 * i + j] + value[BLK * k:BLK * (k + 1), BLK * j:BLK * (j + 1)]
                    w0[k, 2 * i + j] = both
                    partial[k, 2 * i + j] = both
            return carry

        lax.fori_loop(0, PAIRS, one, 0)

    def base_down():
        return remote(partial.at[0], w_ghost.at[1], send_w.at[0], recv_w.at[0], below)

    def base_up():
        return remote(partial.at[1], w_ghost.at[0], send_w.at[1], recv_w.at[1], above)

    send(0, 1, yw)
    send(0, 0, qw)
    send_far(0)
    q012 = product(q2, q01)
    y012 = carry_over(q2, y01, s2)
    inverses = start_wave()
    make_phys()
    yw = carry_over(qw, receive(0, 1), yw)
    send(1, 1, yw)
    send_far(1)
    qw = product(qw, receive(0, 0))
    send(1, 0, qw)
    phys_product(xh, xl, w0)

    @pl.when(has_below)
    def _():
        coupling_up().wait_recv()
        ghost_up().wait_recv()

    @pl.when(has_above)
    def _():
        ghost_down().wait_recv()

    make_ghost_matrices()
    add_ghosts(inverses)

    @pl.when(has_below)
    def _():
        base_down().start()

    @pl.when(has_above)
    def _():
        base_up().start()

    yw = carry_over(qw, receive(1, 1), yw)
    send(2, 1, yw)
    send_far(2)
    send(2, 0, product(qw, receive(1, 0)))

    @pl.when(zz >= 5)
    def _():
        remote(window.at[2, 1], far, send_f.at[0], recv_f.at[0], in_column(zz - 5)).wait_recv()
    y_near = receive(2, 1)
    start = carry_over(receive(2, 0), far[...], y_near)

    def owner(slot):
        return slot + odd * (NX - 1 - 2 * slot)

    def give(slot):
        return remote(ends.at[slot], envs.at[x], send_e.at[slot], recv_e.at[x], in_row(owner(slot)))

    ends[0] = start
    for slot, (q, y) in enumerate(((q0, s0), (q01, y01), (q012, y012))):
        ends[slot + 1] = carry_over(q, start, y)
    for hop in (2, 1, 3):
        for slot in range(NX):
            @pl.when(slot == lax.rem(my_slot + hop, NX))
            def _():
                give(slot).start()
    envs[pl.ds(x, 1)] = ends[pl.ds(my_slot, 1)]
    for column in range(NX):
        @pl.when(x != column)
        def _():
            remote(ends.at[column], envs.at[column], send_e.at[column], recv_e.at[column], in_row(column)).wait_recv()

    def envs_down():
        return remote(envs.at[pl.ds(0, 2)], lr_ghost.at[1], send_v.at[3], recv_v.at[3], below)

    def envs_up():
        return remote(envs.at[pl.ds(2, 2)], lr_ghost.at[0], send_v.at[4], recv_v.at[4], above)

    @pl.when(has_below)
    def _():
        envs_down().start()

    @pl.when(has_above)
    def _():
        envs_up().start()

    def right_of(env):
        high, low = halves(env)
        return jnp.concatenate([jnp.concatenate([high, low], axis=1),
                                jnp.concatenate([high, jnp.zeros_like(low)], axis=1)], axis=0)

    for k in range(2):
        left_ref[k] = envs[2 * k]
        right_w[k] = right_of(envs[2 * k + 1])
    none = jnp.zeros((BLK, BLK), BF16)
    lefts = [halves(envs[2 * k]) for k in range(2)]
    for h in range(2):
        own_l[h] = jnp.concatenate([jnp.concatenate([lefts[0][h], none], axis=1),
                                    jnp.concatenate([none, lefts[1][h]], axis=1)], axis=0)
        own_a[h] = own_a[h] + own_l[h]

    def product_of(refs, i, low, high, left, rights):
        p = 2 * i
        value = split_dot((left[0], left[1]), pair_of(refs, i, low, high))
        blocks = []
        for k, row in enumerate((low, high)):
            rows = slice(BLK * row, BLK * (row + 1))
            lhs = jnp.concatenate([jnp.concatenate([ref[p + j, rows, :] for ref in refs], axis=1)
                                   for j in range(2)], axis=0)
            right = dot(lhs, right_w[rights + k])
            right = right[:, :BLK] + right[:, BLK:]
            blocks.append([value[BLK * k:BLK * (k + 1), BLK * j:BLK * (j + 1)] + right[BLK * j:BLK * (j + 1)]
                           for j in range(2)])
        return blocks

    def first_apply(i, total):
        blocks = product_of((xh, xl), i, 1, 2, own_l, 0)
        for k in range(2):
            for j in range(2):
                p = 2 * i + j
                value = w0[k, p] + blocks[k][j]
                w0[k, p] = value
                high, low = halves(value)
                yh[p, BLK * (k + 1):BLK * (k + 2), :] = high
                yl[p, BLK * (k + 1):BLK * (k + 2), :] = low
                total = total + fold(value * vp[k, p])
        return total

    def ghost_apply(i, carry):
        blocks = product_of((xh, xl), i, 0, 3, ghost_l, 2)
        for side, row in ((0, 0), (1, 3)):
            for j in range(2):
                p = 2 * i + j
                high, low = halves(w_ghost[side, p] + blocks[side][j])
                yh[p, BLK * row:BLK * (row + 1), :] = high
                yl[p, BLK * row:BLK * (row + 1), :] = low
        return carry

    zeros = jnp.zeros((8, BLK), F32)
    spread(1, [lax.fori_loop(0, PAIRS, first_apply, zeros)])
    phys_product(yh, yl, w1)

    @pl.when(has_below)
    def _():
        base_up().wait_recv()
        envs_up().wait_recv()

    @pl.when(has_above)
    def _():
        base_down().wait_recv()
        envs_down().wait_recv()

    lefts = [halves(lr_ghost[side, 0]) for side in range(2)]
    for h in range(2):
        ghost_l[h] = jnp.concatenate([jnp.concatenate([lefts[0][h], none], axis=1),
                                      jnp.concatenate([none, lefts[1][h]], axis=1)], axis=0)
    for side in range(2):
        right_w[2 + side] = right_of(lr_ghost[side, 1])
    lax.fori_loop(0, PAIRS, ghost_apply, 0)
    corr = collect(1, 1)[0]
    corrs = jnp.broadcast_to(corr, (BLK, BLK))

    def finish(i, totals):
        rr, w0r, rt, vt, w0t, tt = totals
        blocks = product_of((yh, yl), i, 1, 2, own_a, 0)
        value = split_dot((ghost_a[0], ghost_a[1]), pair_of((yh, yl), i, 0, 3))
        for k in range(2):
            for j in range(2):
                p = 2 * i + j
                applied = w0[k, p]
                wave = vp[k, p]
                residual = applied - corrs * wave
                turned = (w1[k, p] + blocks[k][j] + value[BLK * k:BLK * (k + 1), BLK * j:BLK * (j + 1)]
                          - corrs * applied)
                r0[k, p] = residual
                w1[k, p] = turned
                high, low = halves(turned)
                xh[p, BLK * (k + 1):BLK * (k + 2), :] = high
                xl[p, BLK * (k + 1):BLK * (k + 2), :] = low
                rr = rr + fold(residual * residual)
                w0r = w0r + fold(applied * residual)
                rt = rt + fold(residual * turned)
                vt = vt + fold(wave * turned)
                w0t = w0t + fold(applied * turned)
                tt = tt + fold(turned * turned)
        return rr, w0r, rt, vt, w0t, tt

    def turned_down(part):
        at = pl.ds(2 * part, 2)
        return remote(w1.at[0, at], t_ghost.at[0, at], send_t.at[0, part], recv_t.at[0, part], below)

    def turned_up(part):
        return remote(w1.at[1, pl.ds(PAIRS + 2 * part, 2)], t_ghost.at[1, pl.ds(2 * part, 2)],
                      send_t.at[1, part], recv_t.at[1, part], above)

    totals = (zeros,) * 6
    for part in range(CHUNKS):
        totals = lax.fori_loop(0, 2, lambda n, c: finish(part + CHUNKS * n, c), totals)

        @pl.when(has_below)
        def _():
            turned_down(part).start()

        @pl.when(has_above)
        def _():
            turned_up(part).start()
    w0t, tt = totals[4:]
    spread(2, list(totals[:4]))

    def third_apply(i, total):
        blocks = product_of((xh, xl), i, 1, 2, own_a, 0)
        for k in range(2):
            for j in range(2):
                total = total + fold(blocks[k][j] * w1[k, 2 * i + j])
        return total

    def third_phys(i, total):
        for k in range(2):
            value = phys_piece(xh, xl, k, i)
            at = pl.multiple_of(32 * i, 32)
            for p in range(PHYS):
                rows = value[PHYS * p:PHYS * (p + 1)]
                both = jnp.concatenate([rows[:, :BLK], rows[:, BLK:]], axis=0)
                total = total + fold(both * w1[k, p, pl.ds(at, 32), :])
        return total

    def cross(i, carry):
        p = 2 * i
        rhs = [jnp.concatenate([
            jnp.concatenate([ref[p + j, 2 * BLK:3 * BLK, :], ref[p + PAIRS + j, BLK:2 * BLK, :]], axis=0)
            for j in range(2)], axis=1) for ref in (xh, xl)]
        value = split_dot((cross_a[0], cross_a[1]), rhs)
        for side in range(2):
            for j in range(2):
                crossed[side, p + j] = value[BLK * side:BLK * (side + 1), BLK * j:BLK * (j + 1)]
        return carry

    lax.fori_loop(0, PAIRS // 2, cross, 0)
    tht = lax.fori_loop(0, PAIRS, third_apply, zeros)
    tht = lax.fori_loop(0, BLK // 32, third_phys, tht)

    rr, w0r, rt, vt = collect(2, 4)
    norm = jnp.sqrt(rr + EPS)
    curvature = rt / (rr + EPS)
    coupled = w0r / norm
    ritz = 0.5 * (corr + curvature) - jnp.sqrt(0.25 * (corr - curvature) ** 2 + coupled * coupled)
    coef = ritz - corr
    magnitude = jnp.sqrt(coupled * coupled + coef * coef)
    wave_v = coupled / magnitude
    wave_r = coef / (magnitude * norm)
    corr2 = wave_v * wave_v * corr + wave_v * wave_r * (vt + w0r) + wave_r * wave_r * rt
    res_v = wave_v * (corr - corr2)
    res_r = wave_v - corr2 * wave_r
    res_t = wave_r

    loads[5].wait()
    masks = [(lax.broadcasted_iota(jnp.int32, (1, BLK), 1) < kept_ref[0, k]).astype(F32) for k in range(2)]
    wide = [jnp.broadcast_to(value, (BLK, BLK)) for value in (wave_v, wave_r, wave_v * corr, res_v, res_r, res_t)]

    def second_residual(p, totals):
        rr2, ar2, mww, mwr, mrr = totals
        for k in range(2):
            wave, residual, turned = vp[k, p], r0[k, p], w1[k, p]
            now = wide[0] * wave + wide[1] * residual
            applied = wide[2] * wave + wide[0] * residual + wide[1] * turned
            second = wide[3] * wave + wide[4] * residual + wide[5] * turned
            rr2 = rr2 + fold(second * second)
            ar2 = ar2 + fold(applied * second)
            mww = mww + masks[k] * fold(now * now)
            mwr = mwr + masks[k] * fold(now * second)
            mrr = mrr + masks[k] * fold(second * second)
        return rr2, ar2, mww, mwr, mrr

    finals = lax.fori_loop(0, PHYS, second_residual, (zeros,) * 5)

    for part in range(CHUNKS):
        @pl.when(has_above)
        def _():
            turned_down(part).wait_recv()

        @pl.when(has_below)
        def _():
            turned_up(part).wait_recv()

    def meet(i, total):
        return total + fold(crossed[0, i] * t_ghost[0, i]) + fold(crossed[1, i] * t_ghost[1, i])

    tht = tht + 2.0 * lax.fori_loop(0, PAIRS, meet, zeros)
    spread(3, list(finals) + [tht, w0t, tt])
    rr2, ar2, mww, mwr, mrr, tht, w0t, tt = collect(3, 8)
    norm2 = jnp.sqrt(rr2 + EPS)
    turned2 = (res_v * res_v * corr + res_r * res_r * rt + res_t * res_t * tht
               + 2.0 * (res_v * res_r * vt + res_v * res_t * w0t + res_r * res_t * tt))
    curvature = turned2 / (rr2 + EPS)
    coupled = ar2 / norm2
    ritz = 0.5 * (corr2 + curvature) - jnp.sqrt(0.25 * (corr2 - curvature) ** 2 + coupled * coupled)
    coef = ritz - corr2
    magnitude = jnp.sqrt(coupled * coupled + coef * coef)
    of_wave = coupled / magnitude
    of_res = coef / (magnitude * norm2)
    kept = of_wave * of_wave * mww + 2.0 * of_wave * of_res * mwr + of_res * of_res * mrr
    scale = 1.0 / jnp.sqrt(kept + EPS)
    energy_ref[...] = jnp.broadcast_to(ritz, (8, BLK))
    last = [jnp.broadcast_to(scale * value, (BLK, BLK)) for value in (
        of_wave * wave_v + of_res * res_v, of_wave * wave_r + of_res * res_r, of_res * res_t)]

    def write(p, carry):
        for k in range(2):
            value = last[0] * vp[k, p] + last[1] * r0[k, p] + last[2] * w1[k, p]
            out_ref[k, p] = value * masks[k]
        return carry

    lax.fori_loop(0, PHYS, write, 0)

    for column in range(NX):
        @pl.when(x != column)
        def _():
            deal(column).wait_send()
    for at in range(3):
        for part in range(2):
            @pl.when(sends[at][part])
            def _():
                step(at, part).wait_send()

    @pl.when(zz < 3)
    def _():
        far_copy(0).wait_send()
    for slot in range(NX):
        @pl.when(my_slot != slot)
        def _():
            give(slot).wait_send()
    for at in range(4):
        for hop in range(1, NS):
            remote(sums.at[at, sector], sums.at[at, sector], send_p.at[at, hop], recv_p.at[at, sector],
                   (chain, peer(hop))).wait_send()

    @pl.when(has_above)
    def _():
        coupling_up().wait_send()
        ghost_up().wait_send()
        base_up().wait_send()
        envs_up().wait_send()
        for part in range(CHUNKS):
            turned_up(part).wait_send()

    @pl.when(has_below)
    def _():
        ghost_down().wait_send()
        base_down().wait_send()
        envs_down().wait_send()
        for part in range(CHUNKS):
            turned_down(part).wait_send()


def write_kernel(wave_ref, energy_in, left_in, out_ref, energy_ref, left_ref, rows, sem):
    left_copy = pltpu.make_async_copy(left_in, left_ref, sem.at[8])
    left_copy.start()
    energy_ref[0] = jnp.sum(energy_in[0:1, 0:1])
    copies = []
    for k in range(2):
        for part in range(CHUNKS):
            size = ROWS // CHUNKS
            for p in range(PHYS):
                rows[k, pl.ds(size * part + p, size // PHYS, stride=PHYS), :] = (
                    wave_ref[k, p, size // PHYS * part:size // PHYS * (part + 1), :])
            at = pl.ds(size * part, size)
            copies.append(pltpu.make_async_copy(rows.at[k, at], out_ref.at[k, at], sem.at[CHUNKS * k + part]))
            copies[-1].start()
    for copy in copies:
        copy.wait()
    left_copy.wait()


def per_device(wave_start, transfer, energy_terms, coupling, physical, kept_ranks):
    hbm = pl.BlockSpec(memory_space=pltpu.HBM)
    vmem = pl.BlockSpec(memory_space=pltpu.VMEM)
    smem = pl.BlockSpec(memory_space=pltpu.SMEM)
    dma = pltpu.SemaphoreType.DMA

    def square(*lead):
        return pltpu.VMEM((*lead, BLK, BLK), F32)

    def wide(*lead):
        return pltpu.VMEM((*lead, 2 * BLK, 2 * BLK), BF16)

    split_waves = pltpu.VMEM((PHYS, 4 * BLK, BLK), BF16)
    wave, energy, left = pl.pallas_call(
        update_kernel,
        out_shape=(
            jax.ShapeDtypeStruct((2, PHYS, BLK, BLK), F32),
            jax.ShapeDtypeStruct((8, BLK), F32),
            jax.ShapeDtypeStruct((2, BLK, BLK), F32),
        ),
        in_specs=[hbm] * 6,
        out_specs=(vmem, vmem, vmem),
        scratch_shapes=[
            pltpu.VMEM((2, ROWS, BLK), F32), square(2), square(2), square(2), pltpu.VMEM((PHYS, PHYS), F32),
            pltpu.SMEM((1, 2), jnp.int32),
            square(NX, 2), square(NX, 2), square(3, 2), square(3, 2), square(), square(2, PHYS), square(NX), square(NX),
            pltpu.VMEM((2, ROWS, BLK), F32), square(), square(2, PHYS), square(2, PHYS), square(2, PHYS), square(2, PHYS),
            square(2, PHYS), square(2, PAIRS), square(2, 2), square(2, PAIRS),
            split_waves, split_waves, split_waves, split_waves,
            wide(2), wide(2), wide(2), wide(2), wide(2), wide(4), wide(2),
            pltpu.VMEM((4, NS, 8, BLK), F32),
            dma((6,)), dma((NX,)), dma((NX,)), dma((3, 2)), dma((3, 2)), dma((1,)), dma((1,)), dma((NX,)), dma((NX,)),
            dma((5,)), dma((5,)), dma((2,)), dma((2,)), dma((2, CHUNKS)), dma((2, CHUNKS)),
            dma((4, NS)), dma((4, NS)),
        ],
        compiler_params=pltpu.CompilerParams(
            collective_id=0, has_side_effects=True, vmem_limit_bytes=50 << 20),
    )(*[pltpu.with_memory_space_constraint(value, pltpu.HBM) for value in (
        wave_start.reshape(2, ROWS, BLK), transfer[0], energy_terms[0], coupling[0], physical[0], kept_ranks)])
    out, energy, left = pl.pallas_call(
        write_kernel,
        out_shape=(
            jax.ShapeDtypeStruct((2, ROWS, BLK), F32),
            jax.ShapeDtypeStruct((1,), F32),
            jax.ShapeDtypeStruct((2, BLK, BLK), F32),
        ),
        in_specs=[vmem] * 3,
        out_specs=(hbm, smem, hbm),
        scratch_shapes=[pltpu.VMEM((2, ROWS, BLK), F32), dma((9,))],
    )(*[pltpu.with_memory_space_constraint(value, pltpu.VMEM) for value in (wave, energy, left)])
    return (out.reshape(wave_start.shape), energy, left[None])


def solution(mesh):
    placed = (
        P("chain", "sector", None, None, None),
        P("chain", "sector", None, None),
        P("chain", "sector", None, None),
        P("chain", "sector", None, None),
        P("chain", None, None),
        P("chain", "sector"),
    )
    return jax.shard_map(
        per_device,
        mesh=mesh,
        in_specs=placed,
        out_specs=(
            P("chain", "sector", None, None, None),
            P("chain"),
            P("chain", "sector", None, None),
        ),
        check_vma=False,
    )
```

```python
import functools

import jax
import jax.numpy as jnp
from jax import lax
from jax.experimental import pallas as pl
from jax.experimental.pallas import tpu as pltpu
from jax.sharding import PartitionSpec as P

BLK = 128
PHYS = 16
NX = 4
NZ = 8
NS = 8
ROWS = BLK * PHYS
CHUNKS = 4
CHUNK = PHYS // CHUNKS
PAIRS = PHYS // 2

EPS = 1e-06
MESH = pl.DeviceIdType.MESH
F32 = jnp.float32
BF16 = jnp.bfloat16
NN = (((1,), (0,)), ((), ()))
NT = (((1,), (1,)), ((), ()))


def halves(value):
    high = value.astype(BF16)
    return high, (value - high.astype(F32)).astype(BF16)


def dot(lhs, rhs, dims=NN):
    return lax.dot_general(lhs, rhs, dims, preferred_element_type=F32)


def product(lhs, rhs, dims=NN):
    lhs_high, lhs_low = halves(lhs)
    rhs_high, rhs_low = halves(rhs)
    both = jnp.concatenate([lhs_high, lhs_low], axis=1)
    twice = jnp.concatenate([rhs_high, rhs_high], axis=1 if dims is NT else 0)
    return dot(both, twice, dims) + dot(lhs_high, rhs_low, dims)


def split_dot(lhs, rhs):
    return dot(lhs[0], rhs[0]) + (dot(lhs[0], rhs[1]) + dot(lhs[1], rhs[0]))


def packed(matrix):
    high, low = halves(matrix)
    return jnp.concatenate([jnp.concatenate([high, high], axis=1),
                            jnp.concatenate([low, jnp.zeros_like(low)], axis=1)], axis=0)


def packed_dot(matrix, refs, p, row):
    rows = slice(BLK * row, BLK * (row + 1))
    rhs = jnp.concatenate([jnp.concatenate([ref[p + j, rows, :] for ref in refs], axis=0) for j in range(2)], axis=1)
    value = dot(matrix, rhs)
    value = value[:BLK] + value[BLK:]
    return value[:, :BLK], value[:, BLK:]


def carry_over(matrix, env, source):
    return product(product(matrix, env), matrix, NT) + source


def fold(value):
    return jnp.sum(value.reshape(-1, 8, BLK), axis=0)


def remote(src, dst, send_sem, recv_sem, device):
    return pltpu.make_async_remote_copy(src, dst, send_sem, recv_sem, device_id=device, device_id_type=MESH)


def update_kernel(v_hbm, t_hbm, e_hbm, c_hbm, p_hbm, kept_hbm, vp, r0, w1, last_ref, left_ref,
                  v_ref, t_ref, e_ref, c_ref, p_ref, kept_ref,
                  mine, elements, window, came, far, partial, outward, ends, envs,
                  ghost, ghost_c, w0, w_ghost, t_ghost, lr_ghost, crossed,
                  xh, xl, yh, yl, left_w, own_a, ghost_a, cross_a, right_w, phys_a, sums,
                  load, send_a, recv_a, send_z, recv_z, send_f, recv_f, send_e, recv_e,
                  send_v, recv_v, send_w, recv_w, send_t, recv_t, send_p, recv_p):
    chain = lax.axis_index("chain")
    sector = lax.axis_index("sector")
    x = lax.rem(chain, NX)
    z = lax.div(chain, NX)
    odd = lax.rem(x, 2)
    zz = z + odd * (NZ - 1 - 2 * z)
    my_slot = x + odd * (NX - 1 - 2 * x)
    has_below = sector > 0
    has_above = sector < NS - 1
    below = (chain, sector - 1)
    above = (chain, sector + 1)

    def in_row(other):
        return (z * NX + other, sector)

    def in_column(other):
        return ((other + odd * (NZ - 1 - 2 * other)) * NX + x, sector)

    def slot_of(column):
        return x if column % 2 == 0 else NX - 1 - x

    def peer(hop):
        return lax.rem(sector + hop, NS)

    loads = [pltpu.make_async_copy(src, dst, load.at[i]) for i, (src, dst) in enumerate((
        (t_hbm, t_ref), (e_hbm, e_ref), (v_hbm, v_ref), (c_hbm, c_ref), (p_hbm, p_ref),
        (kept_hbm, kept_ref)))]
    for copy in loads:
        copy.start()

    barrier = pltpu.get_barrier_semaphore()
    greeted = NX - 1 + NS - 1
    for hop in range(1, NX):
        pl.semaphore_signal(barrier, inc=1, device_id=in_row(lax.rem(x + hop, NX)), device_id_type=MESH)
    for hop in range(1, NS):
        pl.semaphore_signal(barrier, inc=1, device_id=(chain, peer(hop)), device_id_type=MESH)
    for hop in (1, 2, 5):
        for other, there in ((zz + hop, zz + hop < NZ), (zz - hop, zz >= hop)):
            @pl.when(there)
            def _():
                pl.semaphore_signal(barrier, inc=1, device_id=in_column(other), device_id_type=MESH)
            greeted = greeted + there.astype(jnp.int32)

    loads[0].wait()
    loads[1].wait()
    for k in range(2):
        transfer = t_ref[k]
        source = 0.5 * (e_ref[k] + e_ref[k].T)
        mine[2 * k, 0] = transfer.T
        mine[2 * k + 1, 0] = transfer
        mine[2 * k, 1] = source
        mine[2 * k + 1, 1] = source
    pl.semaphore_wait(barrier, greeted)

    def spread(at, parts):
        rows = [jnp.sum(part, axis=0, keepdims=True) for part in parts]
        rows += [jnp.zeros((1, BLK), F32)] * (16 - len(rows))
        sums[at, pl.ds(sector, 1)] = jnp.concatenate(rows, axis=0)[None]
        for hop in range(1, NS):
            remote(sums.at[at, sector], sums.at[at, sector], send_p.at[at, hop], recv_p.at[at, sector],
                   (chain, peer(hop))).start()

    def collect(at, count):
        for hop in range(1, NS):
            other = peer(hop)
            remote(sums.at[at, other], sums.at[at, other], send_p.at[at, hop], recv_p.at[at, other],
                   (chain, other)).wait_recv()
        total = sums[at, 0]
        for other in range(1, NS):
            total = total + sums[at, other]
        total = jnp.sum(total, axis=1, keepdims=True)
        return [total[i:i + 1] for i in range(count)]

    def deal(column):
        slot = slot_of(column)
        return remote(mine.at[column], elements.at[slot], send_a.at[column], recv_a.at[slot], in_row(column))

    for hop in (2, 1, 3):
        for column in range(NX):
            @pl.when(column == lax.rem(x + hop, NX))
            def _():
                deal(column).start()
    elements[pl.ds(my_slot, 1)] = mine[pl.ds(x, 1)]

    def ghost_up():
        return remote(v_hbm.at[1], ghost.at[0], send_v.at[0], recv_v.at[0], above)

    def ghost_down():
        return remote(v_hbm.at[0], ghost.at[1], send_v.at[1], recv_v.at[1], below)

    def coupling_up():
        return remote(c_hbm.at[1], ghost_c, send_v.at[2], recv_v.at[2], above)

    @pl.when(has_above)
    def _():
        coupling_up().start()

    def square(i, total):
        part = v_ref[:, pl.ds(pl.multiple_of(i * 256, 256), 256), :]
        return total + fold(part * part)

    loads[2].wait()
    spread(0, [lax.fori_loop(0, 8, square, jnp.zeros((8, BLK), F32))])

    square_zero = jnp.zeros((BLK, BLK), F32)
    for ref, unused in (
            (came.at[0, 0], (zz < 2) | (zz == NZ - 1)), (came.at[0, 1], (zz < 1) | (zz == NZ - 1)),
            (came.at[1, 0], (zz < 4) | (zz == NZ - 1)), (came.at[1, 1], (zz < 2) | (zz == NZ - 1)),
            (came.at[2, 0], zz < 5), (came.at[2, 1], zz < 1), (far, zz < 5)):
        @pl.when(unused)
        def _():
            ref[...] = square_zero

    @pl.when(sector == 0)
    def _():
        ghost[0] = jnp.zeros((ROWS, BLK), F32)
        ghost_c[...] = square_zero
        w_ghost[0] = jnp.zeros((PHYS, BLK, BLK), F32)
        t_ghost[0] = jnp.zeros((PAIRS, BLK, BLK), F32)
        lr_ghost[0] = jnp.zeros((2, BLK, BLK), F32)

    @pl.when(sector == NS - 1)
    def _():
        ghost[1] = jnp.zeros((ROWS, BLK), F32)
        w_ghost[1] = jnp.zeros((PHYS, BLK, BLK), F32)
        t_ghost[1] = jnp.zeros((PAIRS, BLK, BLK), F32)
        lr_ghost[1] = jnp.zeros((2, BLK, BLK), F32)

    for slot in range(NX):
        @pl.when(my_slot != slot)
        def _():
            remote(mine.at[slot], elements.at[slot], send_a.at[slot], recv_a.at[slot],
                   in_row(lax.rem(x + 1, NX))).wait_recv()

    @pl.when(has_above)
    def _():
        ghost_up().start()

    @pl.when(has_below)
    def _():
        ghost_down().start()

    q0, q1, q2, q3 = [elements[s, 0] for s in range(NX)]
    s0, s1, s2, s3 = [elements[s, 1] for s in range(NX)]
    q01 = product(q1, q0)
    y01 = carry_over(q1, s0, s1)
    q23 = product(q3, q2)
    y23 = carry_over(q3, s2, s3)
    qw = product(q23, q01)
    yw = carry_over(q23, y01, y23)

    hops = (1, 2, 1)
    sends = (((zz >= 1) & (zz <= 5), zz <= 5), ((zz >= 2) & (zz <= 4), zz <= 4), ((zz >= 4) & (zz <= 6), zz <= 6))
    takes = (((zz >= 2) & (zz <= 6), (zz >= 1) & (zz <= 6)), ((zz >= 4) & (zz <= 6), (zz >= 2) & (zz <= 6)),
             (zz >= 5, zz >= 1))

    def step(at, part):
        return remote(window.at[at, part], came.at[at, part], send_z.at[at, part], recv_z.at[at, part],
                      in_column(zz + hops[at]))

    def send(at, part, value):
        window[at, part] = value

        @pl.when(sends[at][part])
        def _():
            step(at, part).start()

    def receive(at, part):
        @pl.when(takes[at][part])
        def _():
            remote(window.at[at, part], came.at[at, part], send_z.at[at, part], recv_z.at[at, part],
                   in_column(zz - hops[at])).wait_recv()
        return came[at, part]

    def far_copy(at):
        return remote(window.at[at, 1], far, send_f.at[0], recv_f.at[0], in_column(zz + 5))

    def send_far(at):
        @pl.when(zz == at)
        def _():
            far_copy(at).start()

    def start_wave():
        inverse = 1.0 / jnp.sqrt(collect(0, 1)[0])
        inverses = jnp.broadcast_to(inverse, (BLK, BLK))

        def one(p, carry):
            for k in range(2):
                value = v_ref[k, pl.ds(p, BLK, stride=PHYS), :] * inverses
                vp[k, p] = value
                high, low = halves(value)
                xh[p, BLK * (k + 1):BLK * (k + 2), :] = high
                xl[p, BLK * (k + 1):BLK * (k + 2), :] = low
            return carry

        lax.fori_loop(0, PHYS, one, 0)
        return inverses

    def make_phys():
        loads[4].wait()
        sym = 0.5 * (p_ref[...] + p_ref[...].T)
        lane = lax.broadcasted_iota(jnp.int32, (PHYS, 256), 1)
        row = lax.broadcasted_iota(jnp.int32, (PHYS, 256), 0)
        spread_p = (lax.div(lane, PHYS) == row).astype(BF16)
        same = (lax.rem(lane, PHYS) == row).astype(F32)
        for i, half in enumerate(halves(sym)):
            wide = dot(half, spread_p)
            for p in range(PHYS):
                phys_a[i, PHYS * p:PHYS * (p + 1), :] = (wide[p:p + 1, :] * same).astype(BF16)

    def phys_rows(ref, k, i):
        first = pl.multiple_of(BLK * (k + 1) + 32 * i, 32)
        second = pl.multiple_of(BLK * (k + 1) + 32 * i + 16, 16)
        return jnp.concatenate([
            jnp.concatenate([ref[p, pl.ds(at, 16), :] for p in range(PHYS)], axis=0)
            for at in (first, second)], axis=1)

    def phys_piece(high, low, k, i):
        return split_dot((phys_a[0], phys_a[1]), (phys_rows(high, k, i), phys_rows(low, k, i)))

    def phys_product(high, low, dst):
        def one(i, carry):
            for k in range(2):
                value = phys_piece(high, low, k, i)
                at = pl.multiple_of(32 * i, 32)
                for p in range(PHYS):
                    rows = value[PHYS * p:PHYS * (p + 1)]
                    dst[k, p, pl.ds(at, 32), :] = jnp.concatenate([rows[:, :BLK], rows[:, BLK:]], axis=0)
            return carry

        lax.fori_loop(0, BLK // 32, one, 0)

    def make_ghost_matrices():
        loads[3].wait()
        zero = jnp.zeros((BLK, BLK), BF16)
        own_up = halves(c_ref[0])
        own_down = halves(c_ref[0].T)
        for i in range(2):
            own_a[i] = jnp.concatenate([jnp.concatenate([zero, own_down[i]], axis=1),
                                        jnp.concatenate([own_up[i], zero], axis=1)], axis=0)
        last = c_ref[1] * has_above.astype(F32)
        ghost_a[0] = packed(ghost_c[...])
        ghost_a[1] = packed(last.T)
        cross_a[0] = packed(ghost_c[...].T)
        cross_a[1] = packed(last)

    def pair_of(refs, i, low, high):
        p = 2 * i
        return [jnp.concatenate([
            jnp.concatenate([ref[p + j, BLK * low:BLK * (low + 1), :], ref[p + j, BLK * high:BLK * (high + 1), :]], axis=0)
            for j in range(2)], axis=1) for ref in refs]

    def add_own(i, carry):
        value = split_dot((own_a[0], own_a[1]), pair_of((xh, xl), i, 1, 2))
        for k in range(2):
            for j in range(2):
                p = 2 * i + j
                both = w0[k, p] + value[BLK * k:BLK * (k + 1), BLK * j:BLK * (j + 1)]
                w0[k, p] = both
                partial[k, p] = both
        return carry

    def add_to_ghosts(i, carry):
        for side in range(2):
            blocks = packed_dot(cross_a[side], (xh, xl), 2 * i, side + 1)
            for j in range(2):
                outward[side, 2 * i + j] = blocks[j]
        return carry

    def add_ghosts(i, inverses):
        for side, row in ((0, 0), (1, 3)):
            for j in range(2):
                p = 2 * i + j
                high, low = halves(ghost[side, pl.ds(p, BLK, stride=PHYS), :] * inverses)
                xh[p, BLK * row:BLK * (row + 1), :] = high
                xl[p, BLK * row:BLK * (row + 1), :] = low
            blocks = packed_dot(ghost_a[side], (xh, xl), 2 * i, row)
            for j in range(2):
                w0[side, 2 * i + j] = w0[side, 2 * i + j] + blocks[j]
        return inverses

    def base_down():
        return remote(partial.at[0], w_ghost.at[1], send_w.at[0], recv_w.at[0], below)

    def base_up():
        return remote(partial.at[1], w_ghost.at[0], send_w.at[1], recv_w.at[1], above)

    send(0, 1, yw)
    send(0, 0, qw)
    send_far(0)
    q012 = product(q2, q01)
    y012 = carry_over(q2, y01, s2)
    inverses = start_wave()
    make_phys()

    @pl.when(has_below)
    def _():
        coupling_up().wait_recv()

    make_ghost_matrices()
    yw = carry_over(qw, receive(0, 1), yw)
    send(1, 1, yw)
    send_far(1)
    qw = product(qw, receive(0, 0))
    send(1, 0, qw)
    phys_product(xh, xl, w0)
    lax.fori_loop(0, PAIRS, add_own, 0)

    @pl.when(has_below)
    def _():
        base_down().start()

    @pl.when(has_above)
    def _():
        base_up().start()

    yw = carry_over(qw, receive(1, 1), yw)
    send(2, 1, yw)
    send_far(2)
    send(2, 0, product(qw, receive(1, 0)))

    @pl.when(has_below)
    def _():
        ghost_up().wait_recv()

    @pl.when(has_above)
    def _():
        ghost_down().wait_recv()

    inverses = lax.fori_loop(0, PAIRS // 2, add_ghosts, inverses)

    @pl.when(zz >= 5)
    def _():
        remote(window.at[2, 1], far, send_f.at[0], recv_f.at[0], in_column(zz - 5)).wait_recv()
    y_near = receive(2, 1)
    start = carry_over(receive(2, 0), far[...], y_near)

    def owner(slot):
        return slot + odd * (NX - 1 - 2 * slot)

    def give(slot):
        return remote(ends.at[slot], envs.at[x], send_e.at[slot], recv_e.at[x], in_row(owner(slot)))

    ends[0] = start
    for slot, (q, y) in enumerate(((q0, s0), (q01, y01), (q012, y012))):
        ends[slot + 1] = carry_over(q, start, y)
    for hop in (2, 1, 3):
        for slot in range(NX):
            @pl.when(slot == lax.rem(my_slot + hop, NX))
            def _():
                give(slot).start()
    envs[pl.ds(x, 1)] = ends[pl.ds(my_slot, 1)]
    lax.fori_loop(PAIRS // 2, PAIRS, add_ghosts, inverses)
    lax.fori_loop(0, PAIRS, add_to_ghosts, 0)
    for column in range(NX):
        @pl.when(x != column)
        def _():
            remote(ends.at[column], envs.at[column], send_e.at[column], recv_e.at[column], in_row(column)).wait_recv()

    def envs_down():
        return remote(envs.at[pl.ds(0, 2)], lr_ghost.at[1], send_v.at[3], recv_v.at[3], below)

    def envs_up():
        return remote(envs.at[pl.ds(2, 2)], lr_ghost.at[0], send_v.at[4], recv_v.at[4], above)

    @pl.when(has_below)
    def _():
        envs_down().start()

    @pl.when(has_above)
    def _():
        envs_up().start()

    def right_of(env):
        high, low = halves(env)
        return jnp.concatenate([jnp.concatenate([high, low], axis=1),
                                jnp.concatenate([high, jnp.zeros_like(low)], axis=1)], axis=0)

    for k in range(2):
        left_ref[k] = envs[2 * k]
        right_w[k] = right_of(envs[2 * k + 1])
    none = jnp.zeros((BLK, BLK), BF16)

    lefts = [halves(envs[2 * k]) for k in range(2)]
    for h in range(2):
        own_a[h] = own_a[h] + jnp.concatenate([jnp.concatenate([lefts[0][h], none], axis=1),
                                               jnp.concatenate([none, lefts[1][h]], axis=1)], axis=0)
        left_w[h] = packed(envs[2 * h])

    def right_products(refs, p, row, matrix):
        rows = slice(BLK * row, BLK * (row + 1))
        lhs = jnp.concatenate([jnp.concatenate([ref[p + j, rows, :] for ref in refs], axis=1)
                               for j in range(2)], axis=0)
        value = dot(lhs, matrix)
        value = value[:, :BLK] + value[:, BLK:]
        return value[:BLK], value[BLK:]

    def environment_products(refs, i, row, at):
        lefts = packed_dot(left_w[at], refs, 2 * i, row)
        rights = right_products(refs, 2 * i, row, right_w[at])
        return [left + right for left, right in zip(lefts, rights)]

    def first_apply(i, total):
        for k in range(2):
            blocks = environment_products((xh, xl), i, k + 1, k)
            for j in range(2):
                p = 2 * i + j
                value = w0[k, p] + blocks[j]
                w0[k, p] = value
                high, low = halves(value)
                yh[p, BLK * (k + 1):BLK * (k + 2), :] = high
                yl[p, BLK * (k + 1):BLK * (k + 2), :] = low
                total = total + fold(value * vp[k, p])
        return total

    def ghost_apply(i, carry):
        for side, row in ((0, 0), (1, 3)):
            blocks = environment_products((xh, xl), i, row, 2 + side)
            for j in range(2):
                p = 2 * i + j
                high, low = halves(w_ghost[side, p] + outward[side, p] + blocks[j])
                yh[p, BLK * row:BLK * (row + 1), :] = high
                yl[p, BLK * row:BLK * (row + 1), :] = low
        return carry

    zeros = jnp.zeros((8, BLK), F32)
    spread(1, [lax.fori_loop(0, PAIRS, first_apply, zeros)])
    phys_product(yh, yl, w1)

    @pl.when(has_below)
    def _():
        envs_up().wait_recv()

    @pl.when(has_above)
    def _():
        envs_down().wait_recv()

    for side in range(2):
        left_w[2 + side] = packed(lr_ghost[side, 0])
        right_w[2 + side] = right_of(lr_ghost[side, 1])

    @pl.when(has_below)
    def _():
        base_up().wait_recv()

    @pl.when(has_above)
    def _():
        base_down().wait_recv()

    lax.fori_loop(0, PAIRS, ghost_apply, 0)
    corr = collect(1, 1)[0]
    corrs = jnp.broadcast_to(corr, (BLK, BLK))

    def finish(i, totals):
        rr, rt, vt, tt = totals
        value = split_dot((own_a[0], own_a[1]), pair_of((yh, yl), i, 1, 2))
        for k in range(2):
            ghosts = packed_dot(ghost_a[k], (yh, yl), 2 * i, 3 * k)
            rights = right_products((yh, yl), 2 * i, k + 1, right_w[k])
            for j in range(2):
                p = 2 * i + j
                applied = w0[k, p]
                wave = vp[k, p]
                residual = applied - corrs * wave
                turned = (w1[k, p] + rights[j] + ghosts[j] + value[BLK * k:BLK * (k + 1), BLK * j:BLK * (j + 1)]
                          - corrs * applied)
                r0[k, p] = residual
                w1[k, p] = turned
                high, low = halves(turned)
                xh[p, BLK * (k + 1):BLK * (k + 2), :] = high
                xl[p, BLK * (k + 1):BLK * (k + 2), :] = low
                rr = rr + fold(residual * residual)
                rt = rt + fold(residual * turned)
                vt = vt + fold(wave * turned)
                tt = tt + fold(turned * turned)
        return rr, rt, vt, tt

    def turned_down(part):
        at = pl.ds(2 * part, 2)
        return remote(w1.at[0, at], t_ghost.at[1, at], send_t.at[0, part], recv_t.at[0, part], below)

    def turned_up(part):
        return remote(w1.at[1, pl.ds(PAIRS + 2 * part, 2)], t_ghost.at[0, pl.ds(2 * part, 2)],
                      send_t.at[1, part], recv_t.at[1, part], above)

    totals = (zeros,) * 4
    for part in range(CHUNKS):
        totals = lax.fori_loop(0, 2, lambda n, c: finish(part + CHUNKS * n, c), totals)

        @pl.when(has_below)
        def _():
            turned_down(part).start()

        @pl.when(has_above)
        def _():
            turned_up(part).start()

    def third_apply(i, total):
        rhs = pair_of((xh,), i, 1, 2)[0]
        value = dot(own_a[0], rhs) + dot(own_a[1], rhs)
        for k in range(2):
            rights = right_products((xh,), 2 * i, k + 1, right_w[k, :BLK])
            for j in range(2):
                p = 2 * i + j
                both = 2.0 * w1[k, p] - xh[p, BLK * (k + 1):BLK * (k + 2), :].astype(F32)
                image = value[BLK * k:BLK * (k + 1), BLK * j:BLK * (j + 1)] + rights[j]
                total = total + fold(image * both)
        return total

    def third_phys(i, total):
        at = pl.multiple_of(32 * i, 32)
        for k in range(2):
            rhs = phys_rows(xh, k, i)
            value = dot(phys_a[0], rhs) + dot(phys_a[1], rhs)
            for p in range(PHYS):
                rows = value[PHYS * p:PHYS * (p + 1)]
                image = jnp.concatenate([rows[:, :BLK], rows[:, BLK:]], axis=0)
                high = xh[p, pl.ds(pl.multiple_of(BLK * (k + 1) + 32 * i, 32), 32), :].astype(F32)
                total = total + fold(image * (2.0 * w1[k, p, pl.ds(at, 32), :] - high))
        return total

    def cross(i, carry):
        for side in range(2):
            blocks = packed_dot(cross_a[side], (xh, xl), 2 * i + PAIRS * (1 - side), side + 1)
            for j in range(2):
                crossed[side, 2 * i + j] = blocks[j]
        return carry

    lax.fori_loop(0, PAIRS // 2, cross, 0)
    tht = lax.fori_loop(0, PAIRS, third_apply, zeros)
    tht = lax.fori_loop(0, BLK // 32, third_phys, tht)

    loads[5].wait()
    masks = [(lax.broadcasted_iota(jnp.int32, (1, BLK), 1) < kept_ref[0, k]).astype(F32) for k in range(2)]

    def masked(p, grams):
        for k in range(2):
            vectors = (vp[k, p], r0[k, p], w1[k, p])
            pairs = [vectors[i] * vectors[j] for i in range(3) for j in range(i, 3)]
            grams = tuple(gram + masks[k] * fold(pair) for gram, pair in zip(grams, pairs))
        return grams

    grams = lax.fori_loop(0, PHYS, masked, (zeros,) * 6)

    for part in range(CHUNKS):
        @pl.when(has_above)
        def _():
            turned_down(part).wait_recv()

        @pl.when(has_below)
        def _():
            turned_up(part).wait_recv()

    def meet(i, total):
        return total + fold(crossed[0, i] * t_ghost[0, i]) + fold(crossed[1, i] * t_ghost[1, i])

    tht = tht + 2.0 * lax.fori_loop(0, PAIRS, meet, zeros)
    spread(2, list(totals) + [tht] + list(grams))
    rr, rt, vt, tt, tht, mvv, mvr, mvt, mrr, mrt, mtt = collect(2, 11)
    w0t = rt + corr * vt
    norm = jnp.sqrt(rr + EPS)
    curvature = rt / (rr + EPS)
    coupled = rr / norm
    ritz = 0.5 * (corr + curvature) - jnp.sqrt(0.25 * (corr - curvature) ** 2 + coupled * coupled)
    coef = ritz - corr
    magnitude = jnp.sqrt(coupled * coupled + coef * coef)
    wave_v = coupled / magnitude
    wave_r = coef / (magnitude * norm)
    corr2 = wave_v * wave_v * corr + wave_v * wave_r * (vt + rr) + wave_r * wave_r * rt
    res_v = wave_v * (corr - corr2)
    res_r = wave_v - corr2 * wave_r
    res_t = wave_r

    rr2 = res_v * res_v + res_r * res_r * rr + res_t * res_t * tt + 2.0 * res_t * (res_v * vt + res_r * rt)
    rr2 = jnp.maximum(rr2, 0.0)
    wr2 = wave_v * res_v + wave_r * res_r * rr + res_t * (wave_v * vt + wave_r * rt)
    ar2 = rr2 + corr2 * wr2
    norm2 = jnp.sqrt(rr2 + EPS)
    turned2 = (res_v * res_v * corr + res_r * res_r * rt + res_t * res_t * tht
               + 2.0 * (res_v * res_r * vt + res_v * res_t * w0t + res_r * res_t * tt))
    curvature = turned2 / (rr2 + EPS)
    coupled = ar2 / norm2
    ritz = 0.5 * (corr2 + curvature) - jnp.sqrt(0.25 * (corr2 - curvature) ** 2 + coupled * coupled)
    coef = ritz - corr2
    magnitude = jnp.sqrt(coupled * coupled + coef * coef)
    of_wave = coupled / magnitude
    of_res = coef / (magnitude * norm2)
    of_v = of_wave * wave_v + of_res * res_v
    of_r = of_wave * wave_r + of_res * res_r
    of_t = of_res * res_t
    kept = (of_v * of_v * mvv + of_r * of_r * mrr + of_t * of_t * mtt
            + 2.0 * (of_v * of_r * mvr + of_v * of_t * mvt + of_r * of_t * mrt))
    scale = 1.0 / jnp.sqrt(jnp.maximum(kept, 0.0) + EPS)
    last = [scale * value for value in (of_v, of_r, of_t)]
    last_ref[...] = jnp.concatenate(
        [jnp.broadcast_to(value, (1, BLK)) for value in last + [ritz]] + masks + [jnp.zeros((2, BLK), F32)], axis=0)

    for column in range(NX):
        @pl.when(x != column)
        def _():
            deal(column).wait_send()
    for at in range(3):
        for part in range(2):
            @pl.when(sends[at][part])
            def _():
                step(at, part).wait_send()

    @pl.when(zz < 3)
    def _():
        far_copy(0).wait_send()
    for slot in range(NX):
        @pl.when(my_slot != slot)
        def _():
            give(slot).wait_send()
    for at in range(3):
        for hop in range(1, NS):
            remote(sums.at[at, sector], sums.at[at, sector], send_p.at[at, hop], recv_p.at[at, sector],
                   (chain, peer(hop))).wait_send()

    @pl.when(has_above)
    def _():
        coupling_up().wait_send()
        ghost_up().wait_send()
        envs_up().wait_send()
        base_up().wait_send()
        for part in range(CHUNKS):
            turned_up(part).wait_send()

    @pl.when(has_below)
    def _():
        ghost_down().wait_send()
        envs_down().wait_send()
        base_down().wait_send()
        for part in range(CHUNKS):
            turned_down(part).wait_send()


def write_kernel(wave_ref, res_ref, turned_ref, last_ref, left_in, out_ref, energy_ref, left_ref, rows, sem):
    left_copy = pltpu.make_async_copy(left_in, left_ref, sem.at[8])
    left_copy.start()
    energy_ref[0] = jnp.sum(last_ref[3:4, 0:1])
    size = ROWS // CHUNKS
    count = size // PHYS
    copies = []
    for k in range(2):
        mask = last_ref[4 + k:5 + k, :]
        coefs = [jnp.broadcast_to(last_ref[i:i + 1, :] * mask, (count, BLK)) for i in range(3)]
        for part in range(CHUNKS):
            at = pl.ds(count * part, count)
            for p in range(PHYS):
                rows[k, pl.ds(size * part + p, count, stride=PHYS), :] = (
                    coefs[0] * wave_ref[k, p, at, :] + coefs[1] * res_ref[k, p, at, :] + coefs[2] * turned_ref[k, p, at, :])
            to = pl.ds(size * part, size)
            copies.append(pltpu.make_async_copy(rows.at[k, to], out_ref.at[k, to], sem.at[CHUNKS * k + part]))
            copies[-1].start()
    for copy in copies:
        copy.wait()
    left_copy.wait()


def per_device(wave_start, transfer, energy_terms, coupling, physical, kept_ranks):
    hbm = pl.BlockSpec(memory_space=pltpu.HBM)
    vmem = pl.BlockSpec(memory_space=pltpu.VMEM)
    smem = pl.BlockSpec(memory_space=pltpu.SMEM)
    dma = pltpu.SemaphoreType.DMA

    def square(*lead):
        return pltpu.VMEM((*lead, BLK, BLK), F32)

    def wide(*lead):
        return pltpu.VMEM((*lead, 2 * BLK, 2 * BLK), BF16)

    split_waves = pltpu.VMEM((PHYS, 4 * BLK, BLK), BF16)
    waves = jax.ShapeDtypeStruct((2, PHYS, BLK, BLK), F32)
    parts = pl.pallas_call(
        update_kernel,
        out_shape=(
            waves, waves, waves,
            jax.ShapeDtypeStruct((8, BLK), F32),
            jax.ShapeDtypeStruct((2, BLK, BLK), F32),
        ),
        in_specs=[hbm] * 6,
        out_specs=(vmem,) * 5,
        scratch_shapes=[
            pltpu.VMEM((2, ROWS, BLK), F32), square(2), square(2), square(2), pltpu.VMEM((PHYS, PHYS), F32),
            pltpu.SMEM((1, 2), jnp.int32),
            square(NX, 2), square(NX, 2), square(3, 2), square(3, 2), square(), square(2, PHYS), square(2, PHYS), square(NX), square(NX),
            pltpu.VMEM((2, ROWS, BLK), F32), square(), square(2, PHYS), square(2, PHYS),
            square(2, PAIRS), square(2, 2), square(2, PAIRS),
            split_waves, split_waves, split_waves, split_waves,
            wide(4), wide(2), wide(2), wide(2), wide(4), wide(2),
            pltpu.VMEM((3, NS, 16, BLK), F32),
            dma((6,)), dma((NX,)), dma((NX,)), dma((3, 2)), dma((3, 2)), dma((1,)), dma((1,)), dma((NX,)), dma((NX,)),
            dma((5,)), dma((5,)), dma((2,)), dma((2,)), dma((2, CHUNKS)), dma((2, CHUNKS)),
            dma((3, NS)), dma((3, NS)),
        ],
        compiler_params=pltpu.CompilerParams(
            collective_id=0, has_side_effects=True, vmem_limit_bytes=36 << 20),
    )(*[pltpu.with_memory_space_constraint(value, pltpu.HBM) for value in (
        wave_start.reshape(2, ROWS, BLK), transfer[0], energy_terms[0], coupling[0], physical[0], kept_ranks)])
    out, energy, left = pl.pallas_call(
        write_kernel,
        out_shape=(
            jax.ShapeDtypeStruct((2, ROWS, BLK), F32),
            jax.ShapeDtypeStruct((1,), F32),
            jax.ShapeDtypeStruct((2, BLK, BLK), F32),
        ),
        in_specs=[vmem] * 5,
        out_specs=(hbm, smem, hbm),
        scratch_shapes=[pltpu.VMEM((2, ROWS, BLK), F32), dma((9,))],
        compiler_params=pltpu.CompilerParams(vmem_limit_bytes=16 << 20),
    )(*[pltpu.with_memory_space_constraint(value, pltpu.VMEM) for value in parts])
    return (out.reshape(wave_start.shape), energy, left[None])


def solution(mesh):
    placed = (
        P("chain", "sector", None, None, None),
        P("chain", "sector", None, None),
        P("chain", "sector", None, None),
        P("chain", "sector", None, None),
        P("chain", None, None),
        P("chain", "sector"),
    )
    return jax.shard_map(
        per_device,
        mesh=mesh,
        in_specs=placed,
        out_specs=(
            P("chain", "sector", None, None, None),
            P("chain"),
            P("chain", "sector", None, None),
        ),
        check_vma=False,
    )
```

```python
import functools

import jax
import jax.numpy as jnp
from jax import lax
from jax.experimental import pallas as pl
from jax.experimental.pallas import tpu as pltpu
from jax.sharding import PartitionSpec as P

BLK = 128
PHYS = 16
NX = 4
NZ = 8
NS = 8
ROWS = BLK * PHYS
CHUNKS = 4
CHUNK = PHYS // CHUNKS
PAIRS = PHYS // 2

EPS = 1e-06
MESH = pl.DeviceIdType.MESH
F32 = jnp.float32
BF16 = jnp.bfloat16
NN = (((1,), (0,)), ((), ()))
NT = (((1,), (1,)), ((), ()))


def halves(value):
    high = value.astype(BF16)
    return high, (value - high.astype(F32)).astype(BF16)


def dot(lhs, rhs, dims=NN):
    return lax.dot_general(lhs, rhs, dims, preferred_element_type=F32)


def product(lhs, rhs, dims=NN):
    lhs_high, lhs_low = halves(lhs)
    rhs_high, rhs_low = halves(rhs)
    both = jnp.concatenate([lhs_high, lhs_low], axis=1)
    twice = jnp.concatenate([rhs_high, rhs_high], axis=1 if dims is NT else 0)
    return dot(both, twice, dims) + dot(lhs_high, rhs_low, dims)


def split_dot(lhs, rhs):
    return dot(lhs[0], rhs[0]) + (dot(lhs[0], rhs[1]) + dot(lhs[1], rhs[0]))


def packed(matrix):
    high, low = halves(matrix)
    return jnp.concatenate([jnp.concatenate([high, high], axis=1),
                            jnp.concatenate([low, jnp.zeros_like(low)], axis=1)], axis=0)


def packed_dot(matrix, refs, p, row):
    rows = slice(BLK * row, BLK * (row + 1))
    rhs = jnp.concatenate([jnp.concatenate([ref[p + j, rows, :] for ref in refs], axis=0) for j in range(2)], axis=1)
    value = dot(matrix, rhs)
    value = value[:BLK] + value[BLK:]
    return value[:, :BLK], value[:, BLK:]


def carry_over(matrix, env, source):
    return product(product(matrix, env), matrix, NT) + source


def fold(value):
    return jnp.sum(value.reshape(-1, 8, BLK), axis=0)


def remote(src, dst, send_sem, recv_sem, device):
    return pltpu.make_async_remote_copy(src, dst, send_sem, recv_sem, device_id=device, device_id_type=MESH)


def update_kernel(v_hbm, t_hbm, e_hbm, c_hbm, p_hbm, kept_hbm, vp, r0, w1, last_ref, left_ref,
                  v_ref, t_ref, e_ref, c_ref, p_ref, kept_ref,
                  mine, elements, window, came, far, partial, outward, ends, envs,
                  ghost, ghost_c, w0, w_ghost, t_ghost, lr_ghost, crossed,
                  xh, xl, yh, yl, left_w, own_a, ghost_a, cross_a, right_w, phys_a, sums,
                  load, send_a, recv_a, send_z, recv_z, send_f, recv_f, send_e, recv_e,
                  send_v, recv_v, send_w, recv_w, send_t, recv_t, send_p, recv_p):
    chain = lax.axis_index("chain")
    sector = lax.axis_index("sector")
    x = lax.rem(chain, NX)
    z = lax.div(chain, NX)
    odd = lax.rem(x, 2)
    zz = z + odd * (NZ - 1 - 2 * z)
    my_slot = x + odd * (NX - 1 - 2 * x)
    has_below = sector > 0
    has_above = sector < NS - 1
    below = (chain, sector - 1)
    above = (chain, sector + 1)

    def in_row(other):
        return (z * NX + other, sector)

    def in_column(other):
        return ((other + odd * (NZ - 1 - 2 * other)) * NX + x, sector)

    def slot_of(column):
        return x if column % 2 == 0 else NX - 1 - x

    def peer(hop):
        return lax.rem(sector + hop, NS)

    loads = [pltpu.make_async_copy(src, dst, load.at[i]) for i, (src, dst) in enumerate((
        (t_hbm, t_ref), (e_hbm, e_ref), (v_hbm, v_ref), (c_hbm, c_ref), (p_hbm, p_ref),
        (kept_hbm, kept_ref)))]
    for copy in loads:
        copy.start()

    barrier = pltpu.get_barrier_semaphore()
    greeted = NX - 1 + NS - 1
    for hop in range(1, NX):
        pl.semaphore_signal(barrier, inc=1, device_id=in_row(lax.rem(x + hop, NX)), device_id_type=MESH)
    for hop in range(1, NS):
        pl.semaphore_signal(barrier, inc=1, device_id=(chain, peer(hop)), device_id_type=MESH)
    for hop in (1, 2, 5):
        for other, there in ((zz + hop, zz + hop < NZ), (zz - hop, zz >= hop)):
            @pl.when(there)
            def _():
                pl.semaphore_signal(barrier, inc=1, device_id=in_column(other), device_id_type=MESH)
            greeted = greeted + there.astype(jnp.int32)

    loads[0].wait()
    loads[1].wait()
    for k in range(2):
        transfer = t_ref[k]
        source = 0.5 * (e_ref[k] + e_ref[k].T)
        mine[2 * k, 0] = transfer.T
        mine[2 * k + 1, 0] = transfer
        mine[2 * k, 1] = source
        mine[2 * k + 1, 1] = source
    pl.semaphore_wait(barrier, greeted)

    def spread(at, parts):
        rows = [jnp.sum(part, axis=0, keepdims=True) for part in parts]
        rows += [jnp.zeros((1, BLK), F32)] * (16 - len(rows))
        sums[at, pl.ds(sector, 1)] = jnp.concatenate(rows, axis=0)[None]
        for hop in range(1, NS):
            remote(sums.at[at, sector], sums.at[at, sector], send_p.at[at, hop], recv_p.at[at, sector],
                   (chain, peer(hop))).start()

    def collect(at, count):
        for hop in range(1, NS):
            other = peer(hop)
            remote(sums.at[at, other], sums.at[at, other], send_p.at[at, hop], recv_p.at[at, other],
                   (chain, other)).wait_recv()
        total = sums[at, 0]
        for other in range(1, NS):
            total = total + sums[at, other]
        total = jnp.sum(total, axis=1, keepdims=True)
        return [total[i:i + 1] for i in range(count)]

    def deal(column):
        slot = slot_of(column)
        return remote(mine.at[column], elements.at[slot], send_a.at[column], recv_a.at[slot], in_row(column))

    for hop in (2, 1, 3):
        for column in range(NX):
            @pl.when(column == lax.rem(x + hop, NX))
            def _():
                deal(column).start()
    elements[pl.ds(my_slot, 1)] = mine[pl.ds(x, 1)]

    def ghost_up():
        return remote(v_hbm.at[1], ghost.at[0], send_v.at[0], recv_v.at[0], above)

    def ghost_down():
        return remote(v_hbm.at[0], ghost.at[1], send_v.at[1], recv_v.at[1], below)

    def coupling_up():
        return remote(c_hbm.at[1], ghost_c, send_v.at[2], recv_v.at[2], above)

    @pl.when(has_above)
    def _():
        coupling_up().start()

    def square(i, total):
        part = v_ref[:, pl.ds(pl.multiple_of(i * 256, 256), 256), :]
        return total + fold(part * part)

    loads[2].wait()
    spread(0, [lax.fori_loop(0, 8, square, jnp.zeros((8, BLK), F32))])

    square_zero = jnp.zeros((BLK, BLK), F32)
    for ref, unused in (
            (came.at[0, 0], (zz < 2) | (zz == NZ - 1)), (came.at[0, 1], (zz < 1) | (zz == NZ - 1)),
            (came.at[1, 0], (zz < 4) | (zz == NZ - 1)), (came.at[1, 1], (zz < 2) | (zz == NZ - 1)),
            (came.at[2, 0], zz < 5), (came.at[2, 1], zz < 1), (far, zz < 5)):
        @pl.when(unused)
        def _():
            ref[...] = square_zero

    @pl.when(sector == 0)
    def _():
        ghost[0] = jnp.zeros((ROWS, BLK), F32)
        ghost_c[...] = square_zero
        w_ghost[0] = jnp.zeros((PHYS, BLK, BLK), F32)
        t_ghost[0] = jnp.zeros((PAIRS, BLK, BLK), F32)
        lr_ghost[0] = jnp.zeros((2, BLK, BLK), F32)

    @pl.when(sector == NS - 1)
    def _():
        ghost[1] = jnp.zeros((ROWS, BLK), F32)
        w_ghost[1] = jnp.zeros((PHYS, BLK, BLK), F32)
        t_ghost[1] = jnp.zeros((PAIRS, BLK, BLK), F32)
        lr_ghost[1] = jnp.zeros((2, BLK, BLK), F32)

    for slot in range(NX):
        @pl.when(my_slot != slot)
        def _():
            remote(mine.at[slot], elements.at[slot], send_a.at[slot], recv_a.at[slot],
                   in_row(lax.rem(x + 1, NX))).wait_recv()

    @pl.when(has_above)
    def _():
        ghost_up().start()

    @pl.when(has_below)
    def _():
        ghost_down().start()

    q0, q1, q2, q3 = [elements[s, 0] for s in range(NX)]
    s0, s1, s2, s3 = [elements[s, 1] for s in range(NX)]
    q01 = product(q1, q0)
    y01 = carry_over(q1, s0, s1)
    q23 = product(q3, q2)
    y23 = carry_over(q3, s2, s3)
    qw = product(q23, q01)
    yw = carry_over(q23, y01, y23)

    hops = (1, 2, 1)
    sends = (((zz >= 1) & (zz <= 5), zz <= 5), ((zz >= 2) & (zz <= 4), zz <= 4), ((zz >= 4) & (zz <= 6), zz <= 6))
    takes = (((zz >= 2) & (zz <= 6), (zz >= 1) & (zz <= 6)), ((zz >= 4) & (zz <= 6), (zz >= 2) & (zz <= 6)),
             (zz >= 5, zz >= 1))

    def step(at, part):
        return remote(window.at[at, part], came.at[at, part], send_z.at[at, part], recv_z.at[at, part],
                      in_column(zz + hops[at]))

    def send(at, part, value):
        window[at, part] = value

        @pl.when(sends[at][part])
        def _():
            step(at, part).start()

    def receive(at, part):
        @pl.when(takes[at][part])
        def _():
            remote(window.at[at, part], came.at[at, part], send_z.at[at, part], recv_z.at[at, part],
                   in_column(zz - hops[at])).wait_recv()
        return came[at, part]

    def far_copy(at):
        return remote(window.at[at, 1], far, send_f.at[0], recv_f.at[0], in_column(zz + 5))

    def send_far(at):
        @pl.when(zz == at)
        def _():
            far_copy(at).start()

    def start_wave():
        inverse = 1.0 / jnp.sqrt(collect(0, 1)[0])
        inverses = jnp.broadcast_to(inverse, (BLK, BLK))

        def one(p, carry):
            for k in range(2):
                value = v_ref[k, pl.ds(p, BLK, stride=PHYS), :] * inverses
                vp[k, p] = value
                high, low = halves(value)
                xh[p, BLK * (k + 1):BLK * (k + 2), :] = high
                xl[p, BLK * (k + 1):BLK * (k + 2), :] = low
            return carry

        lax.fori_loop(0, PHYS, one, 0)
        return inverses

    def make_phys():
        loads[4].wait()
        sym = 0.5 * (p_ref[...] + p_ref[...].T)
        lane = lax.broadcasted_iota(jnp.int32, (PHYS, 256), 1)
        row = lax.broadcasted_iota(jnp.int32, (PHYS, 256), 0)
        spread_p = (lax.div(lane, PHYS) == row).astype(BF16)
        same = (lax.rem(lane, PHYS) == row).astype(F32)
        for i, half in enumerate(halves(sym)):
            wide = dot(half, spread_p)
            for p in range(PHYS):
                phys_a[i, PHYS * p:PHYS * (p + 1), :] = (wide[p:p + 1, :] * same).astype(BF16)

    def phys_rows(ref, k, i):
        first = pl.multiple_of(BLK * (k + 1) + 32 * i, 32)
        second = pl.multiple_of(BLK * (k + 1) + 32 * i + 16, 16)
        return jnp.concatenate([
            jnp.concatenate([ref[p, pl.ds(at, 16), :] for p in range(PHYS)], axis=0)
            for at in (first, second)], axis=1)

    def phys_piece(high, low, k, i):
        return split_dot((phys_a[0], phys_a[1]), (phys_rows(high, k, i), phys_rows(low, k, i)))

    def phys_product(high, low, dst):
        def one(i, carry):
            for k in range(2):
                value = phys_piece(high, low, k, i)
                at = pl.multiple_of(32 * i, 32)
                for p in range(PHYS):
                    rows = value[PHYS * p:PHYS * (p + 1)]
                    dst[k, p, pl.ds(at, 32), :] = jnp.concatenate([rows[:, :BLK], rows[:, BLK:]], axis=0)
            return carry

        lax.fori_loop(0, BLK // 32, one, 0)

    def make_ghost_matrices():
        loads[3].wait()
        zero = jnp.zeros((BLK, BLK), BF16)
        own_up = halves(c_ref[0])
        own_down = halves(c_ref[0].T)
        for i in range(2):
            own_a[i] = jnp.concatenate([jnp.concatenate([zero, own_down[i]], axis=1),
                                        jnp.concatenate([own_up[i], zero], axis=1)], axis=0)
        last = c_ref[1] * has_above.astype(F32)
        ghost_a[0] = packed(ghost_c[...])
        ghost_a[1] = packed(last.T)
        cross_a[0] = packed(ghost_c[...].T)
        cross_a[1] = packed(last)

    def pair_of(refs, i, low, high):
        p = 2 * i
        return [jnp.concatenate([
            jnp.concatenate([ref[p + j, BLK * low:BLK * (low + 1), :], ref[p + j, BLK * high:BLK * (high + 1), :]], axis=0)
            for j in range(2)], axis=1) for ref in refs]

    def add_own(i, carry):
        value = split_dot((own_a[0], own_a[1]), pair_of((xh, xl), i, 1, 2))
        for k in range(2):
            for j in range(2):
                p = 2 * i + j
                both = w0[k, p] + value[BLK * k:BLK * (k + 1), BLK * j:BLK * (j + 1)]
                w0[k, p] = both
                partial[k, p] = both
        return carry

    def add_to_ghosts(i, carry):
        for side in range(2):
            blocks = packed_dot(cross_a[side], (xh, xl), 2 * i, side + 1)
            for j in range(2):
                outward[side, 2 * i + j] = blocks[j]
        return carry

    def add_ghosts(i, inverses):
        for side, row in ((0, 0), (1, 3)):
            for j in range(2):
                p = 2 * i + j
                high, low = halves(ghost[side, pl.ds(p, BLK, stride=PHYS), :] * inverses)
                xh[p, BLK * row:BLK * (row + 1), :] = high
                xl[p, BLK * row:BLK * (row + 1), :] = low
            blocks = packed_dot(ghost_a[side], (xh, xl), 2 * i, row)
            for j in range(2):
                w0[side, 2 * i + j] = w0[side, 2 * i + j] + blocks[j]
        return inverses

    def base_down():
        return remote(partial.at[0], w_ghost.at[1], send_w.at[0], recv_w.at[0], below)

    def base_up():
        return remote(partial.at[1], w_ghost.at[0], send_w.at[1], recv_w.at[1], above)

    send(0, 1, yw)
    send(0, 0, qw)
    send_far(0)
    q012 = product(q2, q01)
    y012 = carry_over(q2, y01, s2)
    inverses = start_wave()
    make_phys()

    @pl.when(has_below)
    def _():
        coupling_up().wait_recv()

    make_ghost_matrices()
    yw = carry_over(qw, receive(0, 1), yw)
    send(1, 1, yw)
    send_far(1)
    qw = product(qw, receive(0, 0))
    send(1, 0, qw)
    phys_product(xh, xl, w0)
    lax.fori_loop(0, PAIRS, add_own, 0)

    @pl.when(has_below)
    def _():
        base_down().start()

    @pl.when(has_above)
    def _():
        base_up().start()

    yw = carry_over(qw, receive(1, 1), yw)
    send(2, 1, yw)
    send_far(2)
    send(2, 0, product(qw, receive(1, 0)))

    @pl.when(zz >= 5)
    def _():
        remote(window.at[2, 1], far, send_f.at[0], recv_f.at[0], in_column(zz - 5)).wait_recv()
    y_near = receive(2, 1)
    start = carry_over(receive(2, 0), far[...], y_near)

    def owner(slot):
        return slot + odd * (NX - 1 - 2 * slot)

    def give(slot):
        return remote(ends.at[slot], envs.at[x], send_e.at[slot], recv_e.at[x], in_row(owner(slot)))

    ends[0] = start
    for slot, (q, y) in enumerate(((q0, s0), (q01, y01), (q012, y012))):
        ends[slot + 1] = carry_over(q, start, y)
    for hop in (2, 1, 3):
        for slot in range(NX):
            @pl.when(slot == lax.rem(my_slot + hop, NX))
            def _():
                give(slot).start()
    envs[pl.ds(x, 1)] = ends[pl.ds(my_slot, 1)]
    @pl.when(has_below)
    def _():
        ghost_up().wait_recv()

    @pl.when(has_above)
    def _():
        ghost_down().wait_recv()

    lax.fori_loop(0, PAIRS, add_ghosts, inverses)
    lax.fori_loop(0, PAIRS, add_to_ghosts, 0)
    for column in range(NX):
        @pl.when(x != column)
        def _():
            remote(ends.at[column], envs.at[column], send_e.at[column], recv_e.at[column], in_row(column)).wait_recv()

    def envs_down():
        return remote(envs.at[pl.ds(0, 2)], lr_ghost.at[1], send_v.at[3], recv_v.at[3], below)

    def envs_up():
        return remote(envs.at[pl.ds(2, 2)], lr_ghost.at[0], send_v.at[4], recv_v.at[4], above)

    @pl.when(has_below)
    def _():
        envs_down().start()

    @pl.when(has_above)
    def _():
        envs_up().start()

    def right_of(env):
        high, low = halves(env)
        return jnp.concatenate([jnp.concatenate([high, low], axis=1),
                                jnp.concatenate([high, jnp.zeros_like(low)], axis=1)], axis=0)

    for k in range(2):
        left_ref[k] = envs[2 * k]
        right_w[k] = right_of(envs[2 * k + 1])
    none = jnp.zeros((BLK, BLK), BF16)

    lefts = [halves(envs[2 * k]) for k in range(2)]
    for h in range(2):
        own_a[h] = own_a[h] + jnp.concatenate([jnp.concatenate([lefts[0][h], none], axis=1),
                                               jnp.concatenate([none, lefts[1][h]], axis=1)], axis=0)
        left_w[h] = packed(envs[2 * h])

    def right_products(refs, p, row, matrix):
        rows = slice(BLK * row, BLK * (row + 1))
        lhs = jnp.concatenate([jnp.concatenate([ref[p + j, rows, :] for ref in refs], axis=1)
                               for j in range(2)], axis=0)
        value = dot(lhs, matrix)
        value = value[:, :BLK] + value[:, BLK:]
        return value[:BLK], value[BLK:]

    def environment_products(refs, i, row, at):
        lefts = packed_dot(left_w[at], refs, 2 * i, row)
        rights = right_products(refs, 2 * i, row, right_w[at])
        return [left + right for left, right in zip(lefts, rights)]

    def first_apply(i, total):
        for k in range(2):
            blocks = environment_products((xh, xl), i, k + 1, k)
            for j in range(2):
                p = 2 * i + j
                value = w0[k, p] + blocks[j]
                w0[k, p] = value
                high, low = halves(value)
                yh[p, BLK * (k + 1):BLK * (k + 2), :] = high
                yl[p, BLK * (k + 1):BLK * (k + 2), :] = low
                total = total + fold(value * vp[k, p])
        return total

    def ghost_apply(i, carry):
        for side, row in ((0, 0), (1, 3)):
            blocks = environment_products((xh, xl), i, row, 2 + side)
            for j in range(2):
                p = 2 * i + j
                high, low = halves(w_ghost[side, p] + outward[side, p] + blocks[j])
                yh[p, BLK * row:BLK * (row + 1), :] = high
                yl[p, BLK * row:BLK * (row + 1), :] = low
        return carry

    zeros = jnp.zeros((8, BLK), F32)
    spread(1, [lax.fori_loop(0, PAIRS, first_apply, zeros)])
    phys_product(yh, yl, w1)

    @pl.when(has_below)
    def _():
        envs_up().wait_recv()

    @pl.when(has_above)
    def _():
        envs_down().wait_recv()

    for side in range(2):
        left_w[2 + side] = packed(lr_ghost[side, 0])
        right_w[2 + side] = right_of(lr_ghost[side, 1])

    @pl.when(has_below)
    def _():
        base_up().wait_recv()

    @pl.when(has_above)
    def _():
        base_down().wait_recv()

    lax.fori_loop(0, PAIRS, ghost_apply, 0)
    corr = collect(1, 1)[0]
    corrs = jnp.broadcast_to(corr, (BLK, BLK))

    def finish(i, totals):
        rr, rt, vt, tt = totals
        value = split_dot((own_a[0], own_a[1]), pair_of((yh, yl), i, 1, 2))
        for k in range(2):
            ghosts = packed_dot(ghost_a[k], (yh, yl), 2 * i, 3 * k)
            rights = right_products((yh, yl), 2 * i, k + 1, right_w[k])
            for j in range(2):
                p = 2 * i + j
                applied = w0[k, p]
                wave = vp[k, p]
                residual = applied - corrs * wave
                turned = (w1[k, p] + rights[j] + ghosts[j] + value[BLK * k:BLK * (k + 1), BLK * j:BLK * (j + 1)]
                          - corrs * applied)
                r0[k, p] = residual
                w1[k, p] = turned
                high, low = halves(turned)
                xh[p, BLK * (k + 1):BLK * (k + 2), :] = high
                xl[p, BLK * (k + 1):BLK * (k + 2), :] = low
                rr = rr + fold(residual * residual)
                rt = rt + fold(residual * turned)
                vt = vt + fold(wave * turned)
                tt = tt + fold(turned * turned)
        return rr, rt, vt, tt

    def turned_down(part):
        at = pl.ds(2 * part, 2)
        return remote(w1.at[0, at], t_ghost.at[1, at], send_t.at[0, part], recv_t.at[0, part], below)

    def turned_up(part):
        return remote(w1.at[1, pl.ds(PAIRS + 2 * part, 2)], t_ghost.at[0, pl.ds(2 * part, 2)],
                      send_t.at[1, part], recv_t.at[1, part], above)

    totals = (zeros,) * 4
    for part in range(CHUNKS):
        totals = lax.fori_loop(0, 2, lambda n, c: finish(part + CHUNKS * n, c), totals)

        @pl.when(has_below)
        def _():
            turned_down(part).start()

        @pl.when(has_above)
        def _():
            turned_up(part).start()

    def third_apply(i, total):
        rhs = pair_of((xh,), i, 1, 2)[0]
        value = dot(own_a[0], rhs) + dot(own_a[1], rhs)
        for k in range(2):
            rights = right_products((xh,), 2 * i, k + 1, right_w[k, :BLK])
            for j in range(2):
                p = 2 * i + j
                both = 2.0 * w1[k, p] - xh[p, BLK * (k + 1):BLK * (k + 2), :].astype(F32)
                image = value[BLK * k:BLK * (k + 1), BLK * j:BLK * (j + 1)] + rights[j]
                total = total + fold(image * both)
        return total

    def third_phys(i, total):
        at = pl.multiple_of(32 * i, 32)
        for k in range(2):
            rhs = phys_rows(xh, k, i)
            value = dot(phys_a[0], rhs) + dot(phys_a[1], rhs)
            for p in range(PHYS):
                rows = value[PHYS * p:PHYS * (p + 1)]
                image = jnp.concatenate([rows[:, :BLK], rows[:, BLK:]], axis=0)
                high = xh[p, pl.ds(pl.multiple_of(BLK * (k + 1) + 32 * i, 32), 32), :].astype(F32)
                total = total + fold(image * (2.0 * w1[k, p, pl.ds(at, 32), :] - high))
        return total

    def cross(i, carry):
        for side in range(2):
            blocks = packed_dot(cross_a[side], (xh, xl), 2 * i + PAIRS * (1 - side), side + 1)
            for j in range(2):
                crossed[side, 2 * i + j] = blocks[j]
        return carry

    def cross_and_phys(i, total):
        cross(i, 0)
        return third_phys(i, total)

    tht = lax.fori_loop(0, PAIRS // 2, cross_and_phys, zeros)

    loads[5].wait()
    masks = [(lax.broadcasted_iota(jnp.int32, (1, BLK), 1) < kept_ref[0, k]).astype(F32) for k in range(2)]

    def masked(p, grams):
        for k in range(2):
            vectors = (vp[k, p], r0[k, p], w1[k, p])
            pairs = [vectors[i] * vectors[j] for i in range(3) for j in range(i, 3)]
            grams = tuple(gram + masks[k] * fold(pair) for gram, pair in zip(grams, pairs))
        return grams

    def apply_and_masked(i, carry):
        total, grams = carry
        return third_apply(i, total), masked(2 * i + 1, masked(2 * i, grams))

    tht, grams = lax.fori_loop(0, PAIRS, apply_and_masked, (tht, (zeros,) * 6))

    for part in range(CHUNKS):
        @pl.when(has_above)
        def _():
            turned_down(part).wait_recv()

        @pl.when(has_below)
        def _():
            turned_up(part).wait_recv()

    def meet(i, total):
        return total + fold(crossed[0, i] * t_ghost[0, i]) + fold(crossed[1, i] * t_ghost[1, i])

    tht = tht + 2.0 * lax.fori_loop(0, PAIRS, meet, zeros)
    spread(2, list(totals) + [tht] + list(grams))
    rr, rt, vt, tt, tht, mvv, mvr, mvt, mrr, mrt, mtt = collect(2, 11)
    w0t = rt + corr * vt
    norm = jnp.sqrt(rr + EPS)
    curvature = rt / (rr + EPS)
    coupled = rr / norm
    ritz = 0.5 * (corr + curvature) - jnp.sqrt(0.25 * (corr - curvature) ** 2 + coupled * coupled)
    coef = ritz - corr
    magnitude = jnp.sqrt(coupled * coupled + coef * coef)
    wave_v = coupled / magnitude
    wave_r = coef / (magnitude * norm)
    corr2 = wave_v * wave_v * corr + wave_v * wave_r * (vt + rr) + wave_r * wave_r * rt
    res_v = wave_v * (corr - corr2)
    res_r = wave_v - corr2 * wave_r
    res_t = wave_r

    rr2 = res_v * res_v + res_r * res_r * rr + res_t * res_t * tt + 2.0 * res_t * (res_v * vt + res_r * rt)
    rr2 = jnp.maximum(rr2, 0.0)
    wr2 = wave_v * res_v + wave_r * res_r * rr + res_t * (wave_v * vt + wave_r * rt)
    ar2 = rr2 + corr2 * wr2
    norm2 = jnp.sqrt(rr2 + EPS)
    turned2 = (res_v * res_v * corr + res_r * res_r * rt + res_t * res_t * tht
               + 2.0 * (res_v * res_r * vt + res_v * res_t * w0t + res_r * res_t * tt))
    curvature = turned2 / (rr2 + EPS)
    coupled = ar2 / norm2
    ritz = 0.5 * (corr2 + curvature) - jnp.sqrt(0.25 * (corr2 - curvature) ** 2 + coupled * coupled)
    coef = ritz - corr2
    magnitude = jnp.sqrt(coupled * coupled + coef * coef)
    of_wave = coupled / magnitude
    of_res = coef / (magnitude * norm2)
    of_v = of_wave * wave_v + of_res * res_v
    of_r = of_wave * wave_r + of_res * res_r
    of_t = of_res * res_t
    kept = (of_v * of_v * mvv + of_r * of_r * mrr + of_t * of_t * mtt
            + 2.0 * (of_v * of_r * mvr + of_v * of_t * mvt + of_r * of_t * mrt))
    scale = 1.0 / jnp.sqrt(jnp.maximum(kept, 0.0) + EPS)
    last = [scale * value for value in (of_v, of_r, of_t)]
    last_ref[...] = jnp.concatenate(
        [jnp.broadcast_to(value, (1, BLK)) for value in last + [ritz]] + masks + [jnp.zeros((2, BLK), F32)], axis=0)

    for column in range(NX):
        @pl.when(x != column)
        def _():
            deal(column).wait_send()
    for at in range(3):
        for part in range(2):
            @pl.when(sends[at][part])
            def _():
                step(at, part).wait_send()

    @pl.when(zz < 3)
    def _():
        far_copy(0).wait_send()
    for slot in range(NX):
        @pl.when(my_slot != slot)
        def _():
            give(slot).wait_send()
    for at in range(3):
        for hop in range(1, NS):
            remote(sums.at[at, sector], sums.at[at, sector], send_p.at[at, hop], recv_p.at[at, sector],
                   (chain, peer(hop))).wait_send()

    @pl.when(has_above)
    def _():
        coupling_up().wait_send()
        ghost_up().wait_send()
        envs_up().wait_send()
        base_up().wait_send()
        for part in range(CHUNKS):
            turned_up(part).wait_send()

    @pl.when(has_below)
    def _():
        ghost_down().wait_send()
        envs_down().wait_send()
        base_down().wait_send()
        for part in range(CHUNKS):
            turned_down(part).wait_send()


def write_kernel(wave_ref, res_ref, turned_ref, last_ref, left_in, out_ref, energy_ref, left_ref, rows, sem):
    left_copy = pltpu.make_async_copy(left_in, left_ref, sem.at[8])
    left_copy.start()
    energy_ref[0] = jnp.sum(last_ref[3:4, 0:1])
    size = ROWS // CHUNKS
    count = size // PHYS
    copies = []
    for k in range(2):
        mask = last_ref[4 + k:5 + k, :]
        coefs = [jnp.broadcast_to(last_ref[i:i + 1, :] * mask, (count, BLK)) for i in range(3)]
        for part in range(CHUNKS):
            at = pl.ds(count * part, count)
            for p in range(PHYS):
                rows[k, pl.ds(size * part + p, count, stride=PHYS), :] = (
                    coefs[0] * wave_ref[k, p, at, :] + coefs[1] * res_ref[k, p, at, :] + coefs[2] * turned_ref[k, p, at, :])
            to = pl.ds(size * part, size)
            copies.append(pltpu.make_async_copy(rows.at[k, to], out_ref.at[k, to], sem.at[CHUNKS * k + part]))
            copies[-1].start()
    for copy in copies:
        copy.wait()
    left_copy.wait()


def per_device(wave_start, transfer, energy_terms, coupling, physical, kept_ranks):
    hbm = pl.BlockSpec(memory_space=pltpu.HBM)
    vmem = pl.BlockSpec(memory_space=pltpu.VMEM)
    smem = pl.BlockSpec(memory_space=pltpu.SMEM)
    dma = pltpu.SemaphoreType.DMA

    def square(*lead):
        return pltpu.VMEM((*lead, BLK, BLK), F32)

    def wide(*lead):
        return pltpu.VMEM((*lead, 2 * BLK, 2 * BLK), BF16)

    split_waves = pltpu.VMEM((PHYS, 4 * BLK, BLK), BF16)
    waves = jax.ShapeDtypeStruct((2, PHYS, BLK, BLK), F32)
    parts = pl.pallas_call(
        update_kernel,
        out_shape=(
            waves, waves, waves,
            jax.ShapeDtypeStruct((8, BLK), F32),
            jax.ShapeDtypeStruct((2, BLK, BLK), F32),
        ),
        in_specs=[hbm] * 6,
        out_specs=(vmem,) * 5,
        scratch_shapes=[
            pltpu.VMEM((2, ROWS, BLK), F32), square(2), square(2), square(2), pltpu.VMEM((PHYS, PHYS), F32),
            pltpu.SMEM((1, 2), jnp.int32),
            square(NX, 2), square(NX, 2), square(3, 2), square(3, 2), square(), square(2, PHYS), square(2, PHYS), square(NX), square(NX),
            pltpu.VMEM((2, ROWS, BLK), F32), square(), square(2, PHYS), square(2, PHYS),
            square(2, PAIRS), square(2, 2), square(2, PAIRS),
            split_waves, split_waves, split_waves, split_waves,
            wide(4), wide(2), wide(2), wide(2), wide(4), wide(2),
            pltpu.VMEM((3, NS, 16, BLK), F32),
            dma((6,)), dma((NX,)), dma((NX,)), dma((3, 2)), dma((3, 2)), dma((1,)), dma((1,)), dma((NX,)), dma((NX,)),
            dma((5,)), dma((5,)), dma((2,)), dma((2,)), dma((2, CHUNKS)), dma((2, CHUNKS)),
            dma((3, NS)), dma((3, NS)),
        ],
        compiler_params=pltpu.CompilerParams(
            collective_id=0, has_side_effects=True, vmem_limit_bytes=36 << 20),
    )(*[pltpu.with_memory_space_constraint(value, pltpu.HBM) for value in (
        wave_start.reshape(2, ROWS, BLK), transfer[0], energy_terms[0], coupling[0], physical[0], kept_ranks)])
    out, energy, left = pl.pallas_call(
        write_kernel,
        out_shape=(
            jax.ShapeDtypeStruct((2, ROWS, BLK), F32),
            jax.ShapeDtypeStruct((1,), F32),
            jax.ShapeDtypeStruct((2, BLK, BLK), F32),
        ),
        in_specs=[vmem] * 5,
        out_specs=(hbm, smem, hbm),
        scratch_shapes=[pltpu.VMEM((2, ROWS, BLK), F32), dma((9,))],
        compiler_params=pltpu.CompilerParams(vmem_limit_bytes=16 << 20),
    )(*[pltpu.with_memory_space_constraint(value, pltpu.VMEM) for value in parts])
    return (out.reshape(wave_start.shape), energy, left[None])


def solution(mesh):
    placed = (
        P("chain", "sector", None, None, None),
        P("chain", "sector", None, None),
        P("chain", "sector", None, None),
        P("chain", "sector", None, None),
        P("chain", None, None),
        P("chain", "sector"),
    )
    return jax.shard_map(
        per_device,
        mesh=mesh,
        in_specs=placed,
        out_specs=(
            P("chain", "sector", None, None, None),
            P("chain"),
            P("chain", "sector", None, None),
        ),
        check_vma=False,
    )
```

```python
import functools

import jax
import jax.numpy as jnp
from jax import lax
from jax.experimental import pallas as pl
from jax.experimental.pallas import tpu as pltpu
from jax.sharding import PartitionSpec as P

BLK = 128
PHYS = 16
NX = 4
NZ = 8
NS = 8
ROWS = BLK * PHYS
CHUNKS = 4
CHUNK = PHYS // CHUNKS
PAIRS = PHYS // 2

EPS = 1e-06
MESH = pl.DeviceIdType.MESH
F32 = jnp.float32
BF16 = jnp.bfloat16
NN = (((1,), (0,)), ((), ()))
NT = (((1,), (1,)), ((), ()))


def halves(value):
    high = value.astype(BF16)
    return high, (value - high.astype(F32)).astype(BF16)


def dot(lhs, rhs, dims=NN):
    return lax.dot_general(lhs, rhs, dims, preferred_element_type=F32)


def product(lhs, rhs, dims=NN):
    lhs_high, lhs_low = halves(lhs)
    rhs_high, rhs_low = halves(rhs)
    both = jnp.concatenate([lhs_high, lhs_low], axis=1)
    twice = jnp.concatenate([rhs_high, rhs_high], axis=1 if dims is NT else 0)
    return dot(both, twice, dims) + dot(lhs_high, rhs_low, dims)


def split_dot(lhs, rhs):
    return dot(lhs[0], rhs[0]) + (dot(lhs[0], rhs[1]) + dot(lhs[1], rhs[0]))


def packed(matrix):
    high, low = halves(matrix)
    return jnp.concatenate([jnp.concatenate([high, high], axis=1),
                            jnp.concatenate([low, jnp.zeros_like(low)], axis=1)], axis=0)


def packed_dot(matrix, refs, p, row):
    rows = slice(BLK * row, BLK * (row + 1))
    rhs = jnp.concatenate([jnp.concatenate([ref[p + j, rows, :] for ref in refs], axis=0) for j in range(2)], axis=1)
    value = dot(matrix, rhs)
    value = value[:BLK] + value[BLK:]
    return value[:, :BLK], value[:, BLK:]


def carry_over(matrix, env, source):
    return product(product(matrix, env), matrix, NT) + source


def fold(value):
    return jnp.sum(value.reshape(-1, 8, BLK), axis=0)


def remote(src, dst, send_sem, recv_sem, device):
    return pltpu.make_async_remote_copy(src, dst, send_sem, recv_sem, device_id=device, device_id_type=MESH)


def update_kernel(v_hbm, t_hbm, e_hbm, c_hbm, p_hbm, kept_hbm, vp, r0, w1, last_ref, left_ref,
                  v_ref, t_ref, e_ref, c_ref, p_ref, kept_ref,
                  mine, elements, window, came, far, partial, outward, ends, envs,
                  ghost, ghost_c, w0, w_ghost, t_ghost, lr_ghost, crossed,
                  xh, xl, yh, yl, left_w, own_a, ghost_a, cross_a, right_w, phys_a, sums,
                  load, send_a, recv_a, send_z, recv_z, send_f, recv_f, send_e, recv_e,
                  send_v, recv_v, send_w, recv_w, send_t, recv_t, send_p, recv_p):
    chain = lax.axis_index("chain")
    sector = lax.axis_index("sector")
    x = lax.rem(chain, NX)
    z = lax.div(chain, NX)
    odd = lax.rem(x, 2)
    zz = z + odd * (NZ - 1 - 2 * z)
    my_slot = x + odd * (NX - 1 - 2 * x)
    has_below = sector > 0
    has_above = sector < NS - 1
    below = (chain, sector - 1)
    above = (chain, sector + 1)

    def in_row(other):
        return (z * NX + other, sector)

    def in_column(other):
        return ((other + odd * (NZ - 1 - 2 * other)) * NX + x, sector)

    def slot_of(column):
        return x if column % 2 == 0 else NX - 1 - x

    def peer(hop):
        return lax.rem(sector + hop, NS)

    loads = [pltpu.make_async_copy(src, dst, load.at[i]) for i, (src, dst) in enumerate((
        (t_hbm, t_ref), (e_hbm, e_ref), (v_hbm, v_ref), (c_hbm, c_ref), (p_hbm, p_ref),
        (kept_hbm, kept_ref)))]
    for copy in loads:
        copy.start()

    barrier = pltpu.get_barrier_semaphore()
    greeted = NX - 1 + NS - 1
    for hop in range(1, NX):
        pl.semaphore_signal(barrier, inc=1, device_id=in_row(lax.rem(x + hop, NX)), device_id_type=MESH)
    for hop in range(1, NS):
        pl.semaphore_signal(barrier, inc=1, device_id=(chain, peer(hop)), device_id_type=MESH)
    for hop in (1, 2, 5):
        for other, there in ((zz + hop, zz + hop < NZ), (zz - hop, zz >= hop)):
            @pl.when(there)
            def _():
                pl.semaphore_signal(barrier, inc=1, device_id=in_column(other), device_id_type=MESH)
            greeted = greeted + there.astype(jnp.int32)

    loads[0].wait()
    loads[1].wait()
    for k in range(2):
        transfer = t_ref[k]
        source = 0.5 * (e_ref[k] + e_ref[k].T)
        mine[2 * k, 0] = transfer.T
        mine[2 * k + 1, 0] = transfer
        mine[2 * k, 1] = source
        mine[2 * k + 1, 1] = source
    pl.semaphore_wait(barrier, greeted)

    def spread(at, parts):
        rows = [jnp.sum(part, axis=0, keepdims=True) for part in parts]
        rows += [jnp.zeros((1, BLK), F32)] * (16 - len(rows))
        sums[at, pl.ds(sector, 1)] = jnp.concatenate(rows, axis=0)[None]
        for hop in range(1, NS):
            remote(sums.at[at, sector], sums.at[at, sector], send_p.at[at, hop], recv_p.at[at, sector],
                   (chain, peer(hop))).start()

    def collect(at, count):
        for hop in range(1, NS):
            other = peer(hop)
            remote(sums.at[at, other], sums.at[at, other], send_p.at[at, hop], recv_p.at[at, other],
                   (chain, other)).wait_recv()
        total = sums[at, 0]
        for other in range(1, NS):
            total = total + sums[at, other]
        total = jnp.sum(total, axis=1, keepdims=True)
        return [total[i:i + 1] for i in range(count)]

    def deal(column):
        slot = slot_of(column)
        return remote(mine.at[column], elements.at[slot], send_a.at[column], recv_a.at[slot], in_row(column))

    for hop in (2, 1, 3):
        for column in range(NX):
            @pl.when(column == lax.rem(x + hop, NX))
            def _():
                deal(column).start()
    elements[pl.ds(my_slot, 1)] = mine[pl.ds(x, 1)]

    def ghost_up():
        return remote(v_hbm.at[1], ghost.at[0], send_v.at[0], recv_v.at[0], above)

    def ghost_down():
        return remote(v_hbm.at[0], ghost.at[1], send_v.at[1], recv_v.at[1], below)

    def coupling_up():
        return remote(c_hbm.at[1], ghost_c, send_v.at[2], recv_v.at[2], above)

    @pl.when(has_above)
    def _():
        coupling_up().start()

    def square(i, total):
        part = v_ref[:, pl.ds(pl.multiple_of(i * 256, 256), 256), :]
        return total + fold(part * part)

    loads[2].wait()
    spread(0, [lax.fori_loop(0, 8, square, jnp.zeros((8, BLK), F32))])

    square_zero = jnp.zeros((BLK, BLK), F32)
    for ref, unused in (
            (came.at[0, 0], (zz < 2) | (zz == NZ - 1)), (came.at[0, 1], (zz < 1) | (zz == NZ - 1)),
            (came.at[1, 0], (zz < 4) | (zz == NZ - 1)), (came.at[1, 1], (zz < 2) | (zz == NZ - 1)),
            (came.at[2, 0], zz < 5), (came.at[2, 1], zz < 1), (far, zz < 5)):
        @pl.when(unused)
        def _():
            ref[...] = square_zero

    @pl.when(sector == 0)
    def _():
        ghost[0] = jnp.zeros((ROWS, BLK), F32)
        ghost_c[...] = square_zero
        w_ghost[0] = jnp.zeros((PHYS, BLK, BLK), F32)
        t_ghost[0] = jnp.zeros((PAIRS, BLK, BLK), F32)
        lr_ghost[0] = jnp.zeros((2, BLK, BLK), F32)

    @pl.when(sector == NS - 1)
    def _():
        ghost[1] = jnp.zeros((ROWS, BLK), F32)
        w_ghost[1] = jnp.zeros((PHYS, BLK, BLK), F32)
        t_ghost[1] = jnp.zeros((PAIRS, BLK, BLK), F32)
        lr_ghost[1] = jnp.zeros((2, BLK, BLK), F32)

    for column in range(NX):
        @pl.when(x != column)
        def _():
            deal(column).wait_send()

    @pl.when(has_above)
    def _():
        ghost_up().start()

    @pl.when(has_below)
    def _():
        ghost_down().start()

    for slot in range(NX):
        @pl.when(my_slot != slot)
        def _():
            remote(mine.at[slot], elements.at[slot], send_a.at[slot], recv_a.at[slot],
                   in_row(lax.rem(x + 1, NX))).wait_recv()

    q0, q1, q2, q3 = [elements[s, 0] for s in range(NX)]
    s0, s1, s2, s3 = [elements[s, 1] for s in range(NX)]
    q01 = product(q1, q0)
    y01 = carry_over(q1, s0, s1)
    q23 = product(q3, q2)
    y23 = carry_over(q3, s2, s3)
    qw = product(q23, q01)
    yw = carry_over(q23, y01, y23)

    hops = (1, 2, 1)
    sends = (((zz >= 1) & (zz <= 5), zz <= 5), ((zz >= 2) & (zz <= 4), zz <= 4), ((zz >= 4) & (zz <= 6), zz <= 6))
    takes = (((zz >= 2) & (zz <= 6), (zz >= 1) & (zz <= 6)), ((zz >= 4) & (zz <= 6), (zz >= 2) & (zz <= 6)),
             (zz >= 5, zz >= 1))

    def step(at, part):
        return remote(window.at[at, part], came.at[at, part], send_z.at[at, part], recv_z.at[at, part],
                      in_column(zz + hops[at]))

    def send(at, part, value):
        window[at, part] = value

        @pl.when(sends[at][part])
        def _():
            step(at, part).start()

    def receive(at, part):
        @pl.when(takes[at][part])
        def _():
            remote(window.at[at, part], came.at[at, part], send_z.at[at, part], recv_z.at[at, part],
                   in_column(zz - hops[at])).wait_recv()
        return came[at, part]

    def far_copy(at):
        return remote(window.at[at, 1], far, send_f.at[0], recv_f.at[0], in_column(zz + 5))

    def send_far(at):
        @pl.when(zz == at)
        def _():
            far_copy(at).start()

    def start_wave():
        inverse = 1.0 / jnp.sqrt(collect(0, 1)[0])
        inverses = jnp.broadcast_to(inverse, (BLK, BLK))

        def one(p, carry):
            for k in range(2):
                value = v_ref[k, pl.ds(p, BLK, stride=PHYS), :] * inverses
                vp[k, p] = value
                high, low = halves(value)
                xh[p, BLK * (k + 1):BLK * (k + 2), :] = high
                xl[p, BLK * (k + 1):BLK * (k + 2), :] = low
            return carry

        lax.fori_loop(0, PHYS, one, 0)
        return inverses

    def make_phys():
        loads[4].wait()
        sym = 0.5 * (p_ref[...] + p_ref[...].T)
        lane = lax.broadcasted_iota(jnp.int32, (PHYS, 256), 1)
        row = lax.broadcasted_iota(jnp.int32, (PHYS, 256), 0)
        spread_p = (lax.div(lane, PHYS) == row).astype(BF16)
        same = (lax.rem(lane, PHYS) == row).astype(F32)
        for i, half in enumerate(halves(sym)):
            wide = dot(half, spread_p)
            for p in range(PHYS):
                phys_a[i, PHYS * p:PHYS * (p + 1), :] = (wide[p:p + 1, :] * same).astype(BF16)

    def phys_rows(ref, k, i):
        first = pl.multiple_of(BLK * (k + 1) + 32 * i, 32)
        second = pl.multiple_of(BLK * (k + 1) + 32 * i + 16, 16)
        return jnp.concatenate([
            jnp.concatenate([ref[p, pl.ds(at, 16), :] for p in range(PHYS)], axis=0)
            for at in (first, second)], axis=1)

    def phys_piece(high, low, k, i):
        return split_dot((phys_a[0], phys_a[1]), (phys_rows(high, k, i), phys_rows(low, k, i)))

    def phys_product(high, low, dst):
        def one(i, carry):
            for k in range(2):
                value = phys_piece(high, low, k, i)
                at = pl.multiple_of(32 * i, 32)
                for p in range(PHYS):
                    rows = value[PHYS * p:PHYS * (p + 1)]
                    dst[k, p, pl.ds(at, 32), :] = jnp.concatenate([rows[:, :BLK], rows[:, BLK:]], axis=0)
            return carry

        lax.fori_loop(0, BLK // 32, one, 0)

    def make_ghost_matrices():
        loads[3].wait()
        zero = jnp.zeros((BLK, BLK), BF16)
        own_up = halves(c_ref[0])
        own_down = halves(c_ref[0].T)
        for i in range(2):
            own_a[i] = jnp.concatenate([jnp.concatenate([zero, own_down[i]], axis=1),
                                        jnp.concatenate([own_up[i], zero], axis=1)], axis=0)
        last = c_ref[1] * has_above.astype(F32)
        ghost_a[0] = packed(ghost_c[...])
        ghost_a[1] = packed(last.T)
        cross_a[0] = packed(ghost_c[...].T)
        cross_a[1] = packed(last)

    def pair_of(refs, i, low, high):
        p = 2 * i
        return [jnp.concatenate([
            jnp.concatenate([ref[p + j, BLK * low:BLK * (low + 1), :], ref[p + j, BLK * high:BLK * (high + 1), :]], axis=0)
            for j in range(2)], axis=1) for ref in refs]

    def add_own(i, carry):
        value = split_dot((own_a[0], own_a[1]), pair_of((xh, xl), i, 1, 2))
        for k in range(2):
            for j in range(2):
                p = 2 * i + j
                both = w0[k, p] + value[BLK * k:BLK * (k + 1), BLK * j:BLK * (j + 1)]
                w0[k, p] = both
                partial[k, p] = both
        return carry

    def add_to_ghosts(i, carry):
        for side in range(2):
            blocks = packed_dot(cross_a[side], (xh, xl), 2 * i, side + 1)
            for j in range(2):
                outward[side, 2 * i + j] = blocks[j]
        return carry

    def add_ghosts(i, inverses):
        for side, row in ((0, 0), (1, 3)):
            for j in range(2):
                p = 2 * i + j
                high, low = halves(ghost[side, pl.ds(p, BLK, stride=PHYS), :] * inverses)
                xh[p, BLK * row:BLK * (row + 1), :] = high
                xl[p, BLK * row:BLK * (row + 1), :] = low
            blocks = packed_dot(ghost_a[side], (xh, xl), 2 * i, row)
            for j in range(2):
                w0[side, 2 * i + j] = w0[side, 2 * i + j] + blocks[j]
        return inverses

    def base_down():
        return remote(partial.at[0], w_ghost.at[1], send_w.at[0], recv_w.at[0], below)

    def base_up():
        return remote(partial.at[1], w_ghost.at[0], send_w.at[1], recv_w.at[1], above)

    send(0, 1, yw)
    send(0, 0, qw)
    send_far(0)
    q012 = product(q2, q01)
    y012 = carry_over(q2, y01, s2)
    inverses = start_wave()
    make_phys()

    @pl.when(has_below)
    def _():
        coupling_up().wait_recv()

    make_ghost_matrices()
    yw = carry_over(qw, receive(0, 1), yw)
    send(1, 1, yw)
    send_far(1)
    qw = product(qw, receive(0, 0))
    send(1, 0, qw)
    phys_product(xh, xl, w0)
    lax.fori_loop(0, PAIRS, add_own, 0)

    @pl.when(has_below)
    def _():
        base_down().start()

    @pl.when(has_above)
    def _():
        base_up().start()

    yw = carry_over(qw, receive(1, 1), yw)
    send(2, 1, yw)
    send_far(2)
    send(2, 0, product(qw, receive(1, 0)))

    @pl.when(zz >= 5)
    def _():
        remote(window.at[2, 1], far, send_f.at[0], recv_f.at[0], in_column(zz - 5)).wait_recv()
    y_near = receive(2, 1)
    start = carry_over(receive(2, 0), far[...], y_near)

    def owner(slot):
        return slot + odd * (NX - 1 - 2 * slot)

    def give(slot):
        return remote(ends.at[slot], envs.at[x], send_e.at[slot], recv_e.at[x], in_row(owner(slot)))

    ends[0] = start
    for slot, (q, y) in enumerate(((q0, s0), (q01, y01), (q012, y012))):
        ends[slot + 1] = carry_over(q, start, y)
    for hop in (2, 1, 3):
        for slot in range(NX):
            @pl.when(slot == lax.rem(my_slot + hop, NX))
            def _():
                give(slot).start()
    envs[pl.ds(x, 1)] = ends[pl.ds(my_slot, 1)]
    @pl.when(has_below)
    def _():
        ghost_up().wait_recv()

    @pl.when(has_above)
    def _():
        ghost_down().wait_recv()

    lax.fori_loop(0, PAIRS, add_ghosts, inverses)
    lax.fori_loop(0, PAIRS, add_to_ghosts, 0)
    for column in range(NX):
        @pl.when(x != column)
        def _():
            remote(ends.at[column], envs.at[column], send_e.at[column], recv_e.at[column], in_row(column)).wait_recv()

    def envs_down():
        return remote(envs.at[pl.ds(0, 2)], lr_ghost.at[1], send_v.at[3], recv_v.at[3], below)

    def envs_up():
        return remote(envs.at[pl.ds(2, 2)], lr_ghost.at[0], send_v.at[4], recv_v.at[4], above)

    @pl.when(has_below)
    def _():
        envs_down().start()

    @pl.when(has_above)
    def _():
        envs_up().start()

    def right_of(env):
        high, low = halves(env)
        return jnp.concatenate([jnp.concatenate([high, low], axis=1),
                                jnp.concatenate([high, jnp.zeros_like(low)], axis=1)], axis=0)

    for k in range(2):
        left_ref[k] = envs[2 * k]
        right_w[k] = right_of(envs[2 * k + 1])
    none = jnp.zeros((BLK, BLK), BF16)

    lefts = [halves(envs[2 * k]) for k in range(2)]
    for h in range(2):
        own_a[h] = own_a[h] + jnp.concatenate([jnp.concatenate([lefts[0][h], none], axis=1),
                                               jnp.concatenate([none, lefts[1][h]], axis=1)], axis=0)
        left_w[h] = packed(envs[2 * h])

    def right_products(refs, p, row, matrix):
        rows = slice(BLK * row, BLK * (row + 1))
        lhs = jnp.concatenate([jnp.concatenate([ref[p + j, rows, :] for ref in refs], axis=1)
                               for j in range(2)], axis=0)
        value = dot(lhs, matrix)
        value = value[:, :BLK] + value[:, BLK:]
        return value[:BLK], value[BLK:]

    def environment_products(refs, i, row, at):
        lefts = packed_dot(left_w[at], refs, 2 * i, row)
        rights = right_products(refs, 2 * i, row, right_w[at])
        return [left + right for left, right in zip(lefts, rights)]

    def first_apply(i, total):
        for k in range(2):
            blocks = environment_products((xh, xl), i, k + 1, k)
            for j in range(2):
                p = 2 * i + j
                value = w0[k, p] + blocks[j]
                w0[k, p] = value
                high, low = halves(value)
                yh[p, BLK * (k + 1):BLK * (k + 2), :] = high
                yl[p, BLK * (k + 1):BLK * (k + 2), :] = low
                total = total + fold(value * vp[k, p])
        return total

    def ghost_apply(i, carry):
        for side, row in ((0, 0), (1, 3)):
            blocks = environment_products((xh, xl), i, row, 2 + side)
            for j in range(2):
                p = 2 * i + j
                high, low = halves(w_ghost[side, p] + outward[side, p] + blocks[j])
                yh[p, BLK * row:BLK * (row + 1), :] = high
                yl[p, BLK * row:BLK * (row + 1), :] = low
        return carry

    zeros = jnp.zeros((8, BLK), F32)
    spread(1, [lax.fori_loop(0, PAIRS, first_apply, zeros)])
    phys_product(yh, yl, w1)

    @pl.when(has_below)
    def _():
        envs_up().wait_recv()

    @pl.when(has_above)
    def _():
        envs_down().wait_recv()

    for side in range(2):
        left_w[2 + side] = packed(lr_ghost[side, 0])
        right_w[2 + side] = right_of(lr_ghost[side, 1])

    @pl.when(has_below)
    def _():
        base_up().wait_recv()

    @pl.when(has_above)
    def _():
        base_down().wait_recv()

    lax.fori_loop(0, PAIRS, ghost_apply, 0)
    corr = collect(1, 1)[0]
    corrs = jnp.broadcast_to(corr, (BLK, BLK))

    def finish(i, totals):
        rr, rt, vt, tt = totals
        value = split_dot((own_a[0], own_a[1]), pair_of((yh, yl), i, 1, 2))
        for k in range(2):
            ghosts = packed_dot(ghost_a[k], (yh, yl), 2 * i, 3 * k)
            rights = right_products((yh, yl), 2 * i, k + 1, right_w[k])
            for j in range(2):
                p = 2 * i + j
                applied = w0[k, p]
                wave = vp[k, p]
                residual = applied - corrs * wave
                turned = (w1[k, p] + rights[j] + ghosts[j] + value[BLK * k:BLK * (k + 1), BLK * j:BLK * (j + 1)]
                          - corrs * applied)
                r0[k, p] = residual
                w1[k, p] = turned
                high, low = halves(turned)
                xh[p, BLK * (k + 1):BLK * (k + 2), :] = high
                xl[p, BLK * (k + 1):BLK * (k + 2), :] = low
                rr = rr + fold(residual * residual)
                rt = rt + fold(residual * turned)
                vt = vt + fold(wave * turned)
                tt = tt + fold(turned * turned)
        return rr, rt, vt, tt

    def turned_down(part):
        at = pl.ds(2 * part, 2)
        return remote(w1.at[0, at], t_ghost.at[1, at], send_t.at[0, part], recv_t.at[0, part], below)

    def turned_up(part):
        return remote(w1.at[1, pl.ds(PAIRS + 2 * part, 2)], t_ghost.at[0, pl.ds(2 * part, 2)],
                      send_t.at[1, part], recv_t.at[1, part], above)

    totals = (zeros,) * 4
    for part in range(CHUNKS):
        totals = lax.fori_loop(0, 2, lambda n, c: finish(part + CHUNKS * n, c), totals)

        @pl.when(has_below)
        def _():
            turned_down(part).start()

        @pl.when(has_above)
        def _():
            turned_up(part).start()

    def third_apply(i, total):
        rhs = pair_of((xh,), i, 1, 2)[0]
        value = dot(own_a[0], rhs) + dot(own_a[1], rhs)
        for k in range(2):
            rights = right_products((xh,), 2 * i, k + 1, right_w[k, :BLK])
            for j in range(2):
                p = 2 * i + j
                both = 2.0 * w1[k, p] - xh[p, BLK * (k + 1):BLK * (k + 2), :].astype(F32)
                image = value[BLK * k:BLK * (k + 1), BLK * j:BLK * (j + 1)] + rights[j]
                total = total + fold(image * both)
        return total

    def third_phys(i, total):
        at = pl.multiple_of(32 * i, 32)
        for k in range(2):
            rhs = phys_rows(xh, k, i)
            value = dot(phys_a[0], rhs) + dot(phys_a[1], rhs)
            for p in range(PHYS):
                rows = value[PHYS * p:PHYS * (p + 1)]
                image = jnp.concatenate([rows[:, :BLK], rows[:, BLK:]], axis=0)
                high = xh[p, pl.ds(pl.multiple_of(BLK * (k + 1) + 32 * i, 32), 32), :].astype(F32)
                total = total + fold(image * (2.0 * w1[k, p, pl.ds(at, 32), :] - high))
        return total

    def cross(i, carry):
        for side in range(2):
            blocks = packed_dot(cross_a[side], (xh, xl), 2 * i + PAIRS * (1 - side), side + 1)
            for j in range(2):
                crossed[side, 2 * i + j] = blocks[j]
        return carry

    def cross_and_phys(i, total):
        cross(i, 0)
        return third_phys(i, total)

    tht = lax.fori_loop(0, PAIRS // 2, cross_and_phys, zeros)

    loads[5].wait()
    masks = [(lax.broadcasted_iota(jnp.int32, (1, BLK), 1) < kept_ref[0, k]).astype(F32) for k in range(2)]

    def masked(p, grams):
        for k in range(2):
            vectors = (vp[k, p], r0[k, p], w1[k, p])
            pairs = [vectors[i] * vectors[j] for i in range(3) for j in range(i, 3)]
            grams = tuple(gram + masks[k] * fold(pair) for gram, pair in zip(grams, pairs))
        return grams

    def apply_and_masked(i, carry):
        total, grams = carry
        return third_apply(i, total), masked(2 * i + 1, masked(2 * i, grams))

    tht, grams = lax.fori_loop(0, PAIRS, apply_and_masked, (tht, (zeros,) * 6))

    for part in range(CHUNKS):
        @pl.when(has_above)
        def _():
            turned_down(part).wait_recv()

        @pl.when(has_below)
        def _():
            turned_up(part).wait_recv()

    def meet(i, total):
        return total + fold(crossed[0, i] * t_ghost[0, i]) + fold(crossed[1, i] * t_ghost[1, i])

    tht = tht + 2.0 * lax.fori_loop(0, PAIRS, meet, zeros)
    spread(2, list(totals) + [tht] + list(grams))
    rr, rt, vt, tt, tht, mvv, mvr, mvt, mrr, mrt, mtt = collect(2, 11)
    w0t = rt + corr * vt
    norm = jnp.sqrt(rr + EPS)
    curvature = rt / (rr + EPS)
    coupled = rr / norm
    ritz = 0.5 * (corr + curvature) - jnp.sqrt(0.25 * (corr - curvature) ** 2 + coupled * coupled)
    coef = ritz - corr
    magnitude = jnp.sqrt(coupled * coupled + coef * coef)
    wave_v = coupled / magnitude
    wave_r = coef / (magnitude * norm)
    corr2 = wave_v * wave_v * corr + wave_v * wave_r * (vt + rr) + wave_r * wave_r * rt
    res_v = wave_v * (corr - corr2)
    res_r = wave_v - corr2 * wave_r
    res_t = wave_r

    rr2 = res_v * res_v + res_r * res_r * rr + res_t * res_t * tt + 2.0 * res_t * (res_v * vt + res_r * rt)
    rr2 = jnp.maximum(rr2, 0.0)
    wr2 = wave_v * res_v + wave_r * res_r * rr + res_t * (wave_v * vt + wave_r * rt)
    ar2 = rr2 + corr2 * wr2
    norm2 = jnp.sqrt(rr2 + EPS)
    turned2 = (res_v * res_v * corr + res_r * res_r * rt + res_t * res_t * tht
               + 2.0 * (res_v * res_r * vt + res_v * res_t * w0t + res_r * res_t * tt))
    curvature = turned2 / (rr2 + EPS)
    coupled = ar2 / norm2
    ritz = 0.5 * (corr2 + curvature) - jnp.sqrt(0.25 * (corr2 - curvature) ** 2 + coupled * coupled)
    coef = ritz - corr2
    magnitude = jnp.sqrt(coupled * coupled + coef * coef)
    of_wave = coupled / magnitude
    of_res = coef / (magnitude * norm2)
    of_v = of_wave * wave_v + of_res * res_v
    of_r = of_wave * wave_r + of_res * res_r
    of_t = of_res * res_t
    kept = (of_v * of_v * mvv + of_r * of_r * mrr + of_t * of_t * mtt
            + 2.0 * (of_v * of_r * mvr + of_v * of_t * mvt + of_r * of_t * mrt))
    scale = 1.0 / jnp.sqrt(jnp.maximum(kept, 0.0) + EPS)
    last = [scale * value for value in (of_v, of_r, of_t)]
    last_ref[...] = jnp.concatenate(
        [jnp.broadcast_to(value, (1, BLK)) for value in last + [ritz]] + masks + [jnp.zeros((2, BLK), F32)], axis=0)

    for at in range(3):
        for part in range(2):
            @pl.when(sends[at][part])
            def _():
                step(at, part).wait_send()

    @pl.when(zz < 3)
    def _():
        far_copy(0).wait_send()
    for slot in range(NX):
        @pl.when(my_slot != slot)
        def _():
            give(slot).wait_send()
    for at in range(3):
        for hop in range(1, NS):
            remote(sums.at[at, sector], sums.at[at, sector], send_p.at[at, hop], recv_p.at[at, sector],
                   (chain, peer(hop))).wait_send()

    @pl.when(has_above)
    def _():
        coupling_up().wait_send()
        ghost_up().wait_send()
        envs_up().wait_send()
        base_up().wait_send()
        for part in range(CHUNKS):
            turned_up(part).wait_send()

    @pl.when(has_below)
    def _():
        ghost_down().wait_send()
        envs_down().wait_send()
        base_down().wait_send()
        for part in range(CHUNKS):
            turned_down(part).wait_send()


def write_kernel(wave_ref, res_ref, turned_ref, last_ref, left_in, out_ref, energy_ref, left_ref, rows, sem):
    left_copy = pltpu.make_async_copy(left_in, left_ref, sem.at[8])
    left_copy.start()
    energy_ref[0] = jnp.sum(last_ref[3:4, 0:1])
    size = ROWS // CHUNKS
    count = size // PHYS
    copies = []
    for k in range(2):
        mask = last_ref[4 + k:5 + k, :]
        coefs = [jnp.broadcast_to(last_ref[i:i + 1, :] * mask, (count, BLK)) for i in range(3)]
        for part in range(CHUNKS):
            at = pl.ds(count * part, count)
            for p in range(PHYS):
                rows[k, pl.ds(size * part + p, count, stride=PHYS), :] = (
                    coefs[0] * wave_ref[k, p, at, :] + coefs[1] * res_ref[k, p, at, :] + coefs[2] * turned_ref[k, p, at, :])
            to = pl.ds(size * part, size)
            copies.append(pltpu.make_async_copy(rows.at[k, to], out_ref.at[k, to], sem.at[CHUNKS * k + part]))
            copies[-1].start()
    for copy in copies:
        copy.wait()
    left_copy.wait()


def per_device(wave_start, transfer, energy_terms, coupling, physical, kept_ranks):
    hbm = pl.BlockSpec(memory_space=pltpu.HBM)
    vmem = pl.BlockSpec(memory_space=pltpu.VMEM)
    smem = pl.BlockSpec(memory_space=pltpu.SMEM)
    dma = pltpu.SemaphoreType.DMA

    def square(*lead):
        return pltpu.VMEM((*lead, BLK, BLK), F32)

    def wide(*lead):
        return pltpu.VMEM((*lead, 2 * BLK, 2 * BLK), BF16)

    split_waves = pltpu.VMEM((PHYS, 4 * BLK, BLK), BF16)
    waves = jax.ShapeDtypeStruct((2, PHYS, BLK, BLK), F32)
    parts = pl.pallas_call(
        update_kernel,
        out_shape=(
            waves, waves, waves,
            jax.ShapeDtypeStruct((8, BLK), F32),
            jax.ShapeDtypeStruct((2, BLK, BLK), F32),
        ),
        in_specs=[hbm] * 6,
        out_specs=(vmem,) * 5,
        scratch_shapes=[
            pltpu.VMEM((2, ROWS, BLK), F32), square(2), square(2), square(2), pltpu.VMEM((PHYS, PHYS), F32),
            pltpu.SMEM((1, 2), jnp.int32),
            square(NX, 2), square(NX, 2), square(3, 2), square(3, 2), square(), square(2, PHYS), square(2, PHYS), square(NX), square(NX),
            pltpu.VMEM((2, ROWS, BLK), F32), square(), square(2, PHYS), square(2, PHYS),
            square(2, PAIRS), square(2, 2), square(2, PAIRS),
            split_waves, split_waves, split_waves, split_waves,
            wide(4), wide(2), wide(2), wide(2), wide(4), wide(2),
            pltpu.VMEM((3, NS, 16, BLK), F32),
            dma((6,)), dma((NX,)), dma((NX,)), dma((3, 2)), dma((3, 2)), dma((1,)), dma((1,)), dma((NX,)), dma((NX,)),
            dma((5,)), dma((5,)), dma((2,)), dma((2,)), dma((2, CHUNKS)), dma((2, CHUNKS)),
            dma((3, NS)), dma((3, NS)),
        ],
        compiler_params=pltpu.CompilerParams(
            collective_id=0, has_side_effects=True, vmem_limit_bytes=36 << 20),
    )(*[pltpu.with_memory_space_constraint(value, pltpu.HBM) for value in (
        wave_start.reshape(2, ROWS, BLK), transfer[0], energy_terms[0], coupling[0], physical[0], kept_ranks)])
    out, energy, left = pl.pallas_call(
        write_kernel,
        out_shape=(
            jax.ShapeDtypeStruct((2, ROWS, BLK), F32),
            jax.ShapeDtypeStruct((1,), F32),
            jax.ShapeDtypeStruct((2, BLK, BLK), F32),
        ),
        in_specs=[vmem] * 5,
        out_specs=(hbm, smem, hbm),
        scratch_shapes=[pltpu.VMEM((2, ROWS, BLK), F32), dma((9,))],
        compiler_params=pltpu.CompilerParams(vmem_limit_bytes=16 << 20),
    )(*[pltpu.with_memory_space_constraint(value, pltpu.VMEM) for value in parts])
    return (out.reshape(wave_start.shape), energy, left[None])


def solution(mesh):
    placed = (
        P("chain", "sector", None, None, None),
        P("chain", "sector", None, None),
        P("chain", "sector", None, None),
        P("chain", "sector", None, None),
        P("chain", None, None),
        P("chain", "sector"),
    )
    return jax.shard_map(
        per_device,
        mesh=mesh,
        in_specs=placed,
        out_specs=(
            P("chain", "sector", None, None, None),
            P("chain"),
            P("chain", "sector", None, None),
        ),
        check_vma=False,
    )
```

```python
import functools

import jax
import jax.numpy as jnp
from jax import lax
from jax.experimental import pallas as pl
from jax.experimental.pallas import tpu as pltpu
from jax.sharding import PartitionSpec as P

BLK = 128
PHYS = 16
NX = 4
NZ = 8
NS = 8
ROWS = BLK * PHYS
CHUNKS = 4
CHUNK = PHYS // CHUNKS
PAIRS = PHYS // 2

EPS = 1e-06
MESH = pl.DeviceIdType.MESH
F32 = jnp.float32
BF16 = jnp.bfloat16
NN = (((1,), (0,)), ((), ()))
NT = (((1,), (1,)), ((), ()))


def halves(value):
    high = value.astype(BF16)
    return high, (value - high.astype(F32)).astype(BF16)


def dot(lhs, rhs, dims=NN):
    return lax.dot_general(lhs, rhs, dims, preferred_element_type=F32)


def product(lhs, rhs, dims=NN):
    lhs_high, lhs_low = halves(lhs)
    rhs_high, rhs_low = halves(rhs)
    both = jnp.concatenate([lhs_high, lhs_low], axis=1)
    twice = jnp.concatenate([rhs_high, rhs_high], axis=1 if dims is NT else 0)
    return dot(both, twice, dims) + dot(lhs_high, rhs_low, dims)


def split_dot(lhs, rhs):
    return dot(lhs[0], rhs[0]) + (dot(lhs[0], rhs[1]) + dot(lhs[1], rhs[0]))


def packed(matrix):
    high, low = halves(matrix)
    return jnp.concatenate([jnp.concatenate([high, high], axis=1),
                            jnp.concatenate([low, jnp.zeros_like(low)], axis=1)], axis=0)


def packed_dot(matrix, refs, p, row):
    rows = slice(BLK * row, BLK * (row + 1))
    rhs = jnp.concatenate([jnp.concatenate([ref[p + j, rows, :] for ref in refs], axis=0) for j in range(2)], axis=1)
    value = dot(matrix, rhs)
    value = value[:BLK] + value[BLK:]
    return value[:, :BLK], value[:, BLK:]


def carry_over(matrix, env, source):
    return product(product(matrix, env), matrix, NT) + source


def fold(value):
    return jnp.sum(value.reshape(-1, 8, BLK), axis=0)


def remote(src, dst, send_sem, recv_sem, device):
    return pltpu.make_async_remote_copy(src, dst, send_sem, recv_sem, device_id=device, device_id_type=MESH)


def update_kernel(v_hbm, t_hbm, e_hbm, c_hbm, p_hbm, kept_hbm, vp, r0, w1, last_ref, left_ref,
                  v_ref, t_ref, e_ref, c_ref, p_ref, kept_ref,
                  mine, elements, window, came, far, partial, outward, ends, envs,
                  ghost, ghost_c, w0, w_ghost, t_ghost, lr_ghost, crossed,
                  xh, xl, yh, yl, left_w, own_a, ghost_a, cross_a, right_w, phys_a, sums,
                  load, send_a, recv_a, send_z, recv_z, send_f, recv_f, send_e, recv_e,
                  send_v, recv_v, send_w, recv_w, send_t, recv_t, send_p, recv_p):
    chain = lax.axis_index("chain")
    sector = lax.axis_index("sector")
    x = lax.rem(chain, NX)
    z = lax.div(chain, NX)
    odd = lax.rem(x, 2)
    zz = z + odd * (NZ - 1 - 2 * z)
    my_slot = x + odd * (NX - 1 - 2 * x)
    has_below = sector > 0
    has_above = sector < NS - 1
    below = (chain, sector - 1)
    above = (chain, sector + 1)

    def in_row(other):
        return (z * NX + other, sector)

    def in_column(other):
        return ((other + odd * (NZ - 1 - 2 * other)) * NX + x, sector)

    def slot_of(column):
        return x if column % 2 == 0 else NX - 1 - x

    def peer(hop):
        return lax.rem(sector + hop, NS)

    loads = [pltpu.make_async_copy(src, dst, load.at[i]) for i, (src, dst) in enumerate((
        (t_hbm, t_ref), (e_hbm, e_ref), (v_hbm, v_ref), (c_hbm, c_ref), (p_hbm, p_ref),
        (kept_hbm, kept_ref)))]
    for copy in loads:
        copy.start()

    barrier = pltpu.get_barrier_semaphore()
    greeted = NX - 1 + NS - 1
    for hop in range(1, NX):
        pl.semaphore_signal(barrier, inc=1, device_id=in_row(lax.rem(x + hop, NX)), device_id_type=MESH)
    for hop in range(1, NS):
        pl.semaphore_signal(barrier, inc=1, device_id=(chain, peer(hop)), device_id_type=MESH)
    for hop in (1, 2, 5):
        for other, there in ((zz + hop, zz + hop < NZ), (zz - hop, zz >= hop)):
            @pl.when(there)
            def _():
                pl.semaphore_signal(barrier, inc=1, device_id=in_column(other), device_id_type=MESH)
            greeted = greeted + there.astype(jnp.int32)

    loads[0].wait()
    loads[1].wait()
    for k in range(2):
        transfer = t_ref[k]
        source = 0.5 * (e_ref[k] + e_ref[k].T)
        mine[2 * k, 0] = transfer.T
        mine[2 * k + 1, 0] = transfer
        mine[2 * k, 1] = source
        mine[2 * k + 1, 1] = source
    pl.semaphore_wait(barrier, greeted)

    def spread(at, parts):
        rows = [jnp.sum(part, axis=0, keepdims=True) for part in parts]
        rows += [jnp.zeros((1, BLK), F32)] * (16 - len(rows))
        sums[at, pl.ds(sector, 1)] = jnp.concatenate(rows, axis=0)[None]
        for hop in range(1, NS):
            remote(sums.at[at, sector], sums.at[at, sector], send_p.at[at, hop], recv_p.at[at, sector],
                   (chain, peer(hop))).start()

    def collect(at, count):
        for hop in range(1, NS):
            other = peer(hop)
            remote(sums.at[at, other], sums.at[at, other], send_p.at[at, hop], recv_p.at[at, other],
                   (chain, other)).wait_recv()
        total = sums[at, 0]
        for other in range(1, NS):
            total = total + sums[at, other]
        total = jnp.sum(total, axis=1, keepdims=True)
        return [total[i:i + 1] for i in range(count)]

    def deal(column):
        slot = slot_of(column)
        return remote(mine.at[column], elements.at[slot], send_a.at[column], recv_a.at[slot], in_row(column))

    for hop in (2, 1, 3):
        for column in range(NX):
            @pl.when(column == lax.rem(x + hop, NX))
            def _():
                deal(column).start()
    elements[pl.ds(my_slot, 1)] = mine[pl.ds(x, 1)]

    def ghost_up():
        return remote(v_hbm.at[1], ghost.at[0], send_v.at[0], recv_v.at[0], above)

    def ghost_down():
        return remote(v_hbm.at[0], ghost.at[1], send_v.at[1], recv_v.at[1], below)

    def coupling_up():
        return remote(c_hbm.at[1], ghost_c, send_v.at[2], recv_v.at[2], above)

    @pl.when(has_above)
    def _():
        coupling_up().start()

    def square(i, total):
        part = v_ref[:, pl.ds(pl.multiple_of(i * 256, 256), 256), :]
        return total + fold(part * part)

    loads[2].wait()
    spread(0, [lax.fori_loop(0, 8, square, jnp.zeros((8, BLK), F32))])

    square_zero = jnp.zeros((BLK, BLK), F32)
    for ref, unused in (
            (came.at[0, 0], (zz < 2) | (zz == NZ - 1)), (came.at[0, 1], (zz < 1) | (zz == NZ - 1)),
            (came.at[1, 0], (zz < 4) | (zz == NZ - 1)), (came.at[1, 1], (zz < 2) | (zz == NZ - 1)),
            (came.at[2, 0], zz < 5), (came.at[2, 1], zz < 1), (far, zz < 5)):
        @pl.when(unused)
        def _():
            ref[...] = square_zero

    @pl.when(sector == 0)
    def _():
        ghost[0] = jnp.zeros((ROWS, BLK), F32)
        ghost_c[...] = square_zero
        w_ghost[0] = jnp.zeros((PHYS, BLK, BLK), F32)
        t_ghost[0] = jnp.zeros((PAIRS, BLK, BLK), F32)
        lr_ghost[0] = jnp.zeros((2, BLK, BLK), F32)

    @pl.when(sector == NS - 1)
    def _():
        ghost[1] = jnp.zeros((ROWS, BLK), F32)
        w_ghost[1] = jnp.zeros((PHYS, BLK, BLK), F32)
        t_ghost[1] = jnp.zeros((PAIRS, BLK, BLK), F32)
        lr_ghost[1] = jnp.zeros((2, BLK, BLK), F32)

    for column in range(NX):
        @pl.when(x != column)
        def _():
            deal(column).wait_send()

    @pl.when(has_above)
    def _():
        ghost_up().start()

    @pl.when(has_below)
    def _():
        ghost_down().start()

    for slot in range(NX):
        @pl.when(my_slot != slot)
        def _():
            remote(mine.at[slot], elements.at[slot], send_a.at[slot], recv_a.at[slot],
                   in_row(lax.rem(x + 1, NX))).wait_recv()

    q0, q1, q2, q3 = [elements[s, 0] for s in range(NX)]
    s0, s1, s2, s3 = [elements[s, 1] for s in range(NX)]
    q01 = product(q1, q0)
    y01 = carry_over(q1, s0, s1)
    q23 = product(q3, q2)
    y23 = carry_over(q3, s2, s3)
    qw = product(q23, q01)
    yw = carry_over(q23, y01, y23)

    hops = (1, 2, 1)
    sends = (((zz >= 1) & (zz <= 5), zz <= 5), ((zz >= 2) & (zz <= 4), zz <= 4), ((zz >= 4) & (zz <= 6), zz <= 6))
    takes = (((zz >= 2) & (zz <= 6), (zz >= 1) & (zz <= 6)), ((zz >= 4) & (zz <= 6), (zz >= 2) & (zz <= 6)),
             (zz >= 5, zz >= 1))

    def step(at, part):
        return remote(window.at[at, part], came.at[at, part], send_z.at[at, part], recv_z.at[at, part],
                      in_column(zz + hops[at]))

    def send(at, part, value):
        window[at, part] = value

        @pl.when(sends[at][part])
        def _():
            step(at, part).start()

    def receive(at, part):
        @pl.when(takes[at][part])
        def _():
            remote(window.at[at, part], came.at[at, part], send_z.at[at, part], recv_z.at[at, part],
                   in_column(zz - hops[at])).wait_recv()
        return came[at, part]

    def far_copy(at):
        return remote(window.at[at, 1], far, send_f.at[0], recv_f.at[0], in_column(zz + 5))

    def send_far(at):
        @pl.when(zz == at)
        def _():
            far_copy(at).start()

    def start_wave():
        inverse = 1.0 / jnp.sqrt(collect(0, 1)[0])
        inverses = jnp.broadcast_to(inverse, (BLK, BLK))

        def one(p, carry):
            for k in range(2):
                value = v_ref[k, pl.ds(p, BLK, stride=PHYS), :] * inverses
                vp[k, p] = value
                high, low = halves(value)
                xh[p, BLK * (k + 1):BLK * (k + 2), :] = high
                xl[p, BLK * (k + 1):BLK * (k + 2), :] = low
            return carry

        lax.fori_loop(0, PHYS, one, 0)
        return inverses

    def make_phys():
        loads[4].wait()
        sym = 0.5 * (p_ref[...] + p_ref[...].T)
        lane = lax.broadcasted_iota(jnp.int32, (PHYS, 256), 1)
        row = lax.broadcasted_iota(jnp.int32, (PHYS, 256), 0)
        spread_p = (lax.div(lane, PHYS) == row).astype(BF16)
        same = (lax.rem(lane, PHYS) == row).astype(F32)
        for i, half in enumerate(halves(sym)):
            wide = dot(half, spread_p)
            for p in range(PHYS):
                phys_a[i, PHYS * p:PHYS * (p + 1), :] = (wide[p:p + 1, :] * same).astype(BF16)

    def phys_rows(ref, k, i):
        first = pl.multiple_of(BLK * (k + 1) + 32 * i, 32)
        second = pl.multiple_of(BLK * (k + 1) + 32 * i + 16, 16)
        return jnp.concatenate([
            jnp.concatenate([ref[p, pl.ds(at, 16), :] for p in range(PHYS)], axis=0)
            for at in (first, second)], axis=1)

    def phys_piece(high, low, k, i):
        return split_dot((phys_a[0], phys_a[1]), (phys_rows(high, k, i), phys_rows(low, k, i)))

    def phys_product(high, low, dst):
        def one(i, carry):
            for k in range(2):
                value = phys_piece(high, low, k, i)
                at = pl.multiple_of(32 * i, 32)
                for p in range(PHYS):
                    rows = value[PHYS * p:PHYS * (p + 1)]
                    dst[k, p, pl.ds(at, 32), :] = jnp.concatenate([rows[:, :BLK], rows[:, BLK:]], axis=0)
            return carry

        lax.fori_loop(0, BLK // 32, one, 0)

    def make_ghost_matrices():
        loads[3].wait()
        zero = jnp.zeros((BLK, BLK), BF16)
        own_up = halves(c_ref[0])
        own_down = halves(c_ref[0].T)
        for i in range(2):
            own_a[i] = jnp.concatenate([jnp.concatenate([zero, own_down[i]], axis=1),
                                        jnp.concatenate([own_up[i], zero], axis=1)], axis=0)
        last = c_ref[1] * has_above.astype(F32)
        ghost_a[0] = packed(ghost_c[...])
        ghost_a[1] = packed(last.T)
        cross_a[0] = packed(ghost_c[...].T)
        cross_a[1] = packed(last)

    def pair_of(refs, i, low, high):
        p = 2 * i
        return [jnp.concatenate([
            jnp.concatenate([ref[p + j, BLK * low:BLK * (low + 1), :], ref[p + j, BLK * high:BLK * (high + 1), :]], axis=0)
            for j in range(2)], axis=1) for ref in refs]

    def add_own(i, carry):
        value = split_dot((own_a[0], own_a[1]), pair_of((xh, xl), i, 1, 2))
        for k in range(2):
            for j in range(2):
                p = 2 * i + j
                both = w0[k, p] + value[BLK * k:BLK * (k + 1), BLK * j:BLK * (j + 1)]
                w0[k, p] = both
                partial[k, p] = both
        return carry

    def add_to_ghosts(i, carry):
        for side in range(2):
            blocks = packed_dot(cross_a[side], (xh, xl), 2 * i, side + 1)
            for j in range(2):
                outward[side, 2 * i + j] = blocks[j]
        return carry

    def add_ghosts(i, inverses):
        for side, row in ((0, 0), (1, 3)):
            for j in range(2):
                p = 2 * i + j
                high, low = halves(ghost[side, pl.ds(p, BLK, stride=PHYS), :] * inverses)
                xh[p, BLK * row:BLK * (row + 1), :] = high
                xl[p, BLK * row:BLK * (row + 1), :] = low
            blocks = packed_dot(ghost_a[side], (xh, xl), 2 * i, row)
            for j in range(2):
                w0[side, 2 * i + j] = w0[side, 2 * i + j] + blocks[j]
        return inverses

    def base_down():
        return remote(partial.at[0], w_ghost.at[1], send_w.at[0], recv_w.at[0], below)

    def base_up():
        return remote(partial.at[1], w_ghost.at[0], send_w.at[1], recv_w.at[1], above)

    send(0, 1, yw)
    send(0, 0, qw)
    send_far(0)
    q012 = product(q2, q01)
    y012 = carry_over(q2, y01, s2)
    inverses = start_wave()
    make_phys()

    @pl.when(has_below)
    def _():
        coupling_up().wait_recv()

    make_ghost_matrices()
    yw = carry_over(qw, receive(0, 1), yw)
    send(1, 1, yw)
    send_far(1)
    qw = product(qw, receive(0, 0))
    send(1, 0, qw)
    phys_product(xh, xl, w0)
    lax.fori_loop(0, PAIRS, add_own, 0)

    @pl.when(has_below)
    def _():
        base_down().start()

    @pl.when(has_above)
    def _():
        base_up().start()

    yw = carry_over(qw, receive(1, 1), yw)
    send(2, 1, yw)
    send_far(2)
    send(2, 0, product(qw, receive(1, 0)))

    lax.fori_loop(0, PAIRS, add_to_ghosts, 0)

    @pl.when(zz >= 5)
    def _():
        remote(window.at[2, 1], far, send_f.at[0], recv_f.at[0], in_column(zz - 5)).wait_recv()
    y_near = receive(2, 1)
    start = carry_over(receive(2, 0), far[...], y_near)

    def owner(slot):
        return slot + odd * (NX - 1 - 2 * slot)

    def give(slot):
        return remote(ends.at[slot], envs.at[x], send_e.at[slot], recv_e.at[x], in_row(owner(slot)))

    ends[0] = start
    for slot, (q, y) in enumerate(((q0, s0), (q01, y01), (q012, y012))):
        ends[slot + 1] = carry_over(q, start, y)
    for hop in (2, 1, 3):
        for slot in range(NX):
            @pl.when(slot == lax.rem(my_slot + hop, NX))
            def _():
                give(slot).start()
    envs[pl.ds(x, 1)] = ends[pl.ds(my_slot, 1)]
    @pl.when(has_below)
    def _():
        ghost_up().wait_recv()

    @pl.when(has_above)
    def _():
        ghost_down().wait_recv()

    lax.fori_loop(0, PAIRS, add_ghosts, inverses)
    for column in range(NX):
        @pl.when(x != column)
        def _():
            remote(ends.at[column], envs.at[column], send_e.at[column], recv_e.at[column], in_row(column)).wait_recv()

    def envs_down():
        return remote(envs.at[pl.ds(0, 2)], lr_ghost.at[1], send_v.at[3], recv_v.at[3], below)

    def envs_up():
        return remote(envs.at[pl.ds(2, 2)], lr_ghost.at[0], send_v.at[4], recv_v.at[4], above)

    @pl.when(has_below)
    def _():
        envs_down().start()

    @pl.when(has_above)
    def _():
        envs_up().start()

    def right_of(env):
        high, low = halves(env)
        return jnp.concatenate([jnp.concatenate([high, low], axis=1),
                                jnp.concatenate([high, jnp.zeros_like(low)], axis=1)], axis=0)

    for k in range(2):
        left_ref[k] = envs[2 * k]
        right_w[k] = right_of(envs[2 * k + 1])
    none = jnp.zeros((BLK, BLK), BF16)

    lefts = [halves(envs[2 * k]) for k in range(2)]
    for h in range(2):
        own_a[h] = own_a[h] + jnp.concatenate([jnp.concatenate([lefts[0][h], none], axis=1),
                                               jnp.concatenate([none, lefts[1][h]], axis=1)], axis=0)
        left_w[h] = packed(envs[2 * h])

    def right_products(refs, p, row, matrix):
        rows = slice(BLK * row, BLK * (row + 1))
        lhs = jnp.concatenate([jnp.concatenate([ref[p + j, rows, :] for ref in refs], axis=1)
                               for j in range(2)], axis=0)
        value = dot(lhs, matrix)
        value = value[:, :BLK] + value[:, BLK:]
        return value[:BLK], value[BLK:]

    def environment_products(refs, i, row, at):
        lefts = packed_dot(left_w[at], refs, 2 * i, row)
        rights = right_products(refs, 2 * i, row, right_w[at])
        return [left + right for left, right in zip(lefts, rights)]

    def first_apply(i, total):
        for k in range(2):
            blocks = environment_products((xh, xl), i, k + 1, k)
            for j in range(2):
                p = 2 * i + j
                value = w0[k, p] + blocks[j]
                w0[k, p] = value
                high, low = halves(value)
                yh[p, BLK * (k + 1):BLK * (k + 2), :] = high
                yl[p, BLK * (k + 1):BLK * (k + 2), :] = low
                total = total + fold(value * vp[k, p])
        return total

    def ghost_apply(i, carry):
        for side, row in ((0, 0), (1, 3)):
            blocks = environment_products((xh, xl), i, row, 2 + side)
            for j in range(2):
                p = 2 * i + j
                high, low = halves(w_ghost[side, p] + outward[side, p] + blocks[j])
                yh[p, BLK * row:BLK * (row + 1), :] = high
                yl[p, BLK * row:BLK * (row + 1), :] = low
        return carry

    zeros = jnp.zeros((8, BLK), F32)
    spread(1, [lax.fori_loop(0, PAIRS, first_apply, zeros)])
    phys_product(yh, yl, w1)

    @pl.when(has_below)
    def _():
        envs_up().wait_recv()

    @pl.when(has_above)
    def _():
        envs_down().wait_recv()

    for side in range(2):
        left_w[2 + side] = packed(lr_ghost[side, 0])
        right_w[2 + side] = right_of(lr_ghost[side, 1])

    @pl.when(has_below)
    def _():
        base_up().wait_recv()

    @pl.when(has_above)
    def _():
        base_down().wait_recv()

    lax.fori_loop(0, PAIRS, ghost_apply, 0)
    corr = collect(1, 1)[0]
    corrs = jnp.broadcast_to(corr, (BLK, BLK))

    def finish(i, totals):
        rr, rt, vt, tt = totals
        value = split_dot((own_a[0], own_a[1]), pair_of((yh, yl), i, 1, 2))
        for k in range(2):
            ghosts = packed_dot(ghost_a[k], (yh, yl), 2 * i, 3 * k)
            rights = right_products((yh, yl), 2 * i, k + 1, right_w[k])
            for j in range(2):
                p = 2 * i + j
                applied = w0[k, p]
                wave = vp[k, p]
                residual = applied - corrs * wave
                turned = (w1[k, p] + rights[j] + ghosts[j] + value[BLK * k:BLK * (k + 1), BLK * j:BLK * (j + 1)]
                          - corrs * applied)
                r0[k, p] = residual
                w1[k, p] = turned
                high, low = halves(turned)
                xh[p, BLK * (k + 1):BLK * (k + 2), :] = high
                xl[p, BLK * (k + 1):BLK * (k + 2), :] = low
                rr = rr + fold(residual * residual)
                rt = rt + fold(residual * turned)
                vt = vt + fold(wave * turned)
                tt = tt + fold(turned * turned)
        return rr, rt, vt, tt

    def turned_down(part):
        at = pl.ds(2 * part, 2)
        return remote(w1.at[0, at], t_ghost.at[1, at], send_t.at[0, part], recv_t.at[0, part], below)

    def turned_up(part):
        return remote(w1.at[1, pl.ds(PAIRS + 2 * part, 2)], t_ghost.at[0, pl.ds(2 * part, 2)],
                      send_t.at[1, part], recv_t.at[1, part], above)

    totals = (zeros,) * 4
    for part in range(CHUNKS):
        totals = lax.fori_loop(0, 2, lambda n, c: finish(part + CHUNKS * n, c), totals)

        @pl.when(has_below)
        def _():
            turned_down(part).start()

        @pl.when(has_above)
        def _():
            turned_up(part).start()

    def third_apply(i, total):
        rhs = pair_of((xh,), i, 1, 2)[0]
        value = dot(own_a[0], rhs) + dot(own_a[1], rhs)
        for k in range(2):
            rights = right_products((xh,), 2 * i, k + 1, right_w[k, :BLK])
            for j in range(2):
                p = 2 * i + j
                both = 2.0 * w1[k, p] - xh[p, BLK * (k + 1):BLK * (k + 2), :].astype(F32)
                image = value[BLK * k:BLK * (k + 1), BLK * j:BLK * (j + 1)] + rights[j]
                total = total + fold(image * both)
        return total

    def third_phys(i, total):
        at = pl.multiple_of(32 * i, 32)
        for k in range(2):
            rhs = phys_rows(xh, k, i)
            value = dot(phys_a[0], rhs) + dot(phys_a[1], rhs)
            for p in range(PHYS):
                rows = value[PHYS * p:PHYS * (p + 1)]
                image = jnp.concatenate([rows[:, :BLK], rows[:, BLK:]], axis=0)
                high = xh[p, pl.ds(pl.multiple_of(BLK * (k + 1) + 32 * i, 32), 32), :].astype(F32)
                total = total + fold(image * (2.0 * w1[k, p, pl.ds(at, 32), :] - high))
        return total

    def cross(i, carry):
        for side in range(2):
            blocks = packed_dot(cross_a[side], (xh, xl), 2 * i + PAIRS * (1 - side), side + 1)
            for j in range(2):
                crossed[side, 2 * i + j] = blocks[j]
        return carry

    def cross_and_phys(i, total):
        cross(i, 0)
        return third_phys(i, total)

    tht = lax.fori_loop(0, PAIRS // 2, cross_and_phys, zeros)

    loads[5].wait()
    masks = [(lax.broadcasted_iota(jnp.int32, (1, BLK), 1) < kept_ref[0, k]).astype(F32) for k in range(2)]

    def masked(p, grams):
        for k in range(2):
            vectors = (vp[k, p], r0[k, p], w1[k, p])
            pairs = [vectors[i] * vectors[j] for i in range(3) for j in range(i, 3)]
            grams = tuple(gram + masks[k] * fold(pair) for gram, pair in zip(grams, pairs))
        return grams

    def apply_and_masked(i, carry):
        total, grams = carry
        return third_apply(i, total), masked(2 * i + 1, masked(2 * i, grams))

    tht, grams = lax.fori_loop(0, PAIRS, apply_and_masked, (tht, (zeros,) * 6))

    for part in range(CHUNKS):
        @pl.when(has_above)
        def _():
            turned_down(part).wait_recv()

        @pl.when(has_below)
        def _():
            turned_up(part).wait_recv()

    def meet(i, total):
        return total + fold(crossed[0, i] * t_ghost[0, i]) + fold(crossed[1, i] * t_ghost[1, i])

    tht = tht + 2.0 * lax.fori_loop(0, PAIRS, meet, zeros)
    spread(2, list(totals) + [tht] + list(grams))
    rr, rt, vt, tt, tht, mvv, mvr, mvt, mrr, mrt, mtt = collect(2, 11)
    w0t = rt + corr * vt
    norm = jnp.sqrt(rr + EPS)
    curvature = rt / (rr + EPS)
    coupled = rr / norm
    ritz = 0.5 * (corr + curvature) - jnp.sqrt(0.25 * (corr - curvature) ** 2 + coupled * coupled)
    coef = ritz - corr
    magnitude = jnp.sqrt(coupled * coupled + coef * coef)
    wave_v = coupled / magnitude
    wave_r = coef / (magnitude * norm)
    corr2 = wave_v * wave_v * corr + wave_v * wave_r * (vt + rr) + wave_r * wave_r * rt
    res_v = wave_v * (corr - corr2)
    res_r = wave_v - corr2 * wave_r
    res_t = wave_r

    rr2 = res_v * res_v + res_r * res_r * rr + res_t * res_t * tt + 2.0 * res_t * (res_v * vt + res_r * rt)
    rr2 = jnp.maximum(rr2, 0.0)
    wr2 = wave_v * res_v + wave_r * res_r * rr + res_t * (wave_v * vt + wave_r * rt)
    ar2 = rr2 + corr2 * wr2
    norm2 = jnp.sqrt(rr2 + EPS)
    turned2 = (res_v * res_v * corr + res_r * res_r * rt + res_t * res_t * tht
               + 2.0 * (res_v * res_r * vt + res_v * res_t * w0t + res_r * res_t * tt))
    curvature = turned2 / (rr2 + EPS)
    coupled = ar2 / norm2
    ritz = 0.5 * (corr2 + curvature) - jnp.sqrt(0.25 * (corr2 - curvature) ** 2 + coupled * coupled)
    coef = ritz - corr2
    magnitude = jnp.sqrt(coupled * coupled + coef * coef)
    of_wave = coupled / magnitude
    of_res = coef / (magnitude * norm2)
    of_v = of_wave * wave_v + of_res * res_v
    of_r = of_wave * wave_r + of_res * res_r
    of_t = of_res * res_t
    kept = (of_v * of_v * mvv + of_r * of_r * mrr + of_t * of_t * mtt
            + 2.0 * (of_v * of_r * mvr + of_v * of_t * mvt + of_r * of_t * mrt))
    scale = 1.0 / jnp.sqrt(jnp.maximum(kept, 0.0) + EPS)
    last = [scale * value for value in (of_v, of_r, of_t)]
    last_ref[...] = jnp.concatenate(
        [jnp.broadcast_to(value, (1, BLK)) for value in last + [ritz]] + masks + [jnp.zeros((2, BLK), F32)], axis=0)

    for at in range(3):
        for part in range(2):
            @pl.when(sends[at][part])
            def _():
                step(at, part).wait_send()

    @pl.when(zz < 3)
    def _():
        far_copy(0).wait_send()
    for slot in range(NX):
        @pl.when(my_slot != slot)
        def _():
            give(slot).wait_send()
    for at in range(3):
        for hop in range(1, NS):
            remote(sums.at[at, sector], sums.at[at, sector], send_p.at[at, hop], recv_p.at[at, sector],
                   (chain, peer(hop))).wait_send()

    @pl.when(has_above)
    def _():
        coupling_up().wait_send()
        ghost_up().wait_send()
        envs_up().wait_send()
        base_up().wait_send()
        for part in range(CHUNKS):
            turned_up(part).wait_send()

    @pl.when(has_below)
    def _():
        ghost_down().wait_send()
        envs_down().wait_send()
        base_down().wait_send()
        for part in range(CHUNKS):
            turned_down(part).wait_send()


def write_kernel(wave_ref, res_ref, turned_ref, last_ref, left_in, out_ref, energy_ref, left_ref, rows, sem):
    left_copy = pltpu.make_async_copy(left_in, left_ref, sem.at[8])
    left_copy.start()
    energy_ref[0] = jnp.sum(last_ref[3:4, 0:1])
    size = ROWS // CHUNKS
    count = size // PHYS
    copies = []
    for k in range(2):
        mask = last_ref[4 + k:5 + k, :]
        coefs = [jnp.broadcast_to(last_ref[i:i + 1, :] * mask, (count, BLK)) for i in range(3)]
        for part in range(CHUNKS):
            at = pl.ds(count * part, count)
            for p in range(PHYS):
                rows[k, pl.ds(size * part + p, count, stride=PHYS), :] = (
                    coefs[0] * wave_ref[k, p, at, :] + coefs[1] * res_ref[k, p, at, :] + coefs[2] * turned_ref[k, p, at, :])
            to = pl.ds(size * part, size)
            copies.append(pltpu.make_async_copy(rows.at[k, to], out_ref.at[k, to], sem.at[CHUNKS * k + part]))
            copies[-1].start()
    for copy in copies:
        copy.wait()
    left_copy.wait()


def per_device(wave_start, transfer, energy_terms, coupling, physical, kept_ranks):
    hbm = pl.BlockSpec(memory_space=pltpu.HBM)
    vmem = pl.BlockSpec(memory_space=pltpu.VMEM)
    smem = pl.BlockSpec(memory_space=pltpu.SMEM)
    dma = pltpu.SemaphoreType.DMA

    def square(*lead):
        return pltpu.VMEM((*lead, BLK, BLK), F32)

    def wide(*lead):
        return pltpu.VMEM((*lead, 2 * BLK, 2 * BLK), BF16)

    split_waves = pltpu.VMEM((PHYS, 4 * BLK, BLK), BF16)
    waves = jax.ShapeDtypeStruct((2, PHYS, BLK, BLK), F32)
    parts = pl.pallas_call(
        update_kernel,
        out_shape=(
            waves, waves, waves,
            jax.ShapeDtypeStruct((8, BLK), F32),
            jax.ShapeDtypeStruct((2, BLK, BLK), F32),
        ),
        in_specs=[hbm] * 6,
        out_specs=(vmem,) * 5,
        scratch_shapes=[
            pltpu.VMEM((2, ROWS, BLK), F32), square(2), square(2), square(2), pltpu.VMEM((PHYS, PHYS), F32),
            pltpu.SMEM((1, 2), jnp.int32),
            square(NX, 2), square(NX, 2), square(3, 2), square(3, 2), square(), square(2, PHYS), square(2, PHYS), square(NX), square(NX),
            pltpu.VMEM((2, ROWS, BLK), F32), square(), square(2, PHYS), square(2, PHYS),
            square(2, PAIRS), square(2, 2), square(2, PAIRS),
            split_waves, split_waves, split_waves, split_waves,
            wide(4), wide(2), wide(2), wide(2), wide(4), wide(2),
            pltpu.VMEM((3, NS, 16, BLK), F32),
            dma((6,)), dma((NX,)), dma((NX,)), dma((3, 2)), dma((3, 2)), dma((1,)), dma((1,)), dma((NX,)), dma((NX,)),
            dma((5,)), dma((5,)), dma((2,)), dma((2,)), dma((2, CHUNKS)), dma((2, CHUNKS)),
            dma((3, NS)), dma((3, NS)),
        ],
        compiler_params=pltpu.CompilerParams(
            collective_id=0, has_side_effects=True, vmem_limit_bytes=36 << 20),
    )(*[pltpu.with_memory_space_constraint(value, pltpu.HBM) for value in (
        wave_start.reshape(2, ROWS, BLK), transfer[0], energy_terms[0], coupling[0], physical[0], kept_ranks)])
    out, energy, left = pl.pallas_call(
        write_kernel,
        out_shape=(
            jax.ShapeDtypeStruct((2, ROWS, BLK), F32),
            jax.ShapeDtypeStruct((1,), F32),
            jax.ShapeDtypeStruct((2, BLK, BLK), F32),
        ),
        in_specs=[vmem] * 5,
        out_specs=(hbm, smem, hbm),
        scratch_shapes=[pltpu.VMEM((2, ROWS, BLK), F32), dma((9,))],
        compiler_params=pltpu.CompilerParams(vmem_limit_bytes=16 << 20),
    )(*[pltpu.with_memory_space_constraint(value, pltpu.VMEM) for value in parts])
    return (out.reshape(wave_start.shape), energy, left[None])


def solution(mesh):
    placed = (
        P("chain", "sector", None, None, None),
        P("chain", "sector", None, None),
        P("chain", "sector", None, None),
        P("chain", "sector", None, None),
        P("chain", None, None),
        P("chain", "sector"),
    )
    return jax.shard_map(
        per_device,
        mesh=mesh,
        in_specs=placed,
        out_specs=(
            P("chain", "sector", None, None, None),
            P("chain"),
            P("chain", "sector", None, None),
        ),
        check_vma=False,
    )
```
